512 devices in a mesh: lead: 32 (over z_lo, y, core), tile: 16 (over x, z_hi).
Axes of the slice: x: 4, y: 8, z: 8 (z_hi: 4, z_lo: 2; z = z_hi * 2 + z_lo), core: 2. Of those that a mesh axis runs over, the one named last changes fastest.
Arguments:
- frames: bfloat16 [3, 384, 16, 128], P(None, None, 'tile'), may hold values from -6 to 6
- enc_weight: bfloat16 [384, 4, 9, 768], P('lead'), may hold values from -0.078125 to 0.078125
- enc_bias: float32 [384, 4], P('lead'), may hold values from -4 to 4
- head_weight: bfloat16 [384, 9, 384], replicated, may hold values from -0.109375 to 0.109375
- film_table: float32 [16, 2, 384], replicated, may hold values from -2.5 to 2.5
- lead_index: int32 [32], P('lead'), may hold values from 0 to 15
- cotangent: bfloat16 [32, 384, 16, 128], P('lead', None, 'tile'), may hold values from -6 to 6
Outputs:
- enc_weight_grad: bfloat16 [384, 4, 9, 768], P('lead')
- enc_bias_grad: float32 [384, 4], P('lead')
- head_weight_grad: bfloat16 [384, 9, 384], P('tile')
- film_grad: float32 [16, 2, 384], replicated
The draws below stay inside these ranges and needn't reach their ends.
All inputs are finite; a program needn't handle non-finite values.
Results may differ from the reference program's by a relative error of at most 0.0052.
Values may be sent and summed in bfloat16 or wider, within the bound.
A program may use at most 128 MiB of HBM per device.

```python
import jax
import jax.numpy as jnp
from jax import lax

HID = 384
CIN = 384
LEADS = 16
STEPS = 3
COLS = 128
HEAD_DILATION = 2
NROWS = 16
LEAD_SLOTS = 32


def place_ends(drawn, key, low, high):
    place = [jax.random.randint(jax.random.fold_in(key, axis), (), 0, length) for axis, length in enumerate(drawn.shape)]
    main_axis = drawn.shape.index(max(drawn.shape))
    beside = place[:main_axis] + [(place[main_axis] + 1) % drawn.shape[main_axis]] + place[main_axis + 1:]
    return drawn.at[tuple(place)].set(low).at[tuple(beside)].set(high)


def strengthened(array, rng, source, target, shards_of, factor):
    owner, partner = [(jnp.arange(array.shape[dim]) // (array.shape[dim] // shards_of)).reshape([-1 if axis == dim else 1 for axis in range(array.ndim)]) for dim in (source, target)]
    chosen = jax.random.permutation(rng, shards_of)[partner]
    strong = (owner == chosen) | (owner == (partner + shards_of // 2) % shards_of)
    return jnp.where(strong, factor * array, array)


def shard_levels(stream_key, extent, shards, smallest, top_value):
    def one(position, parts):
        draws = jax.random.uniform(jax.random.fold_in(jax.random.fold_in(stream_key, 6), position), (parts,), jnp.float32, smallest / len(shards), top_value / len(shards))
        return jnp.repeat(jnp.exp(draws), extent[position] // parts).reshape((-1,) + (1,) * (len(extent) - position - 1))

    gain = one(*shards[0])
    for cut in shards[1:]:
        gain = gain * one(*cut)
    return gain


def gaussian(own_key, shape, scale, most, cuts=(), dtype=jnp.bfloat16):
    drawn = jax.random.normal(own_key, shape, jnp.float32) * scale
    if len(cuts) > 0:
        drawn = shard_levels(own_key, shape, cuts, -0.22, 0.18) * drawn
    return jnp.clip(drawn, min=-most, max=most).astype(dtype)


def bell_draw_with(own_key, shape, deviation, reach, cuts, heavy, held_as=jnp.bfloat16):
    entries = deviation * jax.random.normal(own_key, shape, jnp.float32)
    if cuts:
        entries = entries * shard_levels(own_key, shape, cuts, -0.22, 0.18)
    return jnp.clip(strengthened(entries, jax.random.fold_in(own_key, 3), *heavy), -reach, reach).astype(held_as)


def setup_inputs(seed: int = 0) -> dict:
    seeds = jax.random.split(jax.random.key(seed), 8)
    return {
        "frames": gaussian(seeds[0], (STEPS, CIN, NROWS, COLS), 1.0, 6.0, ((2, 16),)),
        "enc_weight": gaussian(seeds[1], (HID, 4, 9, CIN + HID), (9 * (CIN + HID)) ** -0.5, 0.078125, ((0, 32),)),
        "enc_bias": gaussian(seeds[2], (HID, 4), 1.0, 4.0, ((0, 32),), jnp.float32),
        "head_weight": gaussian(seeds[3], (HID, 9, HID), (9 * HID) ** -0.5, 0.109375),
        "film_table": gaussian(seeds[4], (LEADS, 2, HID), 0.5, 2.5, (), jnp.float32),
        "lead_index": place_ends(jax.random.randint(seeds[5], (LEAD_SLOTS,), 0, LEADS), jax.random.fold_in(seeds[5], 1), 0, LEADS - 1).astype(jnp.int32),
        "cotangent": bell_draw_with(seeds[6], (LEAD_SLOTS, HID, NROWS, COLS), 1.0, 6.0, ((0, 32), (2, 16)), (2, 1, 16, 2.0)),
    }


tap_offsets = [(row_off, col_off) for row_off in (-1, 0, 1) for col_off in (-1, 0, 1)]


def shift_cols(field_in, offset):
    col_count = field_in.shape[-1]
    if offset == 0:
        return field_in
    lead_pads = [(0, 0)] * (field_in.ndim - 1)
    if offset > 0:
        return jnp.pad(field_in[..., offset:], lead_pads + [(0, offset)])
    return jnp.pad(field_in[..., :col_count + offset], lead_pads + [(-offset, 0)])


def stacked_taps(field_in, dilation, direction):
    row_count = field_in.shape[1]
    padded = jnp.pad(field_in, ((0, 0), (dilation, dilation), (0, 0)))
    pieces = []
    for row_off, col_off in tap_offsets:
        first_row = dilation + direction * dilation * row_off
        pieces.append(shift_cols(padded[:, first_row:first_row + row_count, :], direction * dilation * col_off))
    return jnp.stack(pieces, 0)


def reference(frames, enc_weight, enc_bias, head_weight, film_table, lead_index, cotangent):
    hidden = enc_weight.shape[0]
    in_chan = frames.shape[1]
    row_total = frames.shape[2]
    col_count = frames.shape[3]
    weight_wide = enc_weight.astype(jnp.float32)
    h_full = jnp.zeros((hidden, row_total, col_count), jnp.bfloat16)
    cell_memory = jnp.zeros((hidden, row_total, col_count), jnp.float32)
    saved = []
    for step_index in range(STEPS):
        stacked = jnp.concatenate([frames[step_index], h_full], 0)
        fwd_taps = stacked_taps(stacked, 1, 1)
        preact = jnp.einsum('ojkc,kcrw->ojrw', weight_wide, fwd_taps.astype(jnp.float32)) + enc_bias[:, :, None, None]
        in_gate = jax.nn.sigmoid(preact[:, 0])
        forget = jax.nn.sigmoid(preact[:, 1])
        cand_gate = jnp.tanh(preact[:, 2])
        output_gate = jax.nn.sigmoid(preact[:, 3])
        previous = cell_memory
        cell_memory = forget * previous + in_gate * cand_gate
        h_full = (output_gate * jnp.tanh(cell_memory)).astype(jnp.bfloat16)
        saved.append((fwd_taps, in_gate, forget, cand_gate, output_gate, previous, cell_memory))
    enc_wide = h_full.astype(jnp.float32)
    head_wide = head_weight.astype(jnp.float32)

    def one_lead(lead_pair):
        lead_slot, cotangent_lead = lead_pair
        chosen = (jnp.arange(film_table.shape[0]) == lead_slot).astype(jnp.float32)
        film_rows = jnp.sum(chosen[:, None, None] * film_table, 0)
        film_scale = 1.0 + film_rows[0]
        film_shift = film_rows[1]
        modulated = film_scale[:, None, None] * enc_wide + film_shift[:, None, None]
        activated_output = jax.nn.silu(modulated).astype(jnp.bfloat16)
        activation_taps = stacked_taps(activated_output, HEAD_DILATION, 1).astype(jnp.float32)
        cotangent_taps = stacked_taps(cotangent_lead, HEAD_DILATION, -1).astype(jnp.float32)
        act_grad = jnp.einsum('okc,korw->crw', head_wide, cotangent_taps)
        logistic = jax.nn.sigmoid(modulated)
        mod_grad = act_grad * logistic * (1.0 + modulated * (1.0 - logistic))
        film_stats = jnp.stack([jnp.sum(mod_grad * enc_wide, axis=(1, 2)), jnp.sum(mod_grad, axis=(1, 2))], 0)
        hid_grad = cotangent_lead.astype(jnp.float32) + film_scale[:, None, None] * mod_grad
        weight_part = jnp.einsum('orw,kcrw->okc', cotangent_lead.astype(jnp.float32), activation_taps)
        return hid_grad, film_stats, weight_part, chosen

    hid_grads, stats_all, weight_parts, chosen_all = lax.map(one_lead, (lead_index, cotangent))
    hid_grad = jnp.sum(hid_grads, 0)
    head_total = jnp.sum(weight_parts, 0)
    table_total = jnp.einsum('lm,ljc->mjc', chosen_all, stats_all)

    weight_grad = jnp.zeros(weight_wide.shape, jnp.float32)
    bias_grad = jnp.zeros(enc_bias.shape, jnp.float32)
    mem_grad = jnp.zeros((hidden, row_total, col_count), jnp.float32)
    flat_weight = weight_wide.reshape(hidden * 4, 9, in_chan + hidden)[:, :, in_chan:]
    for step_index in reversed(range(STEPS)):
        fwd_taps, in_gate, forget, cand_gate, output_gate, previous, cell_memory = saved[step_index]
        squashed = jnp.tanh(cell_memory)
        mem_grad = mem_grad + hid_grad * output_gate * (1.0 - squashed * squashed)
        gate_grad = jnp.stack([mem_grad * cand_gate * in_gate * (1.0 - in_gate),
                               mem_grad * previous * forget * (1.0 - forget),
                               mem_grad * in_gate * (1.0 - cand_gate * cand_gate),
                               hid_grad * squashed * output_gate * (1.0 - output_gate)], 1)
        gate_low = gate_grad.astype(jnp.bfloat16)
        weight_grad = weight_grad + jnp.einsum('ojrw,kcrw->ojkc', gate_low.astype(jnp.float32), fwd_taps.astype(jnp.float32))
        bias_grad = bias_grad + jnp.sum(gate_grad, axis=(2, 3))
        if step_index > 0:
            back_taps = stacked_taps(gate_low.reshape(hidden * 4, row_total, col_count), 1, -1).astype(jnp.float32)
            hid_grad = jnp.einsum('okc,korw->crw', flat_weight, back_taps)
            mem_grad = mem_grad * forget
    loss_scale = (cotangent.shape[0] * row_total * col_count) ** -0.5
    return ((weight_grad * loss_scale).astype(jnp.bfloat16), bias_grad * loss_scale,
            (head_total * loss_scale).astype(jnp.bfloat16), table_total * loss_scale)
```

```python
import numpy as np
import jax
import jax.numpy as jnp
import ml_dtypes
from jax import lax
from jax.experimental import pallas as pl
from jax.experimental.pallas import tpu as pltpu
from jax.sharding import PartitionSpec as P

MESH = pl.DeviceIdType.MESH
BF = jnp.bfloat16
F32 = jnp.float32
L, T, HID, W = 32, 16, 384, 128
OWN, PAD, GATES, TAPS = 12, 16, 4, 9
GR = GATES * PAD
CP = L * PAD


def one_hots():
    a = np.zeros((TAPS * GR, OWN * TAPS * GATES), np.float32)
    pack = np.zeros((TAPS * GR, 512), np.float32)
    unpack = np.zeros((OWN * TAPS * GATES, 512), np.float32)
    for k in range(TAPS):
        for j in range(GATES):
            for o in range(OWN):
                inner = k * GR + j * PAD + o
                outer = (o * TAPS + k) * GATES + j
                column = k * 48 + j * OWN + o + (0 if k < 5 else 16)
                a[inner, outer] = 1
                pack[inner, column] = 1
                unpack[outer, column] = 1
    e = np.zeros((HID, CP), np.float32)
    for i in range(L):
        for o in range(OWN):
            e[i * OWN + o, i * PAD + o] = 1
    spread = np.zeros((512, HID), np.float32)
    for q in range(4):
        for c in range(96):
            spread[128 * q + c, 96 * q + c] = 1
    rows = np.zeros((2, 48, 32), np.float32)
    for half in range(2):
        for c in range(24):
            rows[half, 24 * half + c, (c // OWN) * PAD + c % OWN] = 1
    return [x.astype(ml_dtypes.bfloat16) for x in (a, pack, unpack, e, e.T.copy(), spread, rows)]


def nn(a, b):
    return lax.dot_general(a, b, (((1,), (0,)), ((), ())), preferred_element_type=F32)


def nt(a, b):
    return lax.dot_general(a, b, (((1,), (1,)), ((), ())), preferred_element_type=F32)


def shifted(x, s):
    if s == 0:
        return x
    lane = lax.broadcasted_iota(jnp.int32, x.shape, 1)
    keep = lane < W - s if s > 0 else lane >= -s
    return jnp.where(keep, pltpu.roll(x, (-s) % W, 1), 0.0)


def shifted_rows(x, s):
    if s == 0:
        return x
    row = lax.broadcasted_iota(jnp.int32, x.shape, 0)
    keep = row < W - s if s > 0 else row >= -s
    return jnp.where(keep, pltpu.roll(x, (-s) % W, 0), 0.0)


(S_YX0, S_YX1, S_YX2, S_H1, S_H2, S_H3, S_YH1, S_YH2, S_COTH, S_COTB, S_FR, S_HB1, S_HB2, S_DH3, S_DH2, S_DH1,
 S_V, S_ST, S_STL, S_DZN2, S_DZN1, S_DZN0, S_DZF2, S_DZF1, S_DZF0, S_BI, S_WH, S_WF, S_PR, S_PT, S_PL, NSEM) = range(32)


def kernel(
    frames, wsrc, bias, hw, film, idx, cot, a_ref, pack, unpack, e_ref, et_ref, spread, rsel,
    wg_out, bg_out, hg_out, fg_out,
    wx, whp, whpt, yx, yh, rx, rh, hbuf, coth, cot4, cotb, fsend, fblk, hblk, dv_ref, dhp, dhr,
    v4, vblk, st_send, st_tile, stl_send, stl, dz_send, dzbuf, bi_send, bi, stack, scat,
    wsend, wrecv, xf, cc, vv, pbuf, prec, psum, ptile, plead, ssem, rsem,
):
    li = lax.axis_index("lead")
    ti = lax.axis_index("tile")

    def lead_dev(to):
        return (to, ti)

    def tile_dev(to):
        return (li, to)

    def send(src, dst, sem, dev):
        pltpu.make_async_remote_copy(
            src_ref=src, dst_ref=dst, send_sem=ssem.at[sem], recv_sem=rsem.at[sem], device_id=dev, device_id_type=MESH
        ).start()

    def got(ref, sem):
        pltpu.make_async_copy(ref, ref, rsem.at[sem]).wait()

    def sent(ref, sem):
        pltpu.make_async_copy(ref, ref, ssem.at[sem]).wait()

    def each_lead(fn):
        def body(d, carry):
            fn(lax.rem(li + d, L))
            return carry
        lax.fori_loop(1, L, body, 0)

    def each_tile(fn, first=1, last=T):
        def body(d, carry):
            fn(lax.rem(ti + d, T))
            return carry
        lax.fori_loop(first, last, body, 0)

    bar = pltpu.get_barrier_semaphore()
    each_lead(lambda to: pl.semaphore_signal(bar, inc=1, device_id=lead_dev(to), device_id_type=MESH))
    each_tile(lambda to: pl.semaphore_signal(bar, inc=1, device_id=tile_dev(to), device_id_type=MESH))

    up = lax.rem(ti + 1, T)
    down = lax.rem(ti + T - 1, T)
    has_up = ti < T - 1
    has_down = ti > 0

    wt = nn(a_ref[...], wsrc[...]).astype(BF)
    wx[...] = wt[:, :HID]
    wth = wt[:, HID:]
    whp[...] = nn(wth, e_ref[...]).astype(BF)
    whpt[...] = nt(et_ref[...], wth).astype(BF)

    def row_parts(g):
        parts = []
        for a in range(3):
            total = None
            for b in range(3):
                k = 3 * a + b
                term = shifted(g[k * GR:(k + 1) * GR], b - 1)
                total = term if total is None else total + term
            parts.append(total)
        return parts

    for t in range(3):
        parts = row_parts(nn(wx[...], frames[t]))
        for a in range(3):
            yx[t, a] = parts[a]
    for t in range(3):
        fsend[:, t] = nn(et_ref[...], frames[t]).astype(BF).reshape(T, 2 * PAD, W)
    for p in range(4):
        cot4[p] = cot[96 * p:96 * (p + 1), :]
    stack[...] = jnp.zeros_like(stack)
    cc[...] = jnp.zeros_like(cc)
    vv[...] = jnp.zeros_like(vv)
    pbuf[...] = jnp.zeros_like(pbuf)

    pl.semaphore_wait(bar, L + T - 2)

    def halo(src, dst, sem):
        send(src.at[0], dst.at[0], sem, tile_dev(up))
        send(src.at[2], dst.at[1], sem, tile_dev(down))

    for t in range(3):
        halo(yx.at[t], rx.at[t], (S_YX0, S_YX1, S_YX2)[t])
    send(cot, coth.at[0], S_COTH, tile_dev(lax.rem(ti + 2, T)))
    send(cot, coth.at[1], S_COTH, tile_dev(lax.rem(ti + T - 2, T)))

    def from_neighbours(r):
        return jnp.where(has_down, r[0], 0.0) + jnp.where(has_up, r[1], 0.0)

    def cell(z, previous):
        i_g = jax.nn.sigmoid(z[0:PAD])
        f_g = jax.nn.sigmoid(z[PAD:2 * PAD])
        g_g = jnp.tanh(z[2 * PAD:3 * PAD])
        o_g = jax.nn.sigmoid(z[3 * PAD:4 * PAD])
        now = f_g * previous + i_g * g_g
        return (i_g, f_g, g_g, o_g, previous, now), (o_g * jnp.tanh(now)).astype(BF)

    def share_h(t, h):
        buf = hbuf.at[t]
        buf[li] = h
        sem = (S_H1, S_H2, S_H3)[t]
        each_lead(lambda to: send(buf.at[li], buf.at[li], sem, lead_dev(to)))

    def await_h(t):
        got(hbuf.at[t, pl.ds(0, L - 1)], (S_H1, S_H2, S_H3)[t])

    saved = []
    got(rx.at[0], S_YX0)
    z = yx[0, 1] + from_neighbours(rx.at[0]) + bias[...]
    state, h = cell(z, jnp.zeros((PAD, W), F32))
    saved.append(state)
    share_h(0, h)

    mine = lax.div(ti, 4)

    def send_cot(to):
        send(cot4.at[lax.div(to, 4)], cotb.at[ti], S_COTB, tile_dev(to))

    def send_frames(to):
        send(fsend.at[to], fblk.at[ti], S_FR, tile_dev(to))

    for t in (1, 2):
        await_h(t - 1)
        parts = row_parts(nn(whp[...], hbuf[t - 1].reshape(CP, W)))
        for a in (0, 2):
            yh[t - 1, a] = parts[a]
        sem = (S_YH1, S_YH2)[t - 1]
        halo(yh.at[t - 1], rh.at[t - 1], sem)
        hsem = (S_HB1, S_HB2)[t - 1]
        hb = hblk.at[t - 1]
        hs = hbuf.at[t - 1]
        hb[ti] = hs[pl.ds(2 * ti, 2)]
        each_tile(lambda to: send(hs.at[pl.ds(2 * to, 2)], hb.at[ti], hsem, tile_dev(to)))
        got(rx.at[t], (S_YX0, S_YX1, S_YX2)[t])
        base = yx[t, 1] + from_neighbours(rx.at[t]) + bias[...] + parts[1]
        got(rh.at[t - 1], sem)
        z = base + from_neighbours(rh.at[t - 1])
        state, h = cell(z, saved[-1][5])
        saved.append(state)
        share_h(t, h)
        if t == 1:
            each_tile(send_frames)
            fblk[ti] = fsend[ti]
            got(coth, S_COTH)
            zero = jnp.zeros((HID, W), BF)
            rows = (jnp.where(ti < T - 2, coth[1], zero), cot[...], jnp.where(ti >= 2, coth[0], zero))
            dvt = jnp.zeros((W, HID), F32)
            for a in range(3):
                ct = rows[a].astype(F32).T
                for b in range(3):
                    k = 3 * a + b
                    dvt = dvt + nn(shifted_rows(ct, -2 * (b - 1)).astype(BF), hw[k * HID:(k + 1) * HID, :])
            dv = dvt.T
            dv_ref[...] = jnp.zeros_like(dv_ref)
            for i in range(L):
                dv_ref[0, i, 0:OWN, :] = dv[i * OWN:(i + 1) * OWN]
            dv_ref[1] = nn(et_ref[...], cot[...]).reshape(L, PAD, W)
        else:
            each_tile(send_cot)
            cotb[ti] = cot4[mine]

    await_h(2)
    h_wide = hbuf[2].reshape(CP, W).astype(F32)
    gamma = 1.0 + film[:, 0:1]
    u = gamma * h_wide + film[:, 1:2]
    s = jax.nn.sigmoid(u)
    du = dv_ref[0].reshape(CP, W) * s * (1.0 + u * (1.0 - s))
    dhp[0] = (dv_ref[1].reshape(CP, W) + gamma * du).reshape(L, PAD, W)

    def share_dh(n):
        sem = (S_DH3, S_DH2, S_DH1)[n]
        src = dhp.at[n]
        dst = dhr.at[n]
        each_lead(lambda to: send(src.at[to], dst.at[li], sem, lead_dev(to)))
        dst[li] = src[li]

    def await_dh(n):
        got(dhr.at[n, pl.ds(0, L - 1)], (S_DH3, S_DH2, S_DH1)[n])
        return jnp.sum(dhr[n], axis=0)

    share_dh(0)
    v = nn(e_ref[...], (u * s).astype(BF)).astype(BF)
    for q in range(4):
        v4[q] = v[96 * q:96 * (q + 1)]
    each_tile(lambda to: send(v4.at[lax.rem(to, 4)], vblk.at[ti], S_V, tile_dev(to)))
    vblk[ti] = v4[lax.rem(ti, 4)]
    for n, field in enumerate((du * h_wide, du)):
        line = jnp.sum(field.T, axis=0, keepdims=True)
        for q in range(4):
            st_send[4 * n + q:4 * n + q + 1, :] = line[:, 128 * q:128 * (q + 1)]
    each_tile(lambda to: send(st_send, st_tile.at[ti], S_ST, tile_dev(to)))
    st_tile[ti] = st_send[...]

    bias_sum = jnp.zeros((GR, W), F32)
    dc = jnp.zeros((PAD, W), F32)

    def gate_grads(n, dh, dc):
        i_g, f_g, g_g, o_g, previous, now = saved[2 - n]
        sq = jnp.tanh(now)
        dc = dc + dh * o_g * (1.0 - sq * sq)
        dz = jnp.concatenate(
            [
                dc * g_g * i_g * (1.0 - i_g),
                dc * previous * f_g * (1.0 - f_g),
                dc * i_g * (1.0 - g_g * g_g),
                dh * sq * o_g * (1.0 - o_g),
            ],
            0,
        )
        src = dz_send.at[n]
        dst = dzbuf.at[n]
        src[...] = dz.astype(BF)
        near = (S_DZN2, S_DZN1, S_DZN0)[n]
        far = (S_DZF2, S_DZF1, S_DZF0)[n]
        for to in (up, down):
            send(src, dst.at[ti], near, tile_dev(to))
        each_tile(lambda to: send(src, dst.at[ti], far, tile_dev(to)), 2, T - 1)
        dst[ti] = src[...]
        return dz, dc * f_g

    def await_near(n):
        got(dzbuf.at[n, pl.ds(0, 2)], (S_DZN2, S_DZN1, S_DZN0)[n])

    def await_far(n):
        got(dzbuf.at[n, pl.ds(0, T - 3)], (S_DZF2, S_DZF1, S_DZF0)[n])

    def back(n):
        zero = jnp.zeros((GR, W), F32)
        rows = (
            jnp.where(has_up, dzbuf[n, up].astype(F32), zero),
            dzbuf[n, ti].astype(F32),
            jnp.where(has_down, dzbuf[n, down].astype(F32), zero),
        )
        pieces = [shifted(rows[a], 1 - b).astype(BF) for a in range(3) for b in range(3)]
        dhp[n + 1] = nn(whpt[...], jnp.concatenate(pieces, 0)).reshape(L, PAD, W)

    def weight_part(n):
        t = 2 - n
        src = dzbuf.at[n]

        def body(row, carry):
            block = src[row].astype(F32)
            for b in range(3):
                piece = shifted(block, 1 - b).astype(BF)
                for a in range(3):
                    k = 3 * a + b
                    at = pl.multiple_of((row + a) * W, W)
                    stack[k * GR:(k + 1) * GR, pl.ds(at, W)] = piece
            at = pl.multiple_of(row * W, W)
            scat[0:2 * PAD, pl.ds(at, W)] = fblk[row, t]
            if t > 0:
                scat[2 * PAD:4 * PAD, pl.ds(at, W)] = hblk[t - 1, row].reshape(2 * PAD, W)
            return carry

        lax.fori_loop(0, T, body, 0)
        stack[0:3 * GR, T * W:(T + 1) * W] = jnp.zeros((3 * GR, W), BF)
        stack[6 * GR:9 * GR, W:2 * W] = jnp.zeros((3 * GR, W), BF)
        rows = 4 * PAD if t > 0 else 2 * PAD
        return nt(scat[0:rows, :], stack[:, W:(T + 1) * W])

    def share_weights(n, x):
        sem = (S_WH, S_WF)[n]
        y = nn((x * (1.0 / 256.0)).astype(BF), pack[...]).astype(BF)
        wsend[n] = (nn(rsel[0], y[:, :256]) + nn(rsel[1], y[:, 256:])).astype(BF)
        src = wsend.at[n]
        dst = wrecv.at[n]
        each_tile(lambda to: send(src, dst.at[ti], sem, tile_dev(to)))
        dst[ti] = src[...]

    def finish_weights(n):
        got(wrecv.at[n, pl.ds(0, T - 1)], (S_WH, S_WF)[n])
        for s_ in range(T):
            block = wrecv[n, s_].astype(F32)
            xf[24 * s_:24 * (s_ + 1), 0:256] = block[0:24]
            xf[24 * s_:24 * (s_ + 1), 256:512] = block[24:48]
        out = nt(unpack[...], xf[...].astype(BF)).astype(BF)
        col = HID * (1 - n)
        wg_out[:, col:col + HID] = out

    dz, dc = gate_grads(0, await_dh(0), dc)
    bias_sum = bias_sum + dz
    await_near(0)
    back(0)
    share_dh(1)

    got(st_tile.at[pl.ds(0, T - 1)], S_ST)
    stl_send[0:8, :] = jnp.sum(st_tile[...], axis=0)
    lane = lax.broadcasted_iota(jnp.int32, (8, W), 1)
    stl_send[8:16, :] = jnp.where(lane == idx[...], 1.0, 0.0)
    each_lead(lambda to: send(stl_send, stl.at[li], S_STL, lead_dev(to)))
    stl[li] = stl_send[...]

    got(cotb.at[pl.ds(0, T - 1)], S_COTB)
    got(vblk.at[pl.ds(0, T - 1)], S_V)

    def head_rows(row, carry):
        block = cotb[row].astype(F32)
        at = pl.multiple_of((row + 2) * W, W)
        for b in range(3):
            cc[96 * b:96 * (b + 1), pl.ds(at, W)] = shifted(block, 2 * (1 - b)).astype(BF)
        vv[0:96, pl.ds(pl.multiple_of(row * W, W), W)] = vblk[row]
        return carry

    lax.fori_loop(0, T, head_rows, 0)
    for a in range(3):
        first = (4 - 2 * a) * W
        part = nt(cc[:, first:first + T * W], vv[...])
        for b in range(3):
            k = 3 * a + b
            for d in range(4):
                pbuf[d * 256 + k * 24:d * 256 + (k + 1) * 24, :] = part[b * 96 + d * 24:b * 96 + (d + 1) * 24]
    each_lead(lambda to: send(pbuf.at[pl.ds(pl.multiple_of(32 * to, 32), 32)], prec.at[li], S_PR, lead_dev(to)))
    prec[li] = pbuf[pl.ds(pl.multiple_of(32 * li, 32), 32), :]

    dz, dc = gate_grads(1, await_dh(1), dc)
    bias_sum = bias_sum + dz
    await_near(1)
    back(1)
    share_dh(2)

    await_far(0)
    got(fblk.at[pl.ds(0, T - 1)], S_FR)
    got(hblk.at[1, pl.ds(0, T - 1)], S_HB2)
    grads = weight_part(0)
    await_far(1)
    got(hblk.at[0, pl.ds(0, T - 1)], S_HB1)
    grads = grads + weight_part(1)
    share_weights(0, grads[2 * PAD:4 * PAD])

    dz, dc = gate_grads(2, await_dh(2), dc)
    bias_sum = bias_sum + dz
    column = jnp.sum(bias_sum, axis=1, keepdims=True)
    lane = lax.broadcasted_iota(jnp.int32, (GR, W), 1)
    sub = lax.broadcasted_iota(jnp.int32, (GR, W), 0)
    line = jnp.sum(jnp.where(lane == sub, column, 0.0), axis=0, keepdims=True)
    bi_send[...] = jnp.broadcast_to(line, (8, W))
    each_tile(lambda to: send(bi_send, bi.at[ti], S_BI, tile_dev(to)))
    bi[ti] = bi_send[...]

    got(prec.at[pl.ds(0, L - 1)], S_PR)
    psum[...] = (jnp.sum(prec[...], axis=0) * (1.0 / 256.0)).astype(BF)
    owner = mine * 4 + lax.div(li, 8)
    quarter = lax.rem(ti, 4)

    @pl.when(owner != ti)
    def _():
        send(psum, ptile.at[quarter], S_PT, tile_dev(owner))

    await_near(2)
    await_far(2)
    grads0 = weight_part(2)
    share_weights(1, grads[0:2 * PAD] + grads0)

    @pl.when(owner == ti)
    def _():
        ptile[quarter] = psum[...]
        got(ptile.at[pl.ds(0, 3)], S_PT)
        each_lead(lambda to: send(ptile, plead.at[lax.rem(li, 8)], S_PL, lead_dev(to)))
        plead[lax.rem(li, 8)] = ptile[...]

    got(stl.at[pl.ds(0, L - 1)], S_STL)

    def table(l, acc):
        block = stl[l]
        return tuple(acc[m] + block[8:16, m:m + 1] * block[0:8, :] for m in range(16))

    acc = lax.fori_loop(0, L, table, tuple(jnp.zeros((8, W), F32) for _ in range(16)))
    for m in range(16):
        fg_out[m] = acc[m] * (1.0 / 256.0)
    got(bi.at[pl.ds(0, T - 1)], S_BI)
    bg_out[...] = jnp.sum(bi[...], axis=0) * (1.0 / 256.0)
    finish_weights(0)

    @pl.when(owner == ti)
    def _():
        got(plead.at[pl.ds(0, 7)], S_PL)

    @pl.when(owner != ti)
    def _():
        got(plead, S_PL)

    wide = jnp.concatenate([plead[:, q].reshape(256, W) for q in range(4)], 1)
    hg_out[...] = nn(wide, spread[...])[0:TAPS * 24].astype(BF)
    finish_weights(1)

    for t in range(3):
        sent(rx.at[t], (S_YX0, S_YX1, S_YX2)[t])
        sent(hbuf.at[t, pl.ds(0, L - 1)], (S_H1, S_H2, S_H3)[t])
        sent(dhr.at[t, pl.ds(0, L - 1)], (S_DH3, S_DH2, S_DH1)[t])
        sent(dzbuf.at[t, pl.ds(0, 2)], (S_DZN2, S_DZN1, S_DZN0)[t])
        sent(dzbuf.at[t, pl.ds(0, T - 3)], (S_DZF2, S_DZF1, S_DZF0)[t])
    for t in range(2):
        sent(rh.at[t], (S_YH1, S_YH2)[t])
        sent(hblk.at[t, pl.ds(0, T - 1)], (S_HB1, S_HB2)[t])
        sent(wrecv.at[t, pl.ds(0, T - 1)], (S_WH, S_WF)[t])
    sent(coth, S_COTH)
    sent(cotb.at[pl.ds(0, T - 1)], S_COTB)
    sent(fblk.at[pl.ds(0, T - 1)], S_FR)
    sent(vblk.at[pl.ds(0, T - 1)], S_V)
    sent(st_tile.at[pl.ds(0, T - 1)], S_ST)
    sent(stl.at[pl.ds(0, L - 1)], S_STL)
    sent(bi.at[pl.ds(0, T - 1)], S_BI)
    sent(prec.at[pl.ds(0, L - 1)], S_PR)

    @pl.when(owner != ti)
    def _():
        sent(psum, S_PT)

    @pl.when(owner == ti)
    def _():
        def body(d, carry):
            sent(ptile, S_PL)
            return carry
        lax.fori_loop(1, L, body, 0)


def shards(frames, enc_weight, enc_bias, head_weight, film_table, lead_index, cotangent):
    consts = [jnp.asarray(x) for x in one_hots()]
    wsrc = enc_weight.transpose(0, 2, 1, 3).reshape(OWN * TAPS * GATES, 2 * HID)
    bias = jnp.pad(enc_bias.T, ((0, 0), (0, PAD - OWN))).reshape(GR, 1)
    bias = jnp.broadcast_to(bias, (GR, W))
    chosen = (jnp.arange(film_table.shape[0]) == lead_index[0]).astype(F32)
    film = jnp.sum(chosen[:, None, None] * film_table, 0)
    film = jnp.pad(film.reshape(2, L, OWN), ((0, 0), (0, 0), (0, PAD - OWN))).reshape(2, CP).T
    idx = jnp.broadcast_to(lead_index.reshape(1, 1), (8, W))
    hw = head_weight.transpose(1, 0, 2).reshape(TAPS * HID, HID)
    vm = pltpu.VMEM
    outs = pl.pallas_call(
        kernel,
        out_shape=(
            jax.ShapeDtypeStruct((OWN * TAPS * GATES, 2 * HID), BF),
            jax.ShapeDtypeStruct((8, W), F32),
            jax.ShapeDtypeStruct((TAPS * 24, HID), BF),
            jax.ShapeDtypeStruct((16, 8, W), F32),
        ),
        in_specs=[pl.BlockSpec(memory_space=vm)] * 14,
        out_specs=(pl.BlockSpec(memory_space=vm),) * 4,
        scratch_shapes=[
            vm((TAPS * GR, HID), BF),
            vm((TAPS * GR, CP), BF),
            vm((CP, TAPS * GR), BF),
            vm((3, 3, GR, W), F32),
            vm((2, 3, GR, W), F32),
            vm((3, 2, GR, W), F32),
            vm((2, 2, GR, W), F32),
            vm((3, L, PAD, W), BF),
            vm((2, HID, W), BF),
            vm((4, 96, W), BF),
            vm((T, 96, W), BF),
            vm((T, 3, 2 * PAD, W), BF),
            vm((T, 3, 2 * PAD, W), BF),
            vm((2, T, 2, PAD, W), BF),
            vm((2, L, PAD, W), F32),
            vm((3, L, PAD, W), F32),
            vm((3, L, PAD, W), F32),
            vm((4, 96, W), BF),
            vm((T, 96, W), BF),
            vm((8, W), F32),
            vm((T, 8, W), F32),
            vm((16, W), F32),
            vm((L, 16, W), F32),
            vm((3, GR, W), BF),
            vm((3, T, GR, W), BF),
            vm((8, W), F32),
            vm((T, 8, W), F32),
            vm((TAPS * GR, (T + 2) * W), BF),
            vm((4 * PAD, T * W), BF),
            vm((2, 48, 256), BF),
            vm((2, T, 48, 256), BF),
            vm((HID, 512), F32),
            vm((3 * 96, (T + 4) * W), BF),
            vm((W, T * W), BF),
            vm((L * 32, W), F32),
            vm((L, 32, W), F32),
            vm((32, W), BF),
            vm((4, 32, W), BF),
            vm((8, 4, 32, W), BF),
            pltpu.SemaphoreType.DMA((NSEM,)),
            pltpu.SemaphoreType.DMA((NSEM,)),
        ],
        compiler_params=pltpu.CompilerParams(
            collective_id=0, has_side_effects=True, vmem_limit_bytes=56 * 2**20
        ),
    )(frames.reshape(3, HID, W), wsrc, bias, hw, film, idx, cotangent.reshape(HID, W), *consts)
    wg, bg, hg, fg = outs
    wg = wg.reshape(OWN, TAPS, GATES, 2 * HID).transpose(0, 2, 1, 3)
    bg = bg[0, :GR].reshape(GATES, PAD)[:, :OWN].T
    hg = hg.reshape(TAPS, 24, HID).transpose(1, 0, 2)
    fg = fg.reshape(16, 2, L, PAD)[..., :OWN].reshape(16, 2, HID)
    return wg, bg, hg, fg


def solution(mesh):
    in_specs = (
        P(None, None, "tile", None),
        P("lead", None, None, None),
        P("lead", None),
        P(),
        P(),
        P("lead"),
        P("lead", None, "tile", None),
    )
    out_specs = (P("lead", None, None, None), P("lead", None), P("tile", None, None), P())
    return jax.shard_map(shards, mesh=mesh, in_specs=in_specs, out_specs=out_specs, check_vma=False)
```

```python
import numpy as np
import jax
import jax.numpy as jnp
import ml_dtypes
from jax import lax
from jax.experimental import pallas as pl
from jax.experimental.pallas import tpu as pltpu
from jax.sharding import PartitionSpec as P

MESH = pl.DeviceIdType.MESH
BF = jnp.bfloat16
F32 = jnp.float32
L, T, HID, W = 32, 16, 384, 128
OWN, PAD, GATES, TAPS = 12, 16, 4, 9
GR = GATES * OWN
CP = L * PAD


def one_hots():
    a = np.zeros((TAPS * GR, OWN * TAPS * GATES), np.float32)
    pack = np.zeros((TAPS * GR, 512), np.float32)
    unpack = np.zeros((OWN * TAPS * GATES, 512), np.float32)
    for k in range(TAPS):
        for j in range(GATES):
            for o in range(OWN):
                inner = k * GR + j * OWN + o
                outer = (o * TAPS + k) * GATES + j
                column = inner + (0 if k < 5 else 16)
                a[inner, outer] = 1
                pack[inner, column] = 1
                unpack[outer, column] = 1
    e = np.zeros((HID, CP), np.float32)
    for i in range(L):
        for o in range(OWN):
            e[i * OWN + o, i * PAD + o] = 1
    spread = np.zeros((512, HID), np.float32)
    for q in range(4):
        for c in range(96):
            spread[128 * q + c, 96 * q + c] = 1
    rows = np.zeros((2, 48, 32), np.float32)
    for half in range(2):
        for c in range(24):
            rows[half, 24 * half + c, (c // OWN) * PAD + c % OWN] = 1
    return [x.astype(ml_dtypes.bfloat16) for x in (a, pack, unpack, e, e.T.copy(), spread, rows)]


def nn(a, b):
    return lax.dot_general(a, b, (((1,), (0,)), ((), ())), preferred_element_type=F32)


def nt(a, b):
    return lax.dot_general(a, b, (((1,), (1,)), ((), ())), preferred_element_type=F32)


def shifted(x, s):
    if s == 0:
        return x
    lane = lax.broadcasted_iota(jnp.int32, x.shape, 1)
    keep = lane < W - s if s > 0 else lane >= -s
    return jnp.where(keep, pltpu.roll(x, (-s) % W, 1), 0.0)


def shifted_rows(x, s):
    if s == 0:
        return x
    row = lax.broadcasted_iota(jnp.int32, x.shape, 0)
    keep = row < W - s if s > 0 else row >= -s
    return jnp.where(keep, pltpu.roll(x, (-s) % W, 0), 0.0)


(S_YX0, S_YX1, S_YX2, S_H1, S_H2, S_H3, S_YH1, S_YH2, S_COTH, S_COTB, S_FR, S_HB1, S_HB2, S_DH3, S_DH2, S_DH1,
 S_V, S_ST, S_STL, S_DZN2, S_DZN1, S_DZN0, S_DZF2, S_DZF1, S_DZF0, S_BI, S_WH, S_WF, S_PR, S_PT, S_PL, NSEM) = range(32)


N_IN = 14


def kernel(*refs):
    inputs, (wg_out, bg_out, hg_out, fg_out), refs = refs[:N_IN], refs[N_IN:N_IN + 4], refs[N_IN + 4:]
    held, refs = refs[:N_IN - 1], refs[N_IN - 1:]
    idx = inputs[N_IN - 1]
    (
        wx, whp, whpt, yx, yh, rx, rh, hbuf, coth, cot4, cotb, fsend, fblk, hblk, dv_ref, dhp, dhr,
        v4, vblk, st_send, st_tile, stl_send, stl, dz_send, dzbuf, bi_send, bi, stack, scat,
        wsend, wrecv, xf, cc, vv, pbuf, psend, prec, psum, ptile, plead, film_col, flat, ssem, rsem, lsem,
    ) = refs
    wsrc, a_ref, frames, e_ref, et_ref, bias, film, cot, hw, pack, rsel, unpack, spread = held
    li = lax.axis_index("lead")
    ti = lax.axis_index("tile")

    def lead_dev(to):
        return (to, ti)

    def tile_dev(to):
        return (li, to)

    def send(src, dst, sem, dev):
        pltpu.make_async_remote_copy(
            src_ref=src, dst_ref=dst, send_sem=ssem.at[sem], recv_sem=rsem.at[sem], device_id=dev, device_id_type=MESH
        ).start()

    def got(ref, sem):
        pltpu.make_async_copy(ref, ref, rsem.at[sem]).wait()

    def sent(ref, sem):
        pltpu.make_async_copy(ref, ref, ssem.at[sem]).wait()

    def load(n):
        return pltpu.make_async_copy(inputs[n], held[n], lsem.at[n])

    def each_lead(fn):
        ring, side, core = lax.rem(lax.div(li, 2), 8), lax.div(li, 16), lax.rem(li, 2)

        def body(n, carry):
            m = lax.div(n, 4)
            step = lax.div(m + 1, 2) * (1 - 2 * lax.rem(m, 2))
            other = lax.rem(ring + 12 + step, 8)
            rest = 3 - lax.rem(n, 4)
            side_to = lax.rem(side + lax.div(rest, 2), 2)
            core_to = lax.rem(core + lax.rem(rest, 2), 2)
            fn(side_to * 16 + other * 2 + core_to)
            return carry
        lax.fori_loop(0, L - 1, body, 0)

    def each_tile_far_first(fn):
        row, col = lax.div(ti, 4), lax.rem(ti, 4)

        def away(m):
            return 6 + lax.div(m + 1, 2) * (1 - 2 * lax.rem(m, 2))

        def body(n, carry):
            fn(lax.rem(row + away(lax.div(n, 4)), 4) * 4 + lax.rem(col + away(lax.rem(n, 4)), 4))
            return carry
        lax.fori_loop(0, T - 1, body, 0)

    def each_tile(fn, first=1, last=T):
        def body(d, carry):
            fn(lax.rem(ti + d, T))
            return carry
        lax.fori_loop(first, last, body, 0)

    bar = pltpu.get_barrier_semaphore()
    each_lead(lambda to: pl.semaphore_signal(bar, inc=1, device_id=lead_dev(to), device_id_type=MESH))
    each_tile_far_first(lambda to: pl.semaphore_signal(bar, inc=1, device_id=tile_dev(to), device_id_type=MESH))
    for n in range(N_IN - 1):
        load(n).start()

    up = lax.rem(ti + 1, T)
    down = lax.rem(ti + T - 1, T)
    has_up = ti < T - 1
    has_down = ti > 0

    for n in range(5):
        load(n).wait()
    wt = nn(a_ref[...], wsrc[...]).astype(BF)
    wx[...] = wt[:, :HID]
    wth = wt[:, HID:]
    whp[...] = nn(wth, e_ref[...]).astype(BF)
    whpt[...] = nt(et_ref[...], wth).astype(BF)

    def row_parts(g):
        parts = []
        for a in range(3):
            total = None
            for b in range(3):
                k = 3 * a + b
                term = shifted(g[k * GR:(k + 1) * GR], b - 1)
                total = term if total is None else total + term
            parts.append(total)
        return parts

    own_x = []
    for t in range(3):
        parts = row_parts(nn(wx[...], frames[t]))
        for a in (0, 2):
            yx[t, a] = parts[a].astype(BF)
        own_x.append(parts[1])
    for t in range(3):
        fsend[:, t] = nn(et_ref[...], frames[t]).astype(BF).reshape(T, 2 * PAD, W)
    for n in range(5, N_IN - 1):
        load(n).wait()
    sub = lax.broadcasted_iota(jnp.int32, (OWN, OWN), 0)
    lane = lax.broadcasted_iota(jnp.int32, (OWN, OWN), 1)
    bias_cols = [jnp.sum(jnp.where(sub == lane, bias[j:j + 1, :], 0.0), axis=1, keepdims=True) for j in range(GATES)]
    slot = lax.broadcasted_iota(jnp.int32, (16, 2, HID), 0)
    lines = jnp.sum(jnp.where(slot == idx[0], film[...], 0.0), axis=0)
    lines = jnp.concatenate([lines, jnp.zeros((6, HID), F32)], 0).T
    film_col[...] = jnp.zeros_like(film_col)
    for i in range(L):
        film_col[i, 0:OWN, :] = lines[i * OWN:(i + 1) * OWN]
    for p in range(4):
        cot4[p] = cot[96 * p:96 * (p + 1), :]
    stack[...] = jnp.zeros_like(stack)
    cc[...] = jnp.zeros_like(cc)
    vv[...] = jnp.zeros_like(vv)
    pbuf[...] = jnp.zeros_like(pbuf)

    pl.semaphore_wait(bar, L + T - 2)

    def halo(src, dst, sem):
        send(src.at[0], dst.at[0], sem, tile_dev(up))
        send(src.at[2], dst.at[1], sem, tile_dev(down))

    for t in range(3):
        halo(yx.at[t], rx.at[t], (S_YX0, S_YX1, S_YX2)[t])
    def from_neighbours(r):
        return jnp.where(has_down, r[0].astype(F32), 0.0) + jnp.where(has_up, r[1].astype(F32), 0.0)

    def padded(x):
        return jnp.concatenate([x, jnp.zeros((PAD - OWN, W), F32)], 0)

    def cell(z, previous):
        z = [padded(z[j * OWN:(j + 1) * OWN] + bias_cols[j]) for j in range(GATES)]
        i_g = jax.nn.sigmoid(z[0])
        f_g = jax.nn.sigmoid(z[1])
        g_g = jnp.tanh(z[2])
        o_g = jax.nn.sigmoid(z[3])
        now = f_g * previous + i_g * g_g
        return (i_g, f_g, g_g, o_g, previous, now), (o_g * jnp.tanh(now)).astype(BF)

    def share_h(t, h):
        buf = hbuf.at[t]
        buf[li] = h
        sem = (S_H1, S_H2, S_H3)[t]
        each_lead(lambda to: send(buf.at[li], buf.at[li], sem, lead_dev(to)))

    def await_h(t):
        got(hbuf.at[t, pl.ds(0, L - 1)], (S_H1, S_H2, S_H3)[t])

    saved = []
    got(rx.at[0], S_YX0)
    z = own_x[0] + from_neighbours(rx.at[0])
    state, h = cell(z, jnp.zeros((PAD, W), F32))
    saved.append(state)
    share_h(0, h)
    send(cot, coth.at[0], S_COTH, tile_dev(lax.rem(ti + 2, T)))
    send(cot, coth.at[1], S_COTH, tile_dev(lax.rem(ti + T - 2, T)))

    mine = lax.div(ti, 4)

    def send_cot(to):
        send(cot4.at[lax.div(to, 4)], cotb.at[ti], S_COTB, tile_dev(to))

    def send_frames(to):
        send(fsend.at[to], fblk.at[ti], S_FR, tile_dev(to))

    for t in (1, 2):
        await_h(t - 1)
        parts = row_parts(nn(whp[...], hbuf[t - 1].reshape(CP, W)))
        for a in (0, 2):
            yh[t - 1, a] = parts[a].astype(BF)
        sem = (S_YH1, S_YH2)[t - 1]
        halo(yh.at[t - 1], rh.at[t - 1], sem)
        got(rx.at[t], (S_YX0, S_YX1, S_YX2)[t])
        base = own_x[t] + from_neighbours(rx.at[t]) + parts[1]
        got(rh.at[t - 1], sem)
        z = base + from_neighbours(rh.at[t - 1])
        state, h = cell(z, saved[-1][5])
        saved.append(state)
        share_h(t, h)
        if t == 1:
            each_tile(send_frames)
            fblk[ti] = fsend[ti]
            got(coth, S_COTH)
            zero = jnp.zeros((HID, W), BF)
            rows = (jnp.where(ti < T - 2, coth[1], zero), cot[...], jnp.where(ti >= 2, coth[0], zero))
            dvt = jnp.zeros((W, HID), F32)
            for a in range(3):
                ct = rows[a].astype(F32).T
                for b in range(3):
                    k = 3 * a + b
                    dvt = dvt + nn(shifted_rows(ct, -2 * (b - 1)).astype(BF), hw[k * HID:(k + 1) * HID, :])
            dv = dvt.T
            dv_ref[...] = jnp.zeros_like(dv_ref)
            for i in range(L):
                dv_ref[0, i, 0:OWN, :] = dv[i * OWN:(i + 1) * OWN]
            dv_ref[1] = nn(et_ref[...], cot[...]).reshape(L, PAD, W)
        else:
            each_tile(send_cot)
            cotb[ti] = cot4[mine]

    def share_blocks(t):
        hsem = (S_HB1, S_HB2)[t]
        hb = hblk.at[t]
        hs = hbuf.at[t]
        hb[ti] = hs[pl.ds(2 * ti, 2)]
        each_tile_far_first(lambda to: send(hs.at[pl.ds(2 * to, 2)], hb.at[ti], hsem, tile_dev(to)))

    await_h(2)
    h_wide = hbuf[2].reshape(CP, W).astype(F32)
    columns = film_col[...].reshape(CP, 8)
    gamma = 1.0 + columns[:, 0:1]
    u = gamma * h_wide + columns[:, 1:2]
    s = jax.nn.sigmoid(u)
    du = dv_ref[0].reshape(CP, W) * s * (1.0 + u * (1.0 - s))
    dhp[0] = (dv_ref[1].reshape(CP, W) + gamma * du).astype(BF).reshape(L, PAD, W)

    def share_dh(n):
        sem = (S_DH3, S_DH2, S_DH1)[n]
        src = dhp.at[n]
        dst = dhr.at[n]
        each_lead(lambda to: send(src.at[to], dst.at[li], sem, lead_dev(to)))
        dst[li] = src[li]

    def await_dh(n):
        got(dhr.at[n, pl.ds(0, L - 1)], (S_DH3, S_DH2, S_DH1)[n])
        return jnp.sum(dhr[n].astype(F32), axis=0)

    share_dh(0)
    v = nn(e_ref[...], (u * s).astype(BF)).astype(BF)
    for q in range(4):
        v4[q] = v[96 * q:96 * (q + 1)]
    each_tile(lambda to: send(v4.at[lax.rem(to, 4)], vblk.at[ti], S_V, tile_dev(to)))
    vblk[ti] = v4[lax.rem(ti, 4)]
    st_send[...] = jnp.zeros_like(st_send)
    for n, field in enumerate((du * h_wide, du)):
        for i in range(L):
            flat[i * OWN:(i + 1) * OWN, :] = field[i * PAD:i * PAD + OWN]
        line = jnp.sum(flat[...].T, axis=0, keepdims=True)
        for q in range(3):
            st_send[3 * n + q:3 * n + q + 1, :] = line[:, 128 * q:128 * (q + 1)]
    each_tile(lambda to: send(st_send, st_tile.at[ti], S_ST, tile_dev(to)))
    st_tile[ti] = st_send[...]

    bias_sum = jnp.zeros((GR, W), F32)
    dc = jnp.zeros((PAD, W), F32)

    def gate_grads(n, dh, dc):
        i_g, f_g, g_g, o_g, previous, now = saved[2 - n]
        sq = jnp.tanh(now)
        dc = dc + dh * o_g * (1.0 - sq * sq)
        dz = jnp.concatenate(
            [x[0:OWN] for x in (
                dc * g_g * i_g * (1.0 - i_g),
                dc * previous * f_g * (1.0 - f_g),
                dc * i_g * (1.0 - g_g * g_g),
                dh * sq * o_g * (1.0 - o_g),
            )],
            0,
        )
        src = dz_send.at[n]
        dst = dzbuf.at[n]
        src[...] = dz.astype(BF)
        near = (S_DZN2, S_DZN1, S_DZN0)[n]
        far = (S_DZF2, S_DZF1, S_DZF0)[n]
        dst[ti] = src[...]
        if n < 2:
            for to in (up, down):
                send(src, dst.at[ti], near, tile_dev(to))
        else:
            each_tile_far_first(lambda to: send(src, dst.at[ti], far, tile_dev(to)))
        return dz, dc * f_g

    def share_far(n):
        src = dz_send.at[n]
        dst = dzbuf.at[n]
        each_tile(lambda to: send(src, dst.at[ti], (S_DZF2, S_DZF1)[n], tile_dev(to)), 2, T - 1)

    def await_near(n):
        got(dzbuf.at[n, pl.ds(0, 2)], (S_DZN2, S_DZN1, S_DZN0)[n])

    def await_far(n):
        got(dzbuf.at[n, pl.ds(0, T - 3 if n < 2 else T - 1)], (S_DZF2, S_DZF1, S_DZF0)[n])

    def back(n):
        zero = jnp.zeros((GR, W), F32)
        rows = (
            jnp.where(has_up, dzbuf[n, up].astype(F32), zero),
            dzbuf[n, ti].astype(F32),
            jnp.where(has_down, dzbuf[n, down].astype(F32), zero),
        )
        pieces = [shifted(rows[a], 1 - b).astype(BF) for a in range(3) for b in range(3)]
        dhp[n + 1] = nn(whpt[...], jnp.concatenate(pieces, 0)).astype(BF).reshape(L, PAD, W)

    def weight_part(n):
        t = 2 - n
        src = dzbuf.at[n]

        def body(row, carry):
            block = src[row].astype(F32)
            for b in range(3):
                piece = shifted(block, 1 - b).astype(BF)
                for a in range(3):
                    k = 3 * a + b
                    at = pl.multiple_of((row + a) * W, W)
                    stack[k * GR:(k + 1) * GR, pl.ds(at, W)] = piece
            at = pl.multiple_of(row * W, W)
            scat[0:2 * PAD, pl.ds(at, W)] = fblk[row, t]
            if t > 0:
                scat[2 * PAD:4 * PAD, pl.ds(at, W)] = hblk[t - 1, row].reshape(2 * PAD, W)
            return carry

        lax.fori_loop(0, T, body, 0)
        stack[0:3 * GR, T * W:(T + 1) * W] = jnp.zeros((3 * GR, W), BF)
        stack[6 * GR:9 * GR, W:2 * W] = jnp.zeros((3 * GR, W), BF)
        rows = 4 * PAD if t > 0 else 2 * PAD
        return nt(scat[0:rows, :], stack[:, W:(T + 1) * W])

    def share_weights(n, x):
        sem = (S_WH, S_WF)[n]
        y = nn((x * (1.0 / 256.0)).astype(BF), pack[...]).astype(BF)
        wsend[n] = (nn(rsel[0], y[:, :256]) + nn(rsel[1], y[:, 256:])).astype(BF)
        src = wsend.at[n]
        dst = wrecv.at[n]
        each_tile(lambda to: send(src, dst.at[ti], sem, tile_dev(to)))
        dst[ti] = src[...]

    def finish_weights(n):
        got(wrecv.at[n, pl.ds(0, T - 1)], (S_WH, S_WF)[n])
        for s_ in range(T):
            block = wrecv[n, s_].astype(F32)
            xf[24 * s_:24 * (s_ + 1), 0:256] = block[0:24]
            xf[24 * s_:24 * (s_ + 1), 256:512] = block[24:48]
        out = nt(unpack[...], xf[...].astype(BF)).astype(BF)
        col = HID * (1 - n)
        wg_out[:, col:col + HID] = out

    dz, dc = gate_grads(0, await_dh(0), dc)
    bias_sum = bias_sum + dz
    await_near(0)
    back(0)
    share_dh(1)
    share_far(0)
    share_blocks(1)
    share_blocks(0)

    got(st_tile.at[pl.ds(0, T - 1)], S_ST)
    stl_send[0:8, :] = jnp.sum(st_tile[...], axis=0)
    lane = lax.broadcasted_iota(jnp.int32, (8, W), 1)
    stl_send[8:16, :] = jnp.where(lane == idx[0], 1.0, 0.0)
    each_lead(lambda to: send(stl_send, stl.at[li], S_STL, lead_dev(to)))
    stl[li] = stl_send[...]

    got(cotb.at[pl.ds(0, T - 1)], S_COTB)
    got(vblk.at[pl.ds(0, T - 1)], S_V)

    def head_rows(row, carry):
        block = cotb[row].astype(F32)
        at = pl.multiple_of((row + 2) * W, W)
        for b in range(3):
            cc[96 * b:96 * (b + 1), pl.ds(at, W)] = shifted(block, 2 * (1 - b)).astype(BF)
        vv[0:96, pl.ds(pl.multiple_of(row * W, W), W)] = vblk[row]
        return carry

    lax.fori_loop(0, T, head_rows, 0)
    for a in range(3):
        first = (4 - 2 * a) * W
        part = nt(cc[:, first:first + T * W], vv[...])
        for b in range(3):
            k = 3 * a + b
            for d in range(4):
                pbuf[d * 256 + k * 24:d * 256 + (k + 1) * 24, :] = part[b * 96 + d * 24:b * 96 + (d + 1) * 24]
    psend[...] = pbuf[...].astype(BF).reshape(L, 32, W)
    each_lead(lambda to: send(psend.at[to], prec.at[li], S_PR, lead_dev(to)))
    prec[li] = psend[li]

    dz, dc = gate_grads(1, await_dh(1), dc)
    bias_sum = bias_sum + dz
    await_near(1)
    back(1)
    share_dh(2)
    share_far(1)

    await_far(0)
    got(fblk.at[pl.ds(0, T - 1)], S_FR)
    got(hblk.at[1, pl.ds(0, T - 1)], S_HB2)
    grads = weight_part(0)
    await_far(1)
    got(hblk.at[0, pl.ds(0, T - 1)], S_HB1)
    grads = grads + weight_part(1)
    share_weights(0, grads[2 * PAD:4 * PAD])

    dz, dc = gate_grads(2, await_dh(2), dc)
    bias_sum = bias_sum + dz
    column = jnp.sum(bias_sum, axis=1, keepdims=True)
    lane = lax.broadcasted_iota(jnp.int32, (GR, W), 1)
    sub = lax.broadcasted_iota(jnp.int32, (GR, W), 0)
    line = jnp.sum(jnp.where(lane == sub, column, 0.0), axis=0, keepdims=True)
    bi_send[...] = jnp.broadcast_to(line, (8, W))
    each_tile(lambda to: send(bi_send, bi.at[ti], S_BI, tile_dev(to)))
    bi[ti] = bi_send[...]

    got(prec.at[pl.ds(0, L - 1)], S_PR)
    psum[...] = (jnp.sum(prec[...].astype(F32), axis=0) * (1.0 / 256.0)).astype(BF)
    owner = mine * 4 + lax.div(li, 8)
    quarter = lax.rem(ti, 4)

    @pl.when(owner != ti)
    def _():
        send(psum, ptile.at[quarter], S_PT, tile_dev(owner))

    await_far(2)
    grads0 = weight_part(2)
    share_weights(1, grads[0:2 * PAD] + grads0)

    @pl.when(owner == ti)
    def _():
        ptile[quarter] = psum[...]
        got(ptile.at[pl.ds(0, 3)], S_PT)
        each_lead(lambda to: send(ptile, plead.at[lax.rem(li, 8)], S_PL, lead_dev(to)))
        plead[lax.rem(li, 8)] = ptile[...]

    got(stl.at[pl.ds(0, L - 1)], S_STL)

    def table(l, acc):
        block = stl[l]
        return tuple(acc[m] + block[8:16, m:m + 1] * block[0:8, :] for m in range(16))

    acc = lax.fori_loop(0, L, table, tuple(jnp.zeros((8, W), F32) for _ in range(16)))
    for m in range(16):
        fg_out[m] = acc[m] * (1.0 / 256.0)
    got(bi.at[pl.ds(0, T - 1)], S_BI)
    bg_out[...] = jnp.sum(bi[...], axis=0) * (1.0 / 256.0)
    finish_weights(0)

    @pl.when(owner == ti)
    def _():
        got(plead.at[pl.ds(0, 7)], S_PL)

    @pl.when(owner != ti)
    def _():
        got(plead, S_PL)

    wide = jnp.concatenate([plead[:, q].reshape(256, W) for q in range(4)], 1)
    hg_out[...] = nn(wide, spread[...])[0:TAPS * 24].astype(BF)
    finish_weights(1)

    for t in range(3):
        sent(rx.at[t], (S_YX0, S_YX1, S_YX2)[t])
        sent(hbuf.at[t, pl.ds(0, L - 1)], (S_H1, S_H2, S_H3)[t])
        sent(dhr.at[t, pl.ds(0, L - 1)], (S_DH3, S_DH2, S_DH1)[t])
    sent(dzbuf.at[2, pl.ds(0, T - 1)], S_DZF0)
    for t in range(2):
        sent(dzbuf.at[t, pl.ds(0, 2)], (S_DZN2, S_DZN1)[t])
        sent(dzbuf.at[t, pl.ds(0, T - 3)], (S_DZF2, S_DZF1)[t])
        sent(rh.at[t], (S_YH1, S_YH2)[t])
        sent(hblk.at[t, pl.ds(0, T - 1)], (S_HB1, S_HB2)[t])
        sent(wrecv.at[t, pl.ds(0, T - 1)], (S_WH, S_WF)[t])
    sent(coth, S_COTH)
    sent(cotb.at[pl.ds(0, T - 1)], S_COTB)
    sent(fblk.at[pl.ds(0, T - 1)], S_FR)
    sent(vblk.at[pl.ds(0, T - 1)], S_V)
    sent(st_tile.at[pl.ds(0, T - 1)], S_ST)
    sent(stl.at[pl.ds(0, L - 1)], S_STL)
    sent(bi.at[pl.ds(0, T - 1)], S_BI)
    sent(prec.at[pl.ds(0, L - 1)], S_PR)

    @pl.when(owner != ti)
    def _():
        sent(psum, S_PT)

    @pl.when(owner == ti)
    def _():
        def body(d, carry):
            sent(ptile, S_PL)
            return carry
        lax.fori_loop(1, L, body, 0)


def finish(wg, bg, hg, fg, wg_out, bg_out, hg_out, fg_out):
    wg_out[...] = wg[...].astype(F32).reshape(OWN, TAPS, GATES, 2 * HID).astype(BF)
    hg_out[...] = hg[...]
    for j in range(GATES):
        bg_out[j:j + 1, :] = bg[0:1, j * OWN:(j + 1) * OWN]
    for m in range(16):
        for n in range(2):
            for q in range(3):
                fg_out[m, n:n + 1, W * q:W * (q + 1)] = fg[m, 3 * n + q:3 * n + q + 1, :]


def shards(frames, enc_weight, enc_bias, head_weight, film_table, lead_index, cotangent):
    a, pack, unpack, e, et, spread, rsel = [jnp.asarray(x) for x in one_hots()]
    wsrc = enc_weight.transpose(0, 2, 1, 3).reshape(OWN * TAPS * GATES, 2 * HID)
    hw = head_weight.transpose(1, 0, 2).reshape(TAPS * HID, HID)
    vm = pltpu.VMEM
    inputs = (
        wsrc, a, frames.reshape(3, HID, W), e, et, enc_bias.T, film_table, cotangent.reshape(HID, W), hw, pack, rsel,
        unpack, spread,
    )
    outs = pl.pallas_call(
        kernel,
        out_shape=(
            jax.ShapeDtypeStruct((OWN * TAPS * GATES, 2 * HID), BF),
            jax.ShapeDtypeStruct((8, W), F32),
            jax.ShapeDtypeStruct((TAPS * 24, HID), BF),
            jax.ShapeDtypeStruct((16, 8, W), F32),
        ),
        in_specs=[pl.BlockSpec(memory_space=pl.ANY)] * (N_IN - 1) + [pl.BlockSpec(memory_space=pltpu.SMEM)],
        out_specs=(pl.BlockSpec(memory_space=vm),) * 4,
        scratch_shapes=[vm(x.shape, x.dtype) for x in inputs] + [
            vm((TAPS * GR, HID), BF),
            vm((TAPS * GR, CP), BF),
            vm((CP, TAPS * GR), BF),
            vm((3, 3, GR, W), BF),
            vm((2, 3, GR, W), BF),
            vm((3, 2, GR, W), BF),
            vm((2, 2, GR, W), BF),
            vm((3, L, PAD, W), BF),
            vm((2, HID, W), BF),
            vm((4, 96, W), BF),
            vm((T, 96, W), BF),
            vm((T, 3, 2 * PAD, W), BF),
            vm((T, 3, 2 * PAD, W), BF),
            vm((2, T, 2, PAD, W), BF),
            vm((2, L, PAD, W), F32),
            vm((3, L, PAD, W), BF),
            vm((3, L, PAD, W), BF),
            vm((4, 96, W), BF),
            vm((T, 96, W), BF),
            vm((8, W), F32),
            vm((T, 8, W), F32),
            vm((16, W), F32),
            vm((L, 16, W), F32),
            vm((3, GR, W), BF),
            vm((3, T, GR, W), BF),
            vm((8, W), F32),
            vm((T, 8, W), F32),
            vm((TAPS * GR, (T + 2) * W), BF),
            vm((4 * PAD, T * W), BF),
            vm((2, 48, 256), BF),
            vm((2, T, 48, 256), BF),
            vm((HID, 512), F32),
            vm((3 * 96, (T + 4) * W), BF),
            vm((W, T * W), BF),
            vm((L * 32, W), F32),
            vm((L, 32, W), BF),
            vm((L, 32, W), BF),
            vm((32, W), BF),
            vm((4, 32, W), BF),
            vm((8, 4, 32, W), BF),
            vm((L, PAD, 8), F32),
            vm((HID, W), F32),
            pltpu.SemaphoreType.DMA((NSEM,)),
            pltpu.SemaphoreType.DMA((NSEM,)),
            pltpu.SemaphoreType.DMA((N_IN - 1,)),
        ],
        compiler_params=pltpu.CompilerParams(
            collective_id=0, has_side_effects=True, vmem_limit_bytes=56 * 2**20
        ),
    )(*inputs, lead_index)
    wg, bg, hg, fg = pl.pallas_call(
        finish,
        out_shape=(
            jax.ShapeDtypeStruct((OWN, TAPS, GATES, 2 * HID), BF),
            jax.ShapeDtypeStruct((GATES, OWN), F32),
            jax.ShapeDtypeStruct((TAPS * 24, HID), BF),
            jax.ShapeDtypeStruct((16, 2, HID), F32),
        ),
        in_specs=[pl.BlockSpec(memory_space=vm)] * 4,
        out_specs=(pl.BlockSpec(memory_space=vm),) * 4,
    )(*outs)
    return wg.transpose(0, 2, 1, 3), bg.T, hg.reshape(TAPS, 24, HID).transpose(1, 0, 2), fg


def solution(mesh):
    in_specs = (
        P(None, None, "tile", None),
        P("lead", None, None, None),
        P("lead", None),
        P(),
        P(),
        P("lead"),
        P("lead", None, "tile", None),
    )
    out_specs = (P("lead", None, None, None), P("lead", None), P("tile", None, None), P())
    return jax.shard_map(shards, mesh=mesh, in_specs=in_specs, out_specs=out_specs, check_vma=False)
```

```python
import numpy as np
import jax
import jax.numpy as jnp
import ml_dtypes
from jax import lax
from jax.experimental import pallas as pl
from jax.experimental.pallas import tpu as pltpu
from jax.sharding import PartitionSpec as P

MESH = pl.DeviceIdType.MESH
BF = jnp.bfloat16
F32 = jnp.float32
L, T, HID, W = 32, 16, 384, 128
OWN, PAD, GATES, TAPS = 12, 16, 4, 9
GR = GATES * OWN
CP = L * PAD


def one_hots():
    a = np.zeros((TAPS * GR, OWN * TAPS * GATES), np.float32)
    pack = np.zeros((TAPS * GR, 512), np.float32)
    unpack = np.zeros((OWN * TAPS * GATES, 512), np.float32)
    for k in range(TAPS):
        for j in range(GATES):
            for o in range(OWN):
                inner = k * GR + j * OWN + o
                outer = (o * TAPS + k) * GATES + j
                column = inner + (0 if k < 5 else 16)
                a[inner, outer] = 1
                pack[inner, column] = 1
                unpack[outer, column] = 1
    e = np.zeros((HID, CP), np.float32)
    for i in range(L):
        for o in range(OWN):
            e[i * OWN + o, i * PAD + o] = 1
    spread = np.zeros((512, HID), np.float32)
    for q in range(4):
        for c in range(96):
            spread[128 * q + c, 96 * q + c] = 1
    rows = np.zeros((2, 48, 32), np.float32)
    for half in range(2):
        for c in range(24):
            rows[half, 24 * half + c, (c // OWN) * PAD + c % OWN] = 1
    return [x.astype(ml_dtypes.bfloat16) for x in (a, pack, unpack, e, e.T.copy(), spread, rows)]


def nn(a, b):
    return lax.dot_general(a, b, (((1,), (0,)), ((), ())), preferred_element_type=F32)


def nt(a, b):
    return lax.dot_general(a, b, (((1,), (1,)), ((), ())), preferred_element_type=F32)


def shifted(x, s):
    if s == 0:
        return x
    lane = lax.broadcasted_iota(jnp.int32, x.shape, 1)
    keep = lane < W - s if s > 0 else lane >= -s
    return jnp.where(keep, pltpu.roll(x, (-s) % W, 1), 0.0)


def shifted_rows(x, s):
    if s == 0:
        return x
    row = lax.broadcasted_iota(jnp.int32, x.shape, 0)
    keep = row < W - s if s > 0 else row >= -s
    return jnp.where(keep, pltpu.roll(x, (-s) % W, 0), 0.0)


(S_YX0, S_YX1, S_YX2, S_H1, S_H2, S_H3, S_YH1, S_YH2, S_COTH, S_COTZ, S_COTX, S_FR, S_FRC, S_HB1, S_HB2, S_HB1C, S_HB2C,
 S_DH3, S_DH2, S_DH1, S_HQ, S_HQC, S_ST, S_STL, S_DZN2, S_DZN1, S_DZ0, S_DZZ2, S_DZZ1, S_DZX2, S_DZX1, S_BI, S_WHZ, S_WHX, S_WF,
 S_PR, S_PT, S_PL, NSEM) = range(39)


N_IN = 14


def kernel(*refs):
    inputs, (wg_out, bg_out, hg_out, fg_out), refs = refs[:N_IN], refs[N_IN:N_IN + 4], refs[N_IN + 4:]
    held, refs = refs[:N_IN - 1], refs[N_IN - 1:]
    idx = inputs[N_IN - 1]
    (
        wx, whp, whpt, yx, yh, rx, rh, hbuf, coth, cot4, cotz, cotb, fsend, fblk, hblk, dv_ref, dhp, dhr,
        h8, hq, st_send, st_tile, stl_send, stl, dz_send, dznear, dzbuf, bi_send, bi, stack, scat,
        wsend, wrecv, xf, cc, vv, pbuf, psend, prec, psum, ptile, plead, film_col, film_q, flat, ssem, rsem, lsem,
    ) = refs
    wsrc, a_ref, frames, e_ref, et_ref, bias, film, cot, hw, pack, rsel, unpack, spread = held
    li = lax.axis_index("lead")
    ti = lax.axis_index("tile")

    def lead_dev(to):
        return (to, ti)

    def tile_dev(to):
        return (li, to)

    def send(src, dst, sem, dev):
        pltpu.make_async_remote_copy(
            src_ref=src, dst_ref=dst, send_sem=ssem.at[sem], recv_sem=rsem.at[sem], device_id=dev, device_id_type=MESH
        ).start()

    def got(ref, sem):
        pltpu.make_async_copy(ref, ref, rsem.at[sem]).wait()

    def sent(ref, sem):
        pltpu.make_async_copy(ref, ref, ssem.at[sem]).wait()

    def load(n):
        return pltpu.make_async_copy(inputs[n], held[n], lsem.at[n])

    def each_lead(fn):
        ring, side = lax.rem(lax.div(li, 2), 8), lax.div(li, 16)

        def body(n, carry):
            m = lax.div(n, 4)
            step = lax.div(m + 1, 2) * (1 - 2 * lax.rem(m, 2))
            other = lax.rem(ring + 12 + step, 8)
            rest = 3 - lax.rem(n, 4)
            side_to = lax.rem(side + lax.div(rest, 2), 2)
            core_to = lax.rem(core + lax.rem(rest, 2), 2)
            fn(side_to * 16 + other * 2 + core_to)
            return carry
        lax.fori_loop(0, L - 1, body, 0)

    row, col = lax.div(ti, 4), lax.rem(ti, 4)
    core = lax.rem(li, 2)
    partner = lead_dev(li + 1 - 2 * core)

    def each_z(fn):
        for m in (2, 1, 3):
            fn(lax.rem(col + m, 4))

    def each_x(fn):
        for m in (2, 1, 3):
            fn(lax.rem(row + m, 4))

    def each_tile_far_first(fn):

        def away(m):
            return 6 + lax.div(m + 1, 2) * (1 - 2 * lax.rem(m, 2))

        def body(n, carry):
            fn(lax.rem(row + away(lax.div(n, 4)), 4) * 4 + lax.rem(col + away(lax.rem(n, 4)), 4))
            return carry
        lax.fori_loop(0, T - 1, body, 0)

    def each_tile(fn, first=1, last=T):
        def body(d, carry):
            fn(lax.rem(ti + d, T))
            return carry
        lax.fori_loop(first, last, body, 0)

    bar = pltpu.get_barrier_semaphore()
    each_lead(lambda to: pl.semaphore_signal(bar, inc=1, device_id=lead_dev(to), device_id_type=MESH))
    each_tile_far_first(lambda to: pl.semaphore_signal(bar, inc=1, device_id=tile_dev(to), device_id_type=MESH))
    for n in range(N_IN - 1):
        load(n).start()

    up = lax.rem(ti + 1, T)
    down = lax.rem(ti + T - 1, T)
    has_up = ti < T - 1
    has_down = ti > 0

    for n in range(5):
        load(n).wait()
    wt = nn(a_ref[...], wsrc[...]).astype(BF)
    wx[...] = wt[:, :HID]
    wth = wt[:, HID:]
    whp[...] = nn(wth, e_ref[...]).astype(BF)
    whpt[...] = nt(et_ref[...], wth).astype(BF)

    def row_parts(g):
        parts = []
        for a in range(3):
            total = None
            for b in range(3):
                k = 3 * a + b
                term = shifted(g[k * GR:(k + 1) * GR], b - 1)
                total = term if total is None else total + term
            parts.append(total)
        return parts

    own_x = []
    for t in range(3):
        parts = row_parts(nn(wx[...], frames[t]))
        for a in (0, 2):
            yx[t, a] = parts[a]
        own_x.append(parts[1])
    for t in range(3):
        fsend[:, 2 * t:2 * t + 2] = nn(et_ref[...], frames[t]).astype(BF).reshape(T, 2, PAD, W)
    for n in range(5, N_IN - 1):
        load(n).wait()
    sub = lax.broadcasted_iota(jnp.int32, (OWN, OWN), 0)
    lane = lax.broadcasted_iota(jnp.int32, (OWN, OWN), 1)
    bias_cols = [jnp.sum(jnp.where(sub == lane, bias[j:j + 1, :], 0.0), axis=1, keepdims=True) for j in range(GATES)]
    slot = lax.broadcasted_iota(jnp.int32, (16, 2, HID), 0)
    lines = jnp.sum(jnp.where(slot == idx[0], film[...], 0.0), axis=0)
    lines = jnp.concatenate([lines, jnp.zeros((6, HID), F32)], 0).T
    film_col[...] = jnp.zeros_like(film_col)
    for i in range(L):
        film_col[i, 0:OWN, :] = lines[i * OWN:(i + 1) * OWN]
    film_q[...] = lines.reshape(4, 96, 8)
    for p in range(4):
        cot4[p] = cot[96 * p:96 * (p + 1), :]
    stack[...] = jnp.zeros_like(stack)
    cc[...] = jnp.zeros_like(cc)
    vv[...] = jnp.zeros_like(vv)
    pbuf[...] = jnp.zeros_like(pbuf)

    pl.semaphore_wait(bar, L + T - 2)

    def halo(src, dst, sem):
        send(src.at[0], dst.at[0], sem, tile_dev(up))
        send(src.at[2], dst.at[1], sem, tile_dev(down))

    halo(yx.at[0], rx.at[0], S_YX0)
    def from_neighbours(r):
        return jnp.where(has_down, r[0], 0.0) + jnp.where(has_up, r[1], 0.0)

    def padded(x):
        return jnp.concatenate([x, jnp.zeros((PAD - OWN, W), F32)], 0)

    def cell(z, previous):
        z = [padded(z[j * OWN:(j + 1) * OWN] + bias_cols[j]) for j in range(GATES)]
        i_g = jax.nn.sigmoid(z[0])
        f_g = jax.nn.sigmoid(z[1])
        g_g = jnp.tanh(z[2])
        o_g = jax.nn.sigmoid(z[3])
        now = f_g * previous + i_g * g_g
        return (i_g, f_g, g_g, o_g, previous, now), (o_g * jnp.tanh(now)).astype(BF)

    def share_h(t, h):
        buf = hbuf.at[t]
        buf[li] = h
        sem = (S_H1, S_H2, S_H3)[t]
        each_lead(lambda to: send(buf.at[li], buf.at[li], sem, lead_dev(to)))

    def await_h(t):
        got(hbuf.at[t, pl.ds(0, L - 1)], (S_H1, S_H2, S_H3)[t])

    saved = []
    got(rx.at[0], S_YX0)
    z = own_x[0] + from_neighbours(rx.at[0])
    state, h = cell(z, jnp.zeros((PAD, W), F32))
    saved.append(state)
    share_h(0, h)
    halo(yx.at[1], rx.at[1], S_YX1)
    halo(yx.at[2], rx.at[2], S_YX2)
    send(cot, coth.at[0], S_COTH, tile_dev(lax.rem(ti + 2, T)))

    def half(x):
        return x.at[pl.ds(3 * core, 3)]

    def send_frames(to):
        send(half(fsend.at[to]), half(fblk.at[ti]), S_FR, tile_dev(to))

    for t in (1, 2):
        await_h(t - 1)
        parts = row_parts(nn(whp[...], hbuf[t - 1].reshape(CP, W)))
        for a in (0, 2):
            yh[t - 1, a] = parts[a]
        sem = (S_YH1, S_YH2)[t - 1]
        halo(yh.at[t - 1], rh.at[t - 1], sem)
        got(rx.at[t], (S_YX0, S_YX1, S_YX2)[t])
        base = own_x[t] + from_neighbours(rx.at[t]) + parts[1]
        got(rh.at[t - 1], sem)
        z = base + from_neighbours(rh.at[t - 1])
        state, h = cell(z, saved[-1][5])
        saved.append(state)
        share_h(t, h)
        if t == 1:
            send(cot, coth.at[1], S_COTH, tile_dev(lax.rem(ti + T - 2, T)))
    each_tile_far_first(send_frames)
    fblk[ti, pl.ds(3 * core, 3)] = fsend[ti, pl.ds(3 * core, 3)]
    each_z(lambda to: send(cot4.at[to], cotz.at[col], S_COTZ, tile_dev(row * 4 + to)))
    cotz[col] = cot4[col]
    got(coth, S_COTH)
    zero = jnp.zeros((HID, W), BF)
    rows = (jnp.where(ti < T - 2, coth[1], zero), cot[...], jnp.where(ti >= 2, coth[0], zero))
    dvt = jnp.zeros((W, HID), F32)
    for a in range(3):
        ct = rows[a].astype(F32).T
        for b in range(3):
            k = 3 * a + b
            dvt = dvt + nn(shifted_rows(ct, -2 * (b - 1)).astype(BF), hw[k * HID:(k + 1) * HID, :])
    dv = dvt.T
    dv_ref[...] = jnp.zeros_like(dv_ref)
    for i in range(L):
        dv_ref[0, i, 0:OWN, :] = dv[i * OWN:(i + 1) * OWN]
    dv_ref[1] = nn(et_ref[...], cot[...]).reshape(L, PAD, W)

    def share_blocks(t):
        hsem = (S_HB1, S_HB2)[t]
        hb = hblk.at[t]
        hs = hbuf.at[t]
        hb[ti, core] = hs[2 * ti + core]
        each_tile_far_first(lambda to: send(hs.at[2 * to + core], hb.at[ti, core], hsem, tile_dev(to)))

    def swap_blocks(t):
        got(hblk.at[t, pl.ds(0, T - 1), 0], (S_HB1, S_HB2)[t])
        mine = hblk.at[t, :, core]
        send(mine, mine, (S_HB1C, S_HB2C)[t], partner)

    def await_blocks(t):
        got(hblk.at[t, :, 0], (S_HB1C, S_HB2C)[t])

    await_h(2)
    h_wide = hbuf[2].reshape(CP, W).astype(F32)
    columns = film_col[...].reshape(CP, 8)
    gamma = 1.0 + columns[:, 0:1]
    u = gamma * h_wide + columns[:, 1:2]
    s = jax.nn.sigmoid(u)
    du = dv_ref[0].reshape(CP, W) * s * (1.0 + u * (1.0 - s))
    dhp[0] = (dv_ref[1].reshape(CP, W) + gamma * du).astype(BF).reshape(L, PAD, W)

    def share_dh(n):
        sem = (S_DH3, S_DH2, S_DH1)[n]
        src = dhp.at[n]
        dst = dhr.at[n]
        each_lead(lambda to: send(src.at[to], dst.at[li], sem, lead_dev(to)))
        dst[li] = src[li]

    def await_dh(n):
        got(dhr.at[n, pl.ds(0, L - 1)], (S_DH3, S_DH2, S_DH1)[n])
        return jnp.sum(dhr[n].astype(F32), axis=0)

    share_dh(0)
    h8[...] = nn(e_ref[...], hbuf[2].reshape(CP, W)).astype(BF).reshape(8, 48, W)
    each_tile_far_first(lambda to: send(h8.at[2 * lax.div(to, 4) + core], hq.at[ti, core], S_HQ, tile_dev(to)))
    hq[ti, core] = h8[2 * row + core]
    got(cotz.at[pl.ds(0, 3)], S_COTZ)
    each_x(lambda to: send(cotz, cotb.at[pl.ds(4 * row, 4)], S_COTX, tile_dev(to * 4 + col)))
    cotb[pl.ds(4 * row, 4)] = cotz[...]
    st_send[...] = jnp.zeros_like(st_send)
    for n, field in enumerate((du * h_wide, du)):
        for i in range(L):
            flat[i * OWN:(i + 1) * OWN, :] = field[i * PAD:i * PAD + OWN]
        line = jnp.sum(flat[...].T, axis=0, keepdims=True)
        for q in range(3):
            st_send[3 * n + q:3 * n + q + 1, :] = line[:, 128 * q:128 * (q + 1)]
    each_tile_far_first(lambda to: send(st_send, st_tile.at[ti], S_ST, tile_dev(to)))
    st_tile[ti] = st_send[...]
    got(fblk.at[pl.ds(0, T - 1), pl.ds(0, 3)], S_FR)
    fr_mine = fblk.at[:, pl.ds(3 * core, 3)]
    send(fr_mine, fr_mine, S_FRC, partner)

    bias_sum = jnp.zeros((GR, W), F32)
    dc = jnp.zeros((PAD, W), F32)

    def gate_grads(n, dh, dc):
        i_g, f_g, g_g, o_g, previous, now = saved[2 - n]
        sq = jnp.tanh(now)
        dc = dc + dh * o_g * (1.0 - sq * sq)
        dz = jnp.concatenate(
            [x[0:OWN] for x in (
                dc * g_g * i_g * (1.0 - i_g),
                dc * previous * f_g * (1.0 - f_g),
                dc * i_g * (1.0 - g_g * g_g),
                dh * sq * o_g * (1.0 - o_g),
            )],
            0,
        )
        src = dz_send.at[n]
        dst = dzbuf.at[n]
        src[...] = dz.astype(BF)
        dst[ti] = src[...]
        if n < 2:
            send(src, dznear.at[n, 0], (S_DZN2, S_DZN1)[n], tile_dev(up))
            send(src, dznear.at[n, 1], (S_DZN2, S_DZN1)[n], tile_dev(down))
        else:
            each_tile_far_first(lambda to: send(src, dst.at[ti], S_DZ0, tile_dev(to)))
        return dz, dc * f_g

    def await_near(n):
        got(dznear.at[n], (S_DZN2, S_DZN1)[n])

    def share_z(n):
        each_z(lambda to: send(dz_send.at[n], dzbuf.at[n, ti], (S_DZZ2, S_DZZ1)[n], tile_dev(row * 4 + to)))

    def share_x(n):
        got(dzbuf.at[n, pl.ds(0, 3)], (S_DZZ2, S_DZZ1)[n])
        mine = dzbuf.at[n, pl.ds(4 * row, 4)]
        each_x(lambda to: send(mine, mine, (S_DZX2, S_DZX1)[n], tile_dev(to * 4 + col)))

    def await_x(n):
        got(dzbuf.at[n, pl.ds(0, 12)], (S_DZX2, S_DZX1)[n])

    def back(n):
        zero = jnp.zeros((GR, W), F32)
        rows = (
            jnp.where(has_up, dznear[n, 1].astype(F32), zero),
            dz_send[n].astype(F32),
            jnp.where(has_down, dznear[n, 0].astype(F32), zero),
        )
        pieces = [shifted(rows[a], 1 - b).astype(BF) for a in range(3) for b in range(3)]
        dhp[n + 1] = nn(whpt[...], jnp.concatenate(pieces, 0)).astype(BF).reshape(L, PAD, W)

    def weight_part(n):
        t = 2 - n
        src = dzbuf.at[n]

        def body(row, carry):
            block = src[row].astype(F32)
            for b in range(3):
                piece = shifted(block, 1 - b).astype(BF)
                for a in range(3):
                    k = 3 * a + b
                    at = pl.multiple_of((row + a) * W, W)
                    stack[k * GR:(k + 1) * GR, pl.ds(at, W)] = piece
            at = pl.multiple_of(row * W, W)
            scat[0:2 * PAD, pl.ds(at, W)] = fblk[row, 2 * t:2 * t + 2].reshape(2 * PAD, W)
            if t > 0:
                scat[2 * PAD:4 * PAD, pl.ds(at, W)] = hblk[t - 1, row].reshape(2 * PAD, W)
            return carry

        lax.fori_loop(0, T, body, 0)
        stack[0:3 * GR, T * W:(T + 1) * W] = jnp.zeros((3 * GR, W), BF)
        stack[6 * GR:9 * GR, W:2 * W] = jnp.zeros((3 * GR, W), BF)
        rows = 4 * PAD if t > 0 else 2 * PAD
        return nt(scat[0:rows, :], stack[:, W:(T + 1) * W])

    def share_weights(n, x):
        y = nn((x * (1.0 / 256.0)).astype(BF), pack[...]).astype(BF)
        wsend[n] = (nn(rsel[0], y[:, :256]) + nn(rsel[1], y[:, 256:])).astype(BF)
        src = wsend.at[n]
        dst = wrecv.at[n]
        dst[ti] = src[...]
        if n == 0:
            each_z(lambda to: send(src, dst.at[ti], S_WHZ, tile_dev(row * 4 + to)))
        else:
            each_tile_far_first(lambda to: send(src, dst.at[ti], S_WF, tile_dev(to)))

    def share_weights_x():
        got(wrecv.at[0, pl.ds(0, 3)], S_WHZ)
        mine = wrecv.at[0, pl.ds(4 * row, 4)]
        each_x(lambda to: send(mine, mine, S_WHX, tile_dev(to * 4 + col)))

    def finish_weights(n):
        if n == 0:
            got(wrecv.at[0, pl.ds(0, 12)], S_WHX)
        else:
            got(wrecv.at[1, pl.ds(0, T - 1)], S_WF)
        for s_ in range(T):
            block = wrecv[n, s_].astype(F32)
            xf[24 * s_:24 * (s_ + 1), 0:256] = block[0:24]
            xf[24 * s_:24 * (s_ + 1), 256:512] = block[24:48]
        out = nt(unpack[...], xf[...].astype(BF)).astype(BF)
        col = HID * (1 - n)
        wg_out[:, col:col + HID] = out

    dz, dc = gate_grads(0, await_dh(0), dc)
    bias_sum = bias_sum + dz
    await_near(0)
    back(0)
    share_dh(1)
    share_z(0)
    got(hq.at[pl.ds(0, T - 1), 0], S_HQ)
    hq_mine = hq.at[:, core]
    send(hq_mine, hq_mine, S_HQC, partner)
    share_blocks(1)
    share_blocks(0)
    share_x(0)

    got(st_tile.at[pl.ds(0, T - 1)], S_ST)
    stl_send[0:8, :] = jnp.sum(st_tile[...], axis=0)
    lane = lax.broadcasted_iota(jnp.int32, (8, W), 1)
    stl_send[8:16, :] = jnp.where(lane == idx[0], 1.0, 0.0)
    each_lead(lambda to: send(stl_send, stl.at[li], S_STL, lead_dev(to)))
    stl[li] = stl_send[...]

    got(hq.at[:, 0], S_HQC)
    got(cotb.at[pl.ds(0, 12)], S_COTX)
    gamma_q = 1.0 + film_q[row, :, 0:1]
    beta_q = film_q[row, :, 1:2]

    def head_rows(r, carry):
        block = cotb[r].astype(F32)
        at = pl.multiple_of((r + 2) * W, W)
        for b in range(3):
            cc[96 * b:96 * (b + 1), pl.ds(at, W)] = shifted(block, 2 * (1 - b)).astype(BF)
        uq = gamma_q * hq[r].reshape(96, W).astype(F32) + beta_q
        vv[0:96, pl.ds(pl.multiple_of(r * W, W), W)] = (uq * jax.nn.sigmoid(uq)).astype(BF)
        return carry

    lax.fori_loop(0, T, head_rows, 0)
    for a in range(3):
        first = (4 - 2 * a) * W
        part = nt(cc[:, first:first + T * W], vv[...])
        for b in range(3):
            k = 3 * a + b
            for d in range(4):
                pbuf[d * 256 + k * 24:d * 256 + (k + 1) * 24, :] = part[b * 96 + d * 24:b * 96 + (d + 1) * 24]
    psend[...] = pbuf[...].astype(BF).reshape(L, 32, W)
    prec[li] = psend[li]

    dz, dc = gate_grads(1, await_dh(1), dc)
    bias_sum = bias_sum + dz
    await_near(1)
    back(1)
    share_dh(2)
    share_z(1)
    each_lead(lambda to: send(psend.at[to], prec.at[li], S_PR, lead_dev(to)))
    swap_blocks(1)
    swap_blocks(0)
    share_x(1)
    await_x(0)
    got(fblk.at[:, pl.ds(0, 3)], S_FRC)
    await_blocks(1)
    grads = weight_part(0)

    dz, dc = gate_grads(2, await_dh(2), dc)
    await_x(1)
    await_blocks(0)
    grads = grads + weight_part(1)
    share_weights(0, grads[2 * PAD:4 * PAD])
    bias_sum = bias_sum + dz
    column = jnp.sum(bias_sum, axis=1, keepdims=True)
    lane = lax.broadcasted_iota(jnp.int32, (GR, W), 1)
    sub = lax.broadcasted_iota(jnp.int32, (GR, W), 0)
    line = jnp.sum(jnp.where(lane == sub, column, 0.0), axis=0, keepdims=True)
    bi_send[...] = jnp.broadcast_to(line, (8, W))
    each_tile_far_first(lambda to: send(bi_send, bi.at[ti], S_BI, tile_dev(to)))
    bi[ti] = bi_send[...]

    got(prec.at[pl.ds(0, L - 1)], S_PR)
    psum[...] = (jnp.sum(prec[...].astype(F32), axis=0) * (1.0 / 256.0)).astype(BF)
    owner = col * 4 + lax.div(li, 8)
    gathers = lax.div(li, 8) == col

    @pl.when(owner != ti)
    def _():
        send(psum, ptile.at[row], S_PT, tile_dev(owner))

    @pl.when(owner == ti)
    def _():
        ptile[row] = psum[...]

    got(dzbuf.at[2, pl.ds(0, T - 1)], S_DZ0)
    grads0 = weight_part(2)
    share_weights(1, grads[0:2 * PAD] + grads0)
    share_weights_x()

    @pl.when(gathers)
    def _():
        @pl.when(owner == ti)
        def _():
            got(ptile.at[pl.ds(0, 3)], S_PT)

        @pl.when(owner != ti)
        def _():
            got(ptile, S_PT)

        each_lead(lambda to: send(ptile, plead.at[lax.rem(li, 8)], S_PL, lead_dev(to)))
        plead[lax.rem(li, 8)] = ptile[...]

    got(stl.at[pl.ds(0, L - 1)], S_STL)

    def table(l, acc):
        block = stl[l]
        return tuple(acc[m] + block[8:16, m:m + 1] * block[0:8, :] for m in range(16))

    acc = lax.fori_loop(0, L, table, tuple(jnp.zeros((8, W), F32) for _ in range(16)))
    for m in range(16):
        fg_out[m] = acc[m] * (1.0 / 256.0)
    got(bi.at[pl.ds(0, T - 1)], S_BI)
    bg_out[...] = jnp.sum(bi[...], axis=0) * (1.0 / 256.0)
    finish_weights(0)

    @pl.when(gathers)
    def _():
        got(plead.at[pl.ds(0, 7)], S_PL)

    @pl.when(jnp.logical_not(gathers))
    def _():
        got(plead, S_PL)

    wide = jnp.concatenate([plead[:, q].reshape(256, W) for q in range(4)], 1)
    hg_out[...] = nn(wide, spread[...])[0:TAPS * 24].astype(BF)
    finish_weights(1)

    for t in range(3):
        sent(rx.at[t], (S_YX0, S_YX1, S_YX2)[t])
        sent(hbuf.at[t, pl.ds(0, L - 1)], (S_H1, S_H2, S_H3)[t])
        sent(dhr.at[t, pl.ds(0, L - 1)], (S_DH3, S_DH2, S_DH1)[t])
    for t in range(2):
        sent(rh.at[t], (S_YH1, S_YH2)[t])
        sent(dznear.at[t], (S_DZN2, S_DZN1)[t])
        sent(dzbuf.at[t, pl.ds(0, 3)], (S_DZZ2, S_DZZ1)[t])
        sent(dzbuf.at[t, pl.ds(0, 12)], (S_DZX2, S_DZX1)[t])
        sent(hblk.at[t, pl.ds(0, T - 1), 0], (S_HB1, S_HB2)[t])
        sent(hblk.at[t, :, 0], (S_HB1C, S_HB2C)[t])
    sent(dzbuf.at[2, pl.ds(0, T - 1)], S_DZ0)
    sent(wrecv.at[0, pl.ds(0, 3)], S_WHZ)
    sent(wrecv.at[0, pl.ds(0, 12)], S_WHX)
    sent(wrecv.at[1, pl.ds(0, T - 1)], S_WF)
    sent(coth, S_COTH)
    sent(cotz.at[pl.ds(0, 3)], S_COTZ)
    sent(cotb.at[pl.ds(0, 12)], S_COTX)
    sent(fblk.at[pl.ds(0, T - 1), pl.ds(0, 3)], S_FR)
    sent(fblk.at[:, pl.ds(0, 3)], S_FRC)
    sent(hq.at[pl.ds(0, T - 1), 0], S_HQ)
    sent(hq.at[:, 0], S_HQC)
    sent(st_tile.at[pl.ds(0, T - 1)], S_ST)
    sent(stl.at[pl.ds(0, L - 1)], S_STL)
    sent(bi.at[pl.ds(0, T - 1)], S_BI)
    sent(prec.at[pl.ds(0, L - 1)], S_PR)

    @pl.when(owner != ti)
    def _():
        sent(psum, S_PT)

    @pl.when(gathers)
    def _():
        def body(d, carry):
            sent(ptile, S_PL)
            return carry
        lax.fori_loop(1, L, body, 0)


def finish(wg, bg, hg, fg, wg_out, bg_out, hg_out, fg_out):
    wg_out[...] = wg[...].astype(F32).reshape(OWN, TAPS, GATES, 2 * HID).astype(BF)
    hg_out[...] = hg[...]
    for j in range(GATES):
        bg_out[j:j + 1, :] = bg[0:1, j * OWN:(j + 1) * OWN]
    for m in range(16):
        for n in range(2):
            for q in range(3):
                fg_out[m, n:n + 1, W * q:W * (q + 1)] = fg[m, 3 * n + q:3 * n + q + 1, :]


def shards(frames, enc_weight, enc_bias, head_weight, film_table, lead_index, cotangent):
    a, pack, unpack, e, et, spread, rsel = [jnp.asarray(x) for x in one_hots()]
    wsrc = enc_weight.transpose(0, 2, 1, 3).reshape(OWN * TAPS * GATES, 2 * HID)
    hw = head_weight.transpose(1, 0, 2).reshape(TAPS * HID, HID)
    vm = pltpu.VMEM
    inputs = (
        wsrc, a, frames.reshape(3, HID, W), e, et, enc_bias.T, film_table, cotangent.reshape(HID, W), hw, pack, rsel,
        unpack, spread,
    )
    outs = pl.pallas_call(
        kernel,
        out_shape=(
            jax.ShapeDtypeStruct((OWN * TAPS * GATES, 2 * HID), BF),
            jax.ShapeDtypeStruct((8, W), F32),
            jax.ShapeDtypeStruct((TAPS * 24, HID), BF),
            jax.ShapeDtypeStruct((16, 8, W), F32),
        ),
        in_specs=[pl.BlockSpec(memory_space=pl.ANY)] * (N_IN - 1) + [pl.BlockSpec(memory_space=pltpu.SMEM)],
        out_specs=(pl.BlockSpec(memory_space=vm),) * 4,
        scratch_shapes=[vm(x.shape, x.dtype) for x in inputs] + [
            vm((TAPS * GR, HID), BF),
            vm((TAPS * GR, CP), BF),
            vm((CP, TAPS * GR), BF),
            vm((3, 3, GR, W), F32),
            vm((2, 3, GR, W), F32),
            vm((3, 2, GR, W), F32),
            vm((2, 2, GR, W), F32),
            vm((3, L, PAD, W), BF),
            vm((2, HID, W), BF),
            vm((4, 96, W), BF),
            vm((4, 96, W), BF),
            vm((T, 96, W), BF),
            vm((T, 6, PAD, W), BF),
            vm((T, 6, PAD, W), BF),
            vm((2, T, 2, PAD, W), BF),
            vm((2, L, PAD, W), F32),
            vm((3, L, PAD, W), BF),
            vm((3, L, PAD, W), BF),
            vm((8, 48, W), BF),
            vm((T, 2, 48, W), BF),
            vm((8, W), F32),
            vm((T, 8, W), F32),
            vm((16, W), F32),
            vm((L, 16, W), F32),
            vm((3, GR, W), BF),
            vm((2, 2, GR, W), BF),
            vm((3, T, GR, W), BF),
            vm((8, W), F32),
            vm((T, 8, W), F32),
            vm((TAPS * GR, (T + 2) * W), BF),
            vm((4 * PAD, T * W), BF),
            vm((2, 48, 256), BF),
            vm((2, T, 48, 256), BF),
            vm((HID, 512), F32),
            vm((3 * 96, (T + 4) * W), BF),
            vm((W, T * W), BF),
            vm((L * 32, W), F32),
            vm((L, 32, W), BF),
            vm((L, 32, W), BF),
            vm((32, W), BF),
            vm((4, 32, W), BF),
            vm((8, 4, 32, W), BF),
            vm((L, PAD, 8), F32),
            vm((4, 96, 8), F32),
            vm((HID, W), F32),
            pltpu.SemaphoreType.DMA((NSEM,)),
            pltpu.SemaphoreType.DMA((NSEM,)),
            pltpu.SemaphoreType.DMA((N_IN - 1,)),
        ],
        compiler_params=pltpu.CompilerParams(
            collective_id=0, has_side_effects=True, vmem_limit_bytes=56 * 2**20
        ),
    )(*inputs, lead_index)
    wg, bg, hg, fg = pl.pallas_call(
        finish,
        out_shape=(
            jax.ShapeDtypeStruct((OWN, TAPS, GATES, 2 * HID), BF),
            jax.ShapeDtypeStruct((GATES, OWN), F32),
            jax.ShapeDtypeStruct((TAPS * 24, HID), BF),
            jax.ShapeDtypeStruct((16, 2, HID), F32),
        ),
        in_specs=[pl.BlockSpec(memory_space=vm)] * 4,
        out_specs=(pl.BlockSpec(memory_space=vm),) * 4,
    )(*outs)
    return wg.transpose(0, 2, 1, 3), bg.T, hg.reshape(TAPS, 24, HID).transpose(1, 0, 2), fg


def solution(mesh):
    in_specs = (
        P(None, None, "tile", None),
        P("lead", None, None, None),
        P("lead", None),
        P(),
        P(),
        P("lead"),
        P("lead", None, "tile", None),
    )
    out_specs = (P("lead", None, None, None), P("lead", None), P("tile", None, None), P())
    return jax.shard_map(shards, mesh=mesh, in_specs=in_specs, out_specs=out_specs, check_vma=False)
```

```python
import numpy as np
import jax
import jax.numpy as jnp
import ml_dtypes
from jax import lax
from jax.experimental import pallas as pl
from jax.experimental.pallas import tpu as pltpu
from jax.sharding import PartitionSpec as P

MESH = pl.DeviceIdType.MESH
BF = jnp.bfloat16
F32 = jnp.float32
L, T, HID, W = 32, 16, 384, 128
OWN, PAD, GATES, TAPS = 12, 16, 4, 9
GR = GATES * OWN
CP = L * PAD


def one_hots():
    a = np.zeros((TAPS * GR, OWN * TAPS * GATES), np.float32)
    pack = np.zeros((TAPS * GR, 512), np.float32)
    unpack = np.zeros((OWN * TAPS * GATES, 512), np.float32)
    for k in range(TAPS):
        for j in range(GATES):
            for o in range(OWN):
                inner = k * GR + j * OWN + o
                outer = (o * TAPS + k) * GATES + j
                column = inner + (0 if k < 5 else 16)
                a[inner, outer] = 1
                pack[inner, column] = 1
                unpack[outer, column] = 1
    e = np.zeros((HID, CP), np.float32)
    for i in range(L):
        for o in range(OWN):
            e[i * OWN + o, i * PAD + o] = 1
    spread = np.zeros((512, HID), np.float32)
    for q in range(4):
        for c in range(96):
            spread[128 * q + c, 96 * q + c] = 1
    rows = np.zeros((2, 48, 32), np.float32)
    for half in range(2):
        for c in range(24):
            rows[half, 24 * half + c, (c // OWN) * PAD + c % OWN] = 1
    return [x.astype(ml_dtypes.bfloat16) for x in (a, pack, unpack, e, e.T.copy(), spread, rows)]


def nn(a, b):
    return lax.dot_general(a, b, (((1,), (0,)), ((), ())), preferred_element_type=F32)


def nt(a, b):
    return lax.dot_general(a, b, (((1,), (1,)), ((), ())), preferred_element_type=F32)


def shifted(x, s):
    if s == 0:
        return x
    lane = lax.broadcasted_iota(jnp.int32, x.shape, 1)
    keep = lane < W - s if s > 0 else lane >= -s
    return jnp.where(keep, pltpu.roll(x, (-s) % W, 1), 0.0)


def shifted_rows(x, s):
    if s == 0:
        return x
    row = lax.broadcasted_iota(jnp.int32, x.shape, 0)
    keep = row < W - s if s > 0 else row >= -s
    return jnp.where(keep, pltpu.roll(x, (-s) % W, 0), 0.0)


(S_YX0, S_YX1, S_YX2, S_H1, S_H2, S_H3, S_YH1, S_YH2, S_COTH, S_COTZ, S_COTX, S_FR, S_FRC, S_HB1, S_HB2, S_HB1C, S_HB2C,
 S_DH3, S_DH2, S_DH1, S_HQ, S_HQC, S_ST, S_STL, S_DZN2, S_DZN1, S_DZ0, S_DZZ2, S_DZZ1, S_DZX2, S_DZX1, S_BI, S_WHZ, S_WHX, S_WF,
 S_WFA, S_WFB, S_PR, S_PT, S_PL, NSEM) = range(41)


N_IN = 14


def kernel(*refs):
    inputs, (wg_out, bg_out, hg_out, fg_out), refs = refs[:N_IN], refs[N_IN:N_IN + 4], refs[N_IN + 4:]
    held, refs = refs[:N_IN - 1], refs[N_IN - 1:]
    idx = inputs[N_IN - 1]
    (
        wt, whp, whpt, yx, yh, rx, rh, hbuf, coth, cot4, cotz, cotb, fsend, fblk, hblk, dv_ref, dhp, dhr,
        h8, hq, st_send, st_tile, stl_send, stl, dz_send, dznear, dzbuf, bi_send, bi, stack, scat,
        wsend, wrecv, xf, cc, vv, pbuf, psend, prec, psum, ptile, plead, film_col, film_q, flat, ssem, rsem, lsem,
    ) = refs
    wsrc, a_ref, frames, bias, e_ref, et_ref, film, cot, hw, pack, rsel, unpack, spread = held
    li = lax.axis_index("lead")
    ti = lax.axis_index("tile")

    def lead_dev(to):
        return (to, ti)

    def tile_dev(to):
        return (li, to)

    def send(src, dst, sem, dev):
        pltpu.make_async_remote_copy(
            src_ref=src, dst_ref=dst, send_sem=ssem.at[sem], recv_sem=rsem.at[sem], device_id=dev, device_id_type=MESH
        ).start()

    def got(ref, sem):
        pltpu.make_async_copy(ref, ref, rsem.at[sem]).wait()

    def sent(ref, sem):
        pltpu.make_async_copy(ref, ref, ssem.at[sem]).wait()

    def load(n):
        return pltpu.make_async_copy(inputs[n], held[n], lsem.at[n])

    def each_lead(fn):
        ring, side = lax.rem(lax.div(li, 2), 8), lax.div(li, 16)

        def body(n, carry):
            m = lax.div(n, 4)
            step = lax.div(m + 1, 2) * (1 - 2 * lax.rem(m, 2))
            other = lax.rem(ring + 12 + step, 8)
            rest = 3 - lax.rem(n, 4)
            side_to = lax.rem(side + lax.div(rest, 2), 2)
            core_to = lax.rem(core + lax.rem(rest, 2), 2)
            fn(side_to * 16 + other * 2 + core_to)
            return carry
        lax.fori_loop(0, L - 1, body, 0)

    row, col = lax.div(ti, 4), lax.rem(ti, 4)
    core = lax.rem(li, 2)
    partner = lead_dev(li + 1 - 2 * core)

    def each_z(fn):
        for m in (2, 1, 3):
            fn(lax.rem(col + m, 4))

    def each_x(fn):
        for m in (2, 1, 3):
            fn(lax.rem(row + m, 4))

    def each_tile_far_first(fn):

        def away(m):
            return 6 + lax.div(m + 1, 2) * (1 - 2 * lax.rem(m, 2))

        def body(n, carry):
            fn(lax.rem(row + away(lax.div(n, 4)), 4) * 4 + lax.rem(col + away(lax.rem(n, 4)), 4))
            return carry
        lax.fori_loop(0, T - 1, body, 0)

    def each_tile(fn, first=1, last=T):
        def body(d, carry):
            fn(lax.rem(ti + d, T))
            return carry
        lax.fori_loop(first, last, body, 0)

    bar = pltpu.get_barrier_semaphore()
    each_lead(lambda to: pl.semaphore_signal(bar, inc=1, device_id=lead_dev(to), device_id_type=MESH))
    each_tile_far_first(lambda to: pl.semaphore_signal(bar, inc=1, device_id=tile_dev(to), device_id_type=MESH))
    for n in range(N_IN - 1):
        load(n).start()

    up = lax.rem(ti + 1, T)
    down = lax.rem(ti + T - 1, T)
    has_up = ti < T - 1
    has_down = ti > 0

    for n in range(4):
        load(n).wait()
    outer = wsrc[...].astype(F32).reshape(OWN * TAPS * GATES, 2 * HID).astype(BF)
    wt[...] = nn(a_ref[...], outer).astype(BF)
    sub = lax.broadcasted_iota(jnp.int32, (OWN, OWN), 0)
    lane = lax.broadcasted_iota(jnp.int32, (OWN, OWN), 1)
    bias_cols = [jnp.sum(jnp.where(sub == lane, bias[j:j + 1, :], 0.0), axis=1, keepdims=True) for j in range(GATES)]

    def row_parts(g):
        parts = []
        for a in range(3):
            total = None
            for b in range(3):
                k = 3 * a + b
                term = shifted(g[k * GR:(k + 1) * GR], b - 1)
                total = term if total is None else total + term
            parts.append(total)
        return parts

    own_x = []

    def frame_parts(t):
        parts = row_parts(nn(wt[:, 0:HID], frames[t]))
        for a in (0, 2):
            yx[t, a] = parts[a]
        own_x.append(parts[1])

    frame_parts(0)
    pl.semaphore_wait(bar, L + T - 2)

    def halo(src, dst, sem):
        send(src.at[0], dst.at[0], sem, tile_dev(up))
        send(src.at[2], dst.at[1], sem, tile_dev(down))

    halo(yx.at[0], rx.at[0], S_YX0)
    for n in range(4, N_IN - 1):
        load(n).wait()
    whp[...] = nn(wt[:, HID:], e_ref[...]).astype(BF)
    whpt[...] = nt(et_ref[...], wt[:, HID:]).astype(BF)
    def from_neighbours(r):
        return jnp.where(has_down, r[0], 0.0) + jnp.where(has_up, r[1], 0.0)

    def padded(x):
        return jnp.concatenate([x, jnp.zeros((PAD - OWN, W), F32)], 0)

    def cell(z, previous):
        z = [padded(z[j * OWN:(j + 1) * OWN] + bias_cols[j]) for j in range(GATES)]
        i_g = jax.nn.sigmoid(z[0])
        f_g = jax.nn.sigmoid(z[1])
        g_g = jnp.tanh(z[2])
        o_g = jax.nn.sigmoid(z[3])
        now = f_g * previous + i_g * g_g
        return (i_g, f_g, g_g, o_g, previous, now), (o_g * jnp.tanh(now)).astype(BF)

    def share_h(t, h):
        buf = hbuf.at[t]
        buf[li] = h
        sem = (S_H1, S_H2, S_H3)[t]
        each_lead(lambda to: send(buf.at[li], buf.at[li], sem, lead_dev(to)))

    def await_h(t):
        got(hbuf.at[t, pl.ds(0, L - 1)], (S_H1, S_H2, S_H3)[t])

    saved = []
    got(rx.at[0], S_YX0)
    z = own_x[0] + from_neighbours(rx.at[0])
    state, h = cell(z, jnp.zeros((PAD, W), F32))
    saved.append(state)
    share_h(0, h)
    for t in (1, 2):
        frame_parts(t)
        halo(yx.at[t], rx.at[t], (S_YX0, S_YX1, S_YX2)[t])
    send(cot, coth.at[0], S_COTH, tile_dev(lax.rem(ti + 2, T)))
    for t in range(3):
        fsend[:, 2 * t:2 * t + 2] = nn(et_ref[...], frames[t]).astype(BF).reshape(T, 2, PAD, W)
    for p in range(4):
        cot4[p] = cot[96 * p:96 * (p + 1), :]
    slot = lax.broadcasted_iota(jnp.int32, (16, 2, HID), 0)
    lines = jnp.sum(jnp.where(slot == idx[0], film[...], 0.0), axis=0)
    lines = jnp.concatenate([lines, jnp.zeros((6, HID), F32)], 0).T
    film_col[...] = jnp.zeros_like(film_col)
    for i in range(L):
        film_col[i, 0:OWN, :] = lines[i * OWN:(i + 1) * OWN]
    film_q[...] = lines.reshape(4, 96, 8)
    for at in (0, (T + 1) * W):
        stack[:, at:at + W] = jnp.zeros((3 * GR, W), BF)
    for at in (0, (T + 2) * W):
        cc[:, at:at + 2 * W] = jnp.zeros((3 * 96, 2 * W), BF)
    vv[96:W, :] = jnp.zeros((W - 96, T * W), BF)
    for d in range(4):
        pbuf[256 * d + 216:256 * (d + 1), :] = jnp.zeros((40, W), F32)
    scat[...] = jnp.zeros_like(scat)

    def half(x):
        return x.at[pl.ds(3 * core, 3)]

    def send_frames(to):
        send(half(fsend.at[to]), half(fblk.at[ti]), S_FR, tile_dev(to))

    for t in (1, 2):
        await_h(t - 1)
        parts = row_parts(nn(whp[...], hbuf[t - 1].reshape(CP, W)))
        for a in (0, 2):
            yh[t - 1, a] = parts[a]
        sem = (S_YH1, S_YH2)[t - 1]
        halo(yh.at[t - 1], rh.at[t - 1], sem)
        got(rx.at[t], (S_YX0, S_YX1, S_YX2)[t])
        base = own_x[t] + from_neighbours(rx.at[t]) + parts[1]
        got(rh.at[t - 1], sem)
        z = base + from_neighbours(rh.at[t - 1])
        state, h = cell(z, saved[-1][5])
        saved.append(state)
        share_h(t, h)
        if t == 1:
            send(cot, coth.at[1], S_COTH, tile_dev(lax.rem(ti + T - 2, T)))
    each_tile_far_first(send_frames)
    fblk[ti, pl.ds(3 * core, 3)] = fsend[ti, pl.ds(3 * core, 3)]
    each_z(lambda to: send(cot4.at[to], cotz.at[col], S_COTZ, tile_dev(row * 4 + to)))
    cotz[col] = cot4[col]
    got(coth, S_COTH)
    zero = jnp.zeros((HID, W), BF)
    rows = (jnp.where(ti < T - 2, coth[1], zero), cot[...], jnp.where(ti >= 2, coth[0], zero))
    dvt = jnp.zeros((W, HID), F32)
    for a in range(3):
        ct = rows[a].astype(F32).T
        for b in range(3):
            k = 3 * a + b
            dvt = dvt + nn(shifted_rows(ct, -2 * (b - 1)).astype(BF), hw[k * HID:(k + 1) * HID, :])
    dv = dvt.T
    dv_ref[...] = jnp.zeros_like(dv_ref)
    for i in range(L):
        dv_ref[0, i, 0:OWN, :] = dv[i * OWN:(i + 1) * OWN]
    dv_ref[1] = nn(et_ref[...], cot[...]).reshape(L, PAD, W)

    def share_blocks(t):
        hsem = (S_HB1, S_HB2)[t]
        hb = hblk.at[t]
        hs = hbuf.at[t]
        hb[ti, core] = hs[2 * ti + core]
        each_tile_far_first(lambda to: send(hs.at[2 * to + core], hb.at[ti, core], hsem, tile_dev(to)))

    def swap_blocks(t):
        got(hblk.at[t, pl.ds(0, T - 1), 0], (S_HB1, S_HB2)[t])
        mine = hblk.at[t, :, core]
        send(mine, mine, (S_HB1C, S_HB2C)[t], partner)

    def await_blocks(t):
        got(hblk.at[t, :, 0], (S_HB1C, S_HB2C)[t])

    await_h(2)
    h_wide = hbuf[2].reshape(CP, W).astype(F32)
    columns = film_col[...].reshape(CP, 8)
    gamma = 1.0 + columns[:, 0:1]
    u = gamma * h_wide + columns[:, 1:2]
    s = jax.nn.sigmoid(u)
    du = dv_ref[0].reshape(CP, W) * s * (1.0 + u * (1.0 - s))
    dhp[0] = (dv_ref[1].reshape(CP, W) + gamma * du).astype(BF).reshape(L, PAD, W)

    def share_dh(n):
        sem = (S_DH3, S_DH2, S_DH1)[n]
        src = dhp.at[n]
        dst = dhr.at[n]
        each_lead(lambda to: send(src.at[to], dst.at[li], sem, lead_dev(to)))
        dst[li] = src[li]

    def await_dh(n):
        got(dhr.at[n, pl.ds(0, L - 1)], (S_DH3, S_DH2, S_DH1)[n])
        return jnp.sum(dhr[n].astype(F32), axis=0)

    share_dh(0)
    h8[...] = nn(e_ref[...], hbuf[2].reshape(CP, W)).astype(BF).reshape(8, 48, W)
    each_tile_far_first(lambda to: send(h8.at[2 * lax.div(to, 4) + core], hq.at[ti, core], S_HQ, tile_dev(to)))
    hq[ti, core] = h8[2 * row + core]
    got(cotz.at[pl.ds(0, 3)], S_COTZ)
    each_x(lambda to: send(cotz, cotb.at[pl.ds(4 * row, 4)], S_COTX, tile_dev(to * 4 + col)))
    cotb[pl.ds(4 * row, 4)] = cotz[...]
    st_send[...] = jnp.zeros_like(st_send)
    for n, field in enumerate((du * h_wide, du)):
        for i in range(L):
            flat[i * OWN:(i + 1) * OWN, :] = field[i * PAD:i * PAD + OWN]
        line = jnp.sum(flat[...].T, axis=0, keepdims=True)
        for q in range(3):
            st_send[3 * n + q:3 * n + q + 1, :] = line[:, 128 * q:128 * (q + 1)]
    each_tile_far_first(lambda to: send(st_send, st_tile.at[ti], S_ST, tile_dev(to)))
    st_tile[ti] = st_send[...]
    got(fblk.at[pl.ds(0, T - 1), pl.ds(0, 3)], S_FR)
    fr_mine = fblk.at[:, pl.ds(3 * core, 3)]
    send(fr_mine, fr_mine, S_FRC, partner)

    bias_sum = jnp.zeros((GR, W), F32)
    dc = jnp.zeros((PAD, W), F32)

    def gate_grads(n, dh, dc):
        i_g, f_g, g_g, o_g, previous, now = saved[2 - n]
        sq = jnp.tanh(now)
        dc = dc + dh * o_g * (1.0 - sq * sq)
        dz = jnp.concatenate(
            [x[0:OWN] for x in (
                dc * g_g * i_g * (1.0 - i_g),
                dc * previous * f_g * (1.0 - f_g),
                dc * i_g * (1.0 - g_g * g_g),
                dh * sq * o_g * (1.0 - o_g),
            )],
            0,
        )
        src = dz_send.at[n]
        dst = dzbuf.at[n]
        src[...] = dz.astype(BF)
        dst[ti] = src[...]
        if n < 2:
            send(src, dznear.at[n, 0], (S_DZN2, S_DZN1)[n], tile_dev(up))
            send(src, dznear.at[n, 1], (S_DZN2, S_DZN1)[n], tile_dev(down))
        else:
            each_tile_far_first(lambda to: send(src, dst.at[ti], S_DZ0, tile_dev(to)))
        return dz, dc * f_g

    def await_near(n):
        got(dznear.at[n], (S_DZN2, S_DZN1)[n])

    def share_z(n):
        each_z(lambda to: send(dz_send.at[n], dzbuf.at[n, ti], (S_DZZ2, S_DZZ1)[n], tile_dev(row * 4 + to)))

    def share_x(n):
        got(dzbuf.at[n, pl.ds(0, 3)], (S_DZZ2, S_DZZ1)[n])
        mine = dzbuf.at[n, pl.ds(4 * row, 4)]
        each_x(lambda to: send(mine, mine, (S_DZX2, S_DZX1)[n], tile_dev(to * 4 + col)))

    def await_x(n):
        got(dzbuf.at[n, pl.ds(0, 12)], (S_DZX2, S_DZX1)[n])

    def back(n):
        zero = jnp.zeros((GR, W), F32)
        rows = (
            jnp.where(has_up, dznear[n, 1].astype(F32), zero),
            dz_send[n].astype(F32),
            jnp.where(has_down, dznear[n, 0].astype(F32), zero),
        )
        pieces = [shifted(rows[a], 1 - b).astype(BF) for a in range(3) for b in range(3)]
        dhp[n + 1] = nn(whpt[...], jnp.concatenate(pieces, 0)).astype(BF).reshape(L, PAD, W)

    def weight_part(n):
        t = 2 - n
        src = dzbuf.at[n]

        def body(r, carry):
            block = src[r].astype(F32)
            for b in range(3):
                stack[b * GR:(b + 1) * GR, pl.ds(pl.multiple_of((r + 1) * W, W), W)] = shifted(block, 1 - b).astype(BF)
            at = pl.multiple_of(r * W, W)
            scat[0:2 * PAD, pl.ds(at, W)] = fblk[r, 2 * t:2 * t + 2].reshape(2 * PAD, W)
            if t > 0:
                scat[2 * PAD:4 * PAD, pl.ds(at, W)] = hblk[t - 1, r].reshape(2 * PAD, W)
            return carry

        lax.fori_loop(0, T, body, 0, unroll=8)
        return jnp.concatenate([nt(stack[:, (2 - a) * W:(2 - a + T) * W], scat[...]) for a in range(3)], 0).T

    def share_weights(n, x):
        y = nn((x * (1.0 / 256.0)).astype(BF), pack[...]).astype(BF)
        wsend[n] = (nn(rsel[0], y[:, :256]) + nn(rsel[1], y[:, 256:])).astype(BF)
        src = wsend.at[n]
        dst = wrecv.at[n]
        dst[ti] = src[...]
        if n == 0:
            each_z(lambda to: send(src, dst.at[ti], S_WHZ, tile_dev(row * 4 + to)))
        else:
            send(src, dst.at[ti], S_WFA, tile_dev(row * 4 + lax.rem(col + 2, 4)))
            for mx in (2, 1, 3, 0):
                for mz in (1, 3, 0) if mx else (1, 3):
                    to = lax.rem(row + mx, 4) * 4 + lax.rem(col + mz, 4)
                    send(src, dst.at[ti], S_WF, tile_dev(to))

    def forward_weights():
        opposite = row * 4 + lax.rem(col + 2, 4)
        got(wrecv.at[1, 0], S_WFA)
        mine = wrecv.at[1, opposite]
        each_x(lambda to: send(mine, mine, S_WFB, tile_dev(to * 4 + col)))

    def share_weights_x():
        got(wrecv.at[0, pl.ds(0, 3)], S_WHZ)
        mine = wrecv.at[0, pl.ds(4 * row, 4)]
        each_x(lambda to: send(mine, mine, S_WHX, tile_dev(to * 4 + col)))

    def finish_weights(n):
        if n == 0:
            got(wrecv.at[0, pl.ds(0, 12)], S_WHX)
        else:
            got(wrecv.at[1, pl.ds(0, 11)], S_WF)
            got(wrecv.at[1, pl.ds(0, 3)], S_WFB)
        for s_ in range(T):
            block = wrecv[n, s_].astype(F32)
            xf[24 * s_:24 * (s_ + 1), 0:256] = block[0:24]
            xf[24 * s_:24 * (s_ + 1), 256:512] = block[24:48]
        out = nt(unpack[...], xf[...].astype(BF)).astype(BF)
        col = HID * (1 - n)
        wg_out[:, col:col + HID] = out

    dz, dc = gate_grads(0, await_dh(0), dc)
    bias_sum = bias_sum + dz
    await_near(0)
    back(0)
    share_dh(1)
    share_z(0)
    got(hq.at[pl.ds(0, T - 1), 0], S_HQ)
    hq_mine = hq.at[:, core]
    send(hq_mine, hq_mine, S_HQC, partner)
    share_blocks(1)
    share_blocks(0)
    share_x(0)

    got(st_tile.at[pl.ds(0, T - 1)], S_ST)
    stl_send[0:8, :] = jnp.sum(st_tile[...], axis=0)
    lane = lax.broadcasted_iota(jnp.int32, (8, W), 1)
    stl_send[8:16, :] = jnp.where(lane == idx[0], 1.0, 0.0)
    each_lead(lambda to: send(stl_send, stl.at[li], S_STL, lead_dev(to)))
    stl[li] = stl_send[...]

    got(hq.at[:, 0], S_HQC)
    got(cotb.at[pl.ds(0, 12)], S_COTX)
    gamma_q = 1.0 + film_q[row, :, 0:1]
    beta_q = film_q[row, :, 1:2]

    def head_rows(r, carry):
        block = cotb[r].astype(F32)
        at = pl.multiple_of((r + 2) * W, W)
        for b in range(3):
            cc[96 * b:96 * (b + 1), pl.ds(at, W)] = shifted(block, 2 * (1 - b)).astype(BF)
        uq = gamma_q * hq[r].reshape(96, W).astype(F32) + beta_q
        vv[0:96, pl.ds(pl.multiple_of(r * W, W), W)] = (uq * jax.nn.sigmoid(uq)).astype(BF)
        return carry

    lax.fori_loop(0, T, head_rows, 0)
    for a in range(3):
        first = (4 - 2 * a) * W
        part = nt(cc[:, first:first + T * W], vv[...])
        for b in range(3):
            k = 3 * a + b
            for d in range(4):
                pbuf[d * 256 + k * 24:d * 256 + (k + 1) * 24, :] = part[b * 96 + d * 24:b * 96 + (d + 1) * 24]
    psend[...] = pbuf[...].astype(BF).reshape(L, 32, W)
    prec[li] = psend[8 * lax.rem(li, 4) + lax.div(li, 4)]

    dz, dc = gate_grads(1, await_dh(1), dc)
    bias_sum = bias_sum + dz
    await_near(1)
    back(1)
    share_dh(2)
    share_z(1)
    each_lead(lambda to: send(psend.at[8 * lax.rem(to, 4) + lax.div(to, 4)], prec.at[li], S_PR, lead_dev(to)))
    swap_blocks(1)
    swap_blocks(0)
    share_x(1)
    await_x(0)
    got(fblk.at[:, pl.ds(0, 3)], S_FRC)
    await_blocks(1)
    grads = weight_part(0)

    dz, dc = gate_grads(2, await_dh(2), dc)

    got(prec.at[pl.ds(0, L - 1)], S_PR)
    psum[...] = (jnp.sum(prec[...].astype(F32), axis=0) * (1.0 / 256.0)).astype(BF)
    owner = col * 4 + lax.rem(li, 4)
    gathers = lax.rem(li, 4) == col

    @pl.when(owner != ti)
    def _():
        send(psum, ptile.at[row], S_PT, tile_dev(owner))

    @pl.when(owner == ti)
    def _():
        ptile[row] = psum[...]

    await_x(1)
    await_blocks(0)
    grads = grads + weight_part(1)
    share_weights(0, grads[2 * PAD:4 * PAD])
    bias_sum = bias_sum + dz
    column = jnp.sum(bias_sum, axis=1, keepdims=True)
    lane = lax.broadcasted_iota(jnp.int32, (GR, W), 1)
    sub = lax.broadcasted_iota(jnp.int32, (GR, W), 0)
    line = jnp.sum(jnp.where(lane == sub, column, 0.0), axis=0, keepdims=True)
    bi_send[...] = jnp.broadcast_to(line, (8, W))
    each_tile_far_first(lambda to: send(bi_send, bi.at[ti], S_BI, tile_dev(to)))
    bi[ti] = bi_send[...]

    @pl.when(gathers)
    def _():
        @pl.when(owner == ti)
        def _():
            got(ptile.at[pl.ds(0, 3)], S_PT)

        @pl.when(owner != ti)
        def _():
            got(ptile, S_PT)

        each_lead(lambda to: send(ptile, plead.at[lax.div(li, 4)], S_PL, lead_dev(to)))
        plead[lax.div(li, 4)] = ptile[...]

    got(dzbuf.at[2, pl.ds(0, T - 1)], S_DZ0)
    share_weights_x()
    grads0 = weight_part(2)
    share_weights(1, grads[0:2 * PAD] + grads0[0:2 * PAD])
    forward_weights()

    got(stl.at[pl.ds(0, L - 1)], S_STL)

    def table(l, acc):
        block = stl[l]
        return tuple(acc[m] + block[8:16, m:m + 1] * block[0:8, :] for m in range(16))

    acc = lax.fori_loop(0, L, table, tuple(jnp.zeros((8, W), F32) for _ in range(16)))
    for m in range(16):
        fg_out[m] = acc[m] * (1.0 / 256.0)
    got(bi.at[pl.ds(0, T - 1)], S_BI)
    bg_out[...] = jnp.sum(bi[...], axis=0) * (1.0 / 256.0)
    finish_weights(0)

    @pl.when(gathers)
    def _():
        got(plead.at[pl.ds(0, 7)], S_PL)

    @pl.when(jnp.logical_not(gathers))
    def _():
        got(plead, S_PL)

    wide = jnp.concatenate([plead[:, q].reshape(256, W) for q in range(4)], 1)
    hg_out[...] = nn(wide, spread[...])[0:TAPS * 24].astype(BF)
    finish_weights(1)

    for t in range(3):
        sent(rx.at[t], (S_YX0, S_YX1, S_YX2)[t])
        sent(hbuf.at[t, pl.ds(0, L - 1)], (S_H1, S_H2, S_H3)[t])
        sent(dhr.at[t, pl.ds(0, L - 1)], (S_DH3, S_DH2, S_DH1)[t])
    for t in range(2):
        sent(rh.at[t], (S_YH1, S_YH2)[t])
        sent(dznear.at[t], (S_DZN2, S_DZN1)[t])
        sent(dzbuf.at[t, pl.ds(0, 3)], (S_DZZ2, S_DZZ1)[t])
        sent(dzbuf.at[t, pl.ds(0, 12)], (S_DZX2, S_DZX1)[t])
        sent(hblk.at[t, pl.ds(0, T - 1), 0], (S_HB1, S_HB2)[t])
        sent(hblk.at[t, :, 0], (S_HB1C, S_HB2C)[t])
    sent(dzbuf.at[2, pl.ds(0, T - 1)], S_DZ0)
    sent(wrecv.at[0, pl.ds(0, 3)], S_WHZ)
    sent(wrecv.at[0, pl.ds(0, 12)], S_WHX)
    sent(wrecv.at[1, pl.ds(0, 11)], S_WF)
    sent(wrecv.at[1, 0], S_WFA)
    sent(wrecv.at[1, pl.ds(0, 3)], S_WFB)
    sent(coth, S_COTH)
    sent(cotz.at[pl.ds(0, 3)], S_COTZ)
    sent(cotb.at[pl.ds(0, 12)], S_COTX)
    sent(fblk.at[pl.ds(0, T - 1), pl.ds(0, 3)], S_FR)
    sent(fblk.at[:, pl.ds(0, 3)], S_FRC)
    sent(hq.at[pl.ds(0, T - 1), 0], S_HQ)
    sent(hq.at[:, 0], S_HQC)
    sent(st_tile.at[pl.ds(0, T - 1)], S_ST)
    sent(stl.at[pl.ds(0, L - 1)], S_STL)
    sent(bi.at[pl.ds(0, T - 1)], S_BI)
    sent(prec.at[pl.ds(0, L - 1)], S_PR)

    @pl.when(owner != ti)
    def _():
        sent(psum, S_PT)

    @pl.when(gathers)
    def _():
        def body(d, carry):
            sent(ptile, S_PL)
            return carry
        lax.fori_loop(1, L, body, 0)


def finish(wg, bg, hg, fg, wg_out, bg_out, hg_out, fg_out):
    wg_out[...] = wg[...].astype(F32).reshape(OWN, TAPS, GATES, 2 * HID).astype(BF)
    hg_out[...] = hg[...]
    for j in range(GATES):
        bg_out[j:j + 1, :] = bg[0:1, j * OWN:(j + 1) * OWN]
    for m in range(16):
        for n in range(2):
            for q in range(3):
                fg_out[m, n:n + 1, W * q:W * (q + 1)] = fg[m, 3 * n + q:3 * n + q + 1, :]


def shards(frames, enc_weight, enc_bias, head_weight, film_table, lead_index, cotangent):
    a, pack, unpack, e, et, spread, rsel = [jnp.asarray(x) for x in one_hots()]
    wsrc = enc_weight.transpose(0, 2, 1, 3)
    hw = head_weight.transpose(1, 0, 2).reshape(TAPS * HID, HID)
    vm = pltpu.VMEM
    inputs = (
        wsrc, a, frames.reshape(3, HID, W), enc_bias.T, e, et, film_table, cotangent.reshape(HID, W), hw, pack, rsel,
        unpack, spread,
    )
    outs = pl.pallas_call(
        kernel,
        out_shape=(
            jax.ShapeDtypeStruct((OWN * TAPS * GATES, 2 * HID), BF),
            jax.ShapeDtypeStruct((8, W), F32),
            jax.ShapeDtypeStruct((TAPS * 24, HID), BF),
            jax.ShapeDtypeStruct((16, 8, W), F32),
        ),
        in_specs=[pl.BlockSpec(memory_space=pl.ANY)] * (N_IN - 1) + [pl.BlockSpec(memory_space=pltpu.SMEM)],
        out_specs=(pl.BlockSpec(memory_space=vm),) * 4,
        scratch_shapes=[vm(x.shape, x.dtype) for x in inputs] + [
            vm((TAPS * GR, 2 * HID), BF),
            vm((TAPS * GR, CP), BF),
            vm((CP, TAPS * GR), BF),
            vm((3, 3, GR, W), F32),
            vm((2, 3, GR, W), F32),
            vm((3, 2, GR, W), F32),
            vm((2, 2, GR, W), F32),
            vm((3, L, PAD, W), BF),
            vm((2, HID, W), BF),
            vm((4, 96, W), BF),
            vm((4, 96, W), BF),
            vm((T, 96, W), BF),
            vm((T, 6, PAD, W), BF),
            vm((T, 6, PAD, W), BF),
            vm((2, T, 2, PAD, W), BF),
            vm((2, L, PAD, W), F32),
            vm((3, L, PAD, W), BF),
            vm((3, L, PAD, W), BF),
            vm((8, 48, W), BF),
            vm((T, 2, 48, W), BF),
            vm((8, W), F32),
            vm((T, 8, W), F32),
            vm((16, W), F32),
            vm((L, 16, W), F32),
            vm((3, GR, W), BF),
            vm((2, 2, GR, W), BF),
            vm((3, T, GR, W), BF),
            vm((8, W), F32),
            vm((T, 8, W), F32),
            vm((3 * GR, (T + 2) * W), BF),
            vm((4 * PAD, T * W), BF),
            vm((2, 48, 256), BF),
            vm((2, T, 48, 256), BF),
            vm((HID, 512), F32),
            vm((3 * 96, (T + 4) * W), BF),
            vm((W, T * W), BF),
            vm((L * 32, W), F32),
            vm((L, 32, W), BF),
            vm((L, 32, W), BF),
            vm((32, W), BF),
            vm((4, 32, W), BF),
            vm((8, 4, 32, W), BF),
            vm((L, PAD, 8), F32),
            vm((4, 96, 8), F32),
            vm((HID, W), F32),
            pltpu.SemaphoreType.DMA((NSEM,)),
            pltpu.SemaphoreType.DMA((NSEM,)),
            pltpu.SemaphoreType.DMA((N_IN - 1,)),
        ],
        compiler_params=pltpu.CompilerParams(
            collective_id=0, has_side_effects=True, vmem_limit_bytes=56 * 2**20
        ),
    )(*inputs, lead_index)
    wg, bg, hg, fg = pl.pallas_call(
        finish,
        out_shape=(
            jax.ShapeDtypeStruct((OWN, TAPS, GATES, 2 * HID), BF),
            jax.ShapeDtypeStruct((GATES, OWN), F32),
            jax.ShapeDtypeStruct((TAPS * 24, HID), BF),
            jax.ShapeDtypeStruct((16, 2, HID), F32),
        ),
        in_specs=[pl.BlockSpec(memory_space=vm)] * 4,
        out_specs=(pl.BlockSpec(memory_space=vm),) * 4,
    )(*outs)
    return wg.transpose(0, 2, 1, 3), bg.T, hg.reshape(TAPS, 24, HID).transpose(1, 0, 2), fg


def solution(mesh):
    in_specs = (
        P(None, None, "tile", None),
        P("lead", None, None, None),
        P("lead", None),
        P(),
        P(),
        P("lead"),
        P("lead", None, "tile", None),
    )
    out_specs = (P("lead", None, None, None), P("lead", None), P("tile", None, None), P())
    return jax.shard_map(shards, mesh=mesh, in_specs=in_specs, out_specs=out_specs, check_vma=False)
```

```python
import numpy as np
import jax
import jax.numpy as jnp
import ml_dtypes
from jax import lax
from jax.experimental import pallas as pl
from jax.experimental.pallas import tpu as pltpu
from jax.sharding import PartitionSpec as P

MESH = pl.DeviceIdType.MESH
BF = jnp.bfloat16
F32 = jnp.float32
L, T, HID, W = 32, 16, 384, 128
OWN, PAD, GATES, TAPS = 12, 16, 4, 9
GR = GATES * OWN
CP = L * PAD


def one_hots():
    a = np.zeros((TAPS * GR, OWN * TAPS * GATES), np.float32)
    pack = np.zeros((TAPS * GR, 512), np.float32)
    unpack = np.zeros((OWN * TAPS * GATES, 512), np.float32)
    for k in range(TAPS):
        for j in range(GATES):
            for o in range(OWN):
                inner = k * GR + j * OWN + o
                outer = (o * TAPS + k) * GATES + j
                column = inner + (0 if k < 5 else 16)
                a[inner, outer] = 1
                pack[inner, column] = 1
                unpack[outer, column] = 1
    e = np.zeros((HID, CP), np.float32)
    for i in range(L):
        for o in range(OWN):
            e[i * OWN + o, i * PAD + o] = 1
    spread = np.zeros((512, HID), np.float32)
    for q in range(4):
        for c in range(96):
            spread[128 * q + c, 96 * q + c] = 1
    rows = np.zeros((2, 48, 32), np.float32)
    for half in range(2):
        for c in range(24):
            rows[half, 24 * half + c, (c // OWN) * PAD + c % OWN] = 1
    return [x.astype(ml_dtypes.bfloat16) for x in (a, pack, unpack, e, e.T.copy(), spread, rows)]


def nn(a, b):
    return lax.dot_general(a, b, (((1,), (0,)), ((), ())), preferred_element_type=F32)


def nt(a, b):
    return lax.dot_general(a, b, (((1,), (1,)), ((), ())), preferred_element_type=F32)


def shifted(x, s):
    if s == 0:
        return x
    lane = lax.broadcasted_iota(jnp.int32, x.shape, 1)
    keep = lane < W - s if s > 0 else lane >= -s
    return jnp.where(keep, pltpu.roll(x, (-s) % W, 1), 0.0)


def shifted_rows(x, s):
    if s == 0:
        return x
    row = lax.broadcasted_iota(jnp.int32, x.shape, 0)
    keep = row < W - s if s > 0 else row >= -s
    return jnp.where(keep, pltpu.roll(x, (-s) % W, 0), 0.0)


(S_YX0, S_YX1, S_YX2, S_H1, S_H2, S_H3, S_YH1, S_YH2, S_COTH, S_COTZ, S_COTX, S_FR, S_FRC, S_HB1, S_HB2, S_HB1C, S_HB2C,
 S_DH3, S_DH2, S_DH1, S_HQ, S_HQC, S_ST, S_STL, S_DZN2, S_DZN1, S_DZ0, S_DZZ2, S_DZZ1, S_DZX2, S_DZX1, S_BI, S_WHZ, S_WHX, S_WF,
 S_WFA, S_WFB, S_PR, S_PT, S_PL, S_COTH2, NSEM) = range(42)


N_IN = 14


def kernel(*refs):
    inputs, (wg_out, bg_out, hg_out, fg_out), refs = refs[:N_IN], refs[N_IN:N_IN + 4], refs[N_IN + 4:]
    held, refs = refs[:N_IN - 1], refs[N_IN - 1:]
    idx = inputs[N_IN - 1]
    (
        wt, whp, whpt, whpt2, dvt_ref, yx, yh, rx, rh, hbuf, coth, cot4, cotz, cotb, fsend, fblk, hblk, dv_ref, dhp, dhr,
        h8, hq, st_send, st_tile, stl_send, stl, dz_send, dznear, dzbuf, bi_send, bi, stack, scat,
        wsend, wrecv, xf, cc, vv, pbuf, psend, prec, psum, ptile, plead, film_col, film_q, flat, ssem, rsem, lsem,
    ) = refs
    wsrc, a_ref, frames, bias, e_ref, et_ref, film, cot, hw, pack, rsel, unpack, spread = held
    li = lax.axis_index("lead")
    ti = lax.axis_index("tile")

    def lead_dev(to):
        return (to, ti)

    def tile_dev(to):
        return (li, to)

    def send(src, dst, sem, dev):
        pltpu.make_async_remote_copy(
            src_ref=src, dst_ref=dst, send_sem=ssem.at[sem], recv_sem=rsem.at[sem], device_id=dev, device_id_type=MESH
        ).start()

    def got(ref, sem):
        pltpu.make_async_copy(ref, ref, rsem.at[sem]).wait()

    def sent(ref, sem):
        pltpu.make_async_copy(ref, ref, ssem.at[sem]).wait()

    def load(n):
        return pltpu.make_async_copy(inputs[n], held[n], lsem.at[n])

    def each_lead(fn):
        ring, side = lax.rem(lax.div(li, 2), 8), lax.div(li, 16)

        def body(n, carry):
            m = lax.div(n, 4)
            step = lax.div(m + 1, 2) * (1 - 2 * lax.rem(m, 2))
            other = lax.rem(ring + 12 + step, 8)
            rest = 3 - lax.rem(n, 4)
            side_to = lax.rem(side + lax.div(rest, 2), 2)
            core_to = lax.rem(core + lax.rem(rest, 2), 2)
            fn(side_to * 16 + other * 2 + core_to)
            return carry
        lax.fori_loop(0, L - 1, body, 0)

    row, col = lax.div(ti, 4), lax.rem(ti, 4)
    core = lax.rem(li, 2)
    partner = lead_dev(li + 1 - 2 * core)

    def each_z(fn):
        for m in (2, 1, 3):
            fn(lax.rem(col + m, 4))

    def each_x(fn):
        for m in (2, 1, 3):
            fn(lax.rem(row + m, 4))

    def each_tile_far_first(fn):

        def away(m):
            return 6 + lax.div(m + 1, 2) * (1 - 2 * lax.rem(m, 2))

        def body(n, carry):
            fn(lax.rem(row + away(lax.div(n, 4)), 4) * 4 + lax.rem(col + away(lax.rem(n, 4)), 4))
            return carry
        lax.fori_loop(0, T - 1, body, 0)

    def each_tile(fn, first=1, last=T):
        def body(d, carry):
            fn(lax.rem(ti + d, T))
            return carry
        lax.fori_loop(first, last, body, 0)

    bar = pltpu.get_barrier_semaphore()
    each_lead(lambda to: pl.semaphore_signal(bar, inc=1, device_id=lead_dev(to), device_id_type=MESH))
    each_tile_far_first(lambda to: pl.semaphore_signal(bar, inc=1, device_id=tile_dev(to), device_id_type=MESH))
    for n in range(N_IN - 1):
        load(n).start()

    up = lax.rem(ti + 1, T)
    down = lax.rem(ti + T - 1, T)
    has_up = ti < T - 1
    has_down = ti > 0

    for n in range(4):
        load(n).wait()
    outer = wsrc[...].astype(F32).reshape(OWN * TAPS * GATES, 2 * HID).astype(BF)
    wt[...] = nn(a_ref[...], outer).astype(BF)
    sub = lax.broadcasted_iota(jnp.int32, (OWN, OWN), 0)
    lane = lax.broadcasted_iota(jnp.int32, (OWN, OWN), 1)
    bias_cols = [jnp.sum(jnp.where(sub == lane, bias[j:j + 1, :], 0.0), axis=1, keepdims=True) for j in range(GATES)]

    def row_part(g):
        return sum(shifted(g[b * GR:(b + 1) * GR], b - 1) for b in range(3))

    def tap_rows(a):
        return slice(3 * a * GR, 3 * (a + 1) * GR)

    own_x = []

    def frame_parts(t):
        for a in (0, 2):
            yx[t, a] = row_part(nn(wt[tap_rows(a), 0:HID], frames[t]))
        own_x.append(None if t == 0 else row_part(nn(wt[tap_rows(1), 0:HID], frames[t])))

    frame_parts(0)
    pl.semaphore_wait(bar, L + T - 2)

    def halo(src, dst, sem):
        send(src.at[0], dst.at[0], sem, tile_dev(up))
        send(src.at[2], dst.at[1], sem, tile_dev(down))

    halo(yx.at[0], rx.at[0], S_YX0)
    own_x[0] = row_part(nn(wt[tap_rows(1), 0:HID], frames[0]))
    for n in range(4, N_IN - 1):
        load(n).wait()
    whp[...] = nn(wt[:, HID:], e_ref[...]).astype(BF)
    whpt[...] = nt(et_ref[...], wt[tap_rows(1), HID:]).astype(BF)
    whpt2[...] = nt(et_ref[...], jnp.concatenate([wt[tap_rows(0), HID:], wt[tap_rows(2), HID:]], 0)).astype(BF)
    def from_neighbours(r):
        return jnp.where(has_down, r[0], 0.0) + jnp.where(has_up, r[1], 0.0)

    def padded(x):
        return jnp.concatenate([x, jnp.zeros((PAD - OWN, W), F32)], 0)

    def cell(z, previous):
        z = [padded(z[j * OWN:(j + 1) * OWN] + bias_cols[j]) for j in range(GATES)]
        i_g = jax.nn.sigmoid(z[0])
        f_g = jax.nn.sigmoid(z[1])
        g_g = jnp.tanh(z[2])
        o_g = jax.nn.sigmoid(z[3])
        now = f_g * previous + i_g * g_g
        return (i_g, f_g, g_g, o_g, previous, now), (o_g * jnp.tanh(now)).astype(BF)

    def share_h(t, h):
        buf = hbuf.at[t]
        buf[li] = h
        sem = (S_H1, S_H2, S_H3)[t]
        each_lead(lambda to: send(buf.at[li], buf.at[li], sem, lead_dev(to)))

    def await_h(t):
        got(hbuf.at[t, pl.ds(0, L - 1)], (S_H1, S_H2, S_H3)[t])

    saved = []
    got(rx.at[0], S_YX0)
    z = own_x[0] + from_neighbours(rx.at[0])
    state, h = cell(z, jnp.zeros((PAD, W), F32))
    saved.append(state)
    share_h(0, h)
    for t in (1, 2):
        frame_parts(t)
        halo(yx.at[t], rx.at[t], (S_YX0, S_YX1, S_YX2)[t])
    send(cot, coth.at[0], S_COTH, tile_dev(lax.rem(ti + 2, T)))
    for t in range(3):
        fsend[:, 2 * t:2 * t + 2] = nn(et_ref[...], frames[t]).astype(BF).reshape(T, 2, PAD, W)
    for p in range(4):
        cot4[p] = cot[96 * p:96 * (p + 1), :]
    slot = lax.broadcasted_iota(jnp.int32, (16, 2, HID), 0)
    lines = jnp.sum(jnp.where(slot == idx[0], film[...], 0.0), axis=0)
    lines = jnp.concatenate([lines, jnp.zeros((6, HID), F32)], 0).T
    film_col[...] = jnp.zeros_like(film_col)
    for i in range(L):
        film_col[i, 0:OWN, :] = lines[i * OWN:(i + 1) * OWN]
    film_q[...] = lines.reshape(4, 96, 8)
    for at in (0, (T + 1) * W):
        stack[:, at:at + W] = jnp.zeros((3 * GR, W), BF)
    for at in (0, (T + 2) * W):
        cc[:, at:at + 2 * W] = jnp.zeros((3 * 96, 2 * W), BF)
    vv[96:W, :] = jnp.zeros((W - 96, T * W), BF)
    for d in range(4):
        pbuf[256 * d + 216:256 * (d + 1), :] = jnp.zeros((40, W), F32)
    scat[...] = jnp.zeros_like(scat)

    def half(x):
        return x.at[pl.ds(3 * core, 3)]

    def send_frames(to):
        send(half(fsend.at[to]), half(fblk.at[ti]), S_FR, tile_dev(to))

    zero_row = jnp.zeros((HID, W), BF)

    def head_product(a, x):
        ct = x.astype(F32).T
        total = None
        for b in range(3):
            k = 3 * a + b
            term = nn(shifted_rows(ct, -2 * (b - 1)).astype(BF), hw[k * HID:(k + 1) * HID, :])
            total = term if total is None else total + term
        return total

    for t in (1, 2):
        await_h(t - 1)
        h = hbuf[t - 1].reshape(CP, W)
        for a in (0, 2):
            yh[t - 1, a] = row_part(nn(whp[tap_rows(a), :], h))
        sem = (S_YH1, S_YH2)[t - 1]
        halo(yh.at[t - 1], rh.at[t - 1], sem)
        got(rx.at[t], (S_YX0, S_YX1, S_YX2)[t])
        base = own_x[t] + from_neighbours(rx.at[t]) + row_part(nn(whp[tap_rows(1), :], h))
        got(rh.at[t - 1], sem)
        z = base + from_neighbours(rh.at[t - 1])
        state, h = cell(z, saved[-1][5])
        saved.append(state)
        share_h(t, h)
        if t == 1:
            send(cot, coth.at[1], S_COTH2, tile_dev(lax.rem(ti + T - 2, T)))
            dvt = head_product(1, cot[...])
            got(coth.at[0], S_COTH)
            dvt_ref[...] = dvt + head_product(2, jnp.where(ti >= 2, coth[0], zero_row))
    each_tile_far_first(send_frames)
    fblk[ti, pl.ds(3 * core, 3)] = fsend[ti, pl.ds(3 * core, 3)]
    each_z(lambda to: send(cot4.at[to], cotz.at[col], S_COTZ, tile_dev(row * 4 + to)))
    cotz[col] = cot4[col]
    got(coth.at[1], S_COTH2)
    dv = (dvt_ref[...] + head_product(0, jnp.where(ti < T - 2, coth[1], zero_row))).T
    dv_ref[...] = jnp.zeros_like(dv_ref)
    for i in range(L):
        dv_ref[0, i, 0:OWN, :] = dv[i * OWN:(i + 1) * OWN]
    dv_ref[1] = nn(et_ref[...], cot[...]).reshape(L, PAD, W)
    factors = []
    for i_g, f_g, g_g, o_g, previous, now in saved:
        sq = jnp.tanh(now)
        factors.append((
            o_g * (1.0 - sq * sq), g_g * i_g * (1.0 - i_g), previous * f_g * (1.0 - f_g), i_g * (1.0 - g_g * g_g),
            sq * o_g * (1.0 - o_g), f_g,
        ))

    def share_blocks(t):
        hsem = (S_HB1, S_HB2)[t]
        hb = hblk.at[t]
        hs = hbuf.at[t]
        hb[ti, core] = hs[2 * ti + core]
        each_tile_far_first(lambda to: send(hs.at[2 * to + core], hb.at[ti, core], hsem, tile_dev(to)))

    def swap_blocks(t):
        got(hblk.at[t, pl.ds(0, T - 1), 0], (S_HB1, S_HB2)[t])
        mine = hblk.at[t, :, core]
        send(mine, mine, (S_HB1C, S_HB2C)[t], partner)

    def await_blocks(t):
        got(hblk.at[t, :, 0], (S_HB1C, S_HB2C)[t])

    await_h(2)
    h_wide = hbuf[2].reshape(CP, W).astype(F32)
    columns = film_col[...].reshape(CP, 8)
    gamma = 1.0 + columns[:, 0:1]
    u = gamma * h_wide + columns[:, 1:2]
    s = jax.nn.sigmoid(u)
    du = dv_ref[0].reshape(CP, W) * s * (1.0 + u * (1.0 - s))
    dhp[0] = (dv_ref[1].reshape(CP, W) + gamma * du).astype(BF).reshape(L, PAD, W)

    def share_dh(n):
        sem = (S_DH3, S_DH2, S_DH1)[n]
        src = dhp.at[n]
        dst = dhr.at[n]
        each_lead(lambda to: send(src.at[to], dst.at[li], sem, lead_dev(to)))
        dst[li] = src[li]

    def await_dh(n):
        got(dhr.at[n, pl.ds(0, L - 1)], (S_DH3, S_DH2, S_DH1)[n])
        return jnp.sum(dhr[n].astype(F32), axis=0)

    share_dh(0)
    h8[...] = nn(e_ref[...], hbuf[2].reshape(CP, W)).astype(BF).reshape(8, 48, W)
    each_tile_far_first(lambda to: send(h8.at[2 * lax.div(to, 4) + core], hq.at[ti, core], S_HQ, tile_dev(to)))
    hq[ti, core] = h8[2 * row + core]
    got(cotz.at[pl.ds(0, 3)], S_COTZ)
    each_x(lambda to: send(cotz, cotb.at[pl.ds(4 * row, 4)], S_COTX, tile_dev(to * 4 + col)))
    cotb[pl.ds(4 * row, 4)] = cotz[...]
    st_send[...] = jnp.zeros_like(st_send)
    for n, field in enumerate((du * h_wide, du)):
        for i in range(L):
            flat[i * OWN:(i + 1) * OWN, :] = field[i * PAD:i * PAD + OWN]
        line = jnp.sum(flat[...].T, axis=0, keepdims=True)
        for q in range(3):
            st_send[3 * n + q:3 * n + q + 1, :] = line[:, 128 * q:128 * (q + 1)]
    each_tile_far_first(lambda to: send(st_send, st_tile.at[ti], S_ST, tile_dev(to)))
    st_tile[ti] = st_send[...]
    got(fblk.at[pl.ds(0, T - 1), pl.ds(0, 3)], S_FR)
    fr_mine = fblk.at[:, pl.ds(3 * core, 3)]
    send(fr_mine, fr_mine, S_FRC, partner)

    bias_sum = jnp.zeros((GR, W), F32)
    dc = jnp.zeros((PAD, W), F32)

    def gate_grads(n, dh, dc):
        to_c, to_i, to_f, to_g, to_o, f_g = factors[2 - n]
        dc = dc + dh * to_c
        dz = jnp.concatenate([x[0:OWN] for x in (dc * to_i, dc * to_f, dc * to_g, dh * to_o)], 0)
        src = dz_send.at[n]
        dst = dzbuf.at[n]
        src[...] = dz.astype(BF)
        dst[ti] = src[...]
        if n < 2:
            send(src, dznear.at[n, 0], (S_DZN2, S_DZN1)[n], tile_dev(up))
            send(src, dznear.at[n, 1], (S_DZN2, S_DZN1)[n], tile_dev(down))
        else:
            each_tile_far_first(lambda to: send(src, dst.at[ti], S_DZ0, tile_dev(to)))
        return dz, dc * f_g

    def await_near(n):
        got(dznear.at[n], (S_DZN2, S_DZN1)[n])

    def share_z(n):
        each_z(lambda to: send(dz_send.at[n], dzbuf.at[n, ti], (S_DZZ2, S_DZZ1)[n], tile_dev(row * 4 + to)))

    def share_x(n):
        got(dzbuf.at[n, pl.ds(0, 3)], (S_DZZ2, S_DZZ1)[n])
        mine = dzbuf.at[n, pl.ds(4 * row, 4)]
        each_x(lambda to: send(mine, mine, (S_DZX2, S_DZX1)[n], tile_dev(to * 4 + col)))

    def await_x(n):
        got(dzbuf.at[n, pl.ds(0, 12)], (S_DZX2, S_DZX1)[n])

    def back(n):
        zero = jnp.zeros((GR, W), F32)

        def stacked(x):
            return [shifted(x, 1 - b).astype(BF) for b in range(3)]

        own = nn(whpt[...], jnp.concatenate(stacked(dz_send[n].astype(F32)), 0))
        await_near(n)
        above = stacked(jnp.where(has_up, dznear[n, 1].astype(F32), zero))
        below = stacked(jnp.where(has_down, dznear[n, 0].astype(F32), zero))
        whole = own + nn(whpt2[...], jnp.concatenate(above + below, 0))
        dhp[n + 1] = whole.astype(BF).reshape(L, PAD, W)

    def weight_part(n):
        t = 2 - n
        src = dzbuf.at[n]

        def body(r, carry):
            block = src[r].astype(F32)
            for b in range(3):
                stack[b * GR:(b + 1) * GR, pl.ds(pl.multiple_of((r + 1) * W, W), W)] = shifted(block, 1 - b).astype(BF)
            at = pl.multiple_of(r * W, W)
            scat[0:2 * PAD, pl.ds(at, W)] = fblk[r, 2 * t:2 * t + 2].reshape(2 * PAD, W)
            if t > 0:
                scat[2 * PAD:4 * PAD, pl.ds(at, W)] = hblk[t - 1, r].reshape(2 * PAD, W)
            return carry

        lax.fori_loop(0, T, body, 0, unroll=8)
        return jnp.concatenate([nt(stack[:, (2 - a) * W:(2 - a + T) * W], scat[...]) for a in range(3)], 0).T

    def share_weights(n, x):
        y = nn((x * (1.0 / 256.0)).astype(BF), pack[...]).astype(BF)
        wsend[n] = (nn(rsel[0], y[:, :256]) + nn(rsel[1], y[:, 256:])).astype(BF)
        src = wsend.at[n]
        dst = wrecv.at[n]
        dst[ti] = src[...]
        if n == 0:
            each_z(lambda to: send(src, dst.at[ti], S_WHZ, tile_dev(row * 4 + to)))
        else:
            send(src, dst.at[ti], S_WFA, tile_dev(row * 4 + lax.rem(col + 2, 4)))
            for mx in (2, 1, 3, 0):
                for mz in (1, 3, 0) if mx else (1, 3):
                    to = lax.rem(row + mx, 4) * 4 + lax.rem(col + mz, 4)
                    send(src, dst.at[ti], S_WF, tile_dev(to))

    def forward_weights():
        opposite = row * 4 + lax.rem(col + 2, 4)
        got(wrecv.at[1, 0], S_WFA)
        mine = wrecv.at[1, opposite]
        each_x(lambda to: send(mine, mine, S_WFB, tile_dev(to * 4 + col)))

    def share_weights_x():
        got(wrecv.at[0, pl.ds(0, 3)], S_WHZ)
        mine = wrecv.at[0, pl.ds(4 * row, 4)]
        each_x(lambda to: send(mine, mine, S_WHX, tile_dev(to * 4 + col)))

    def finish_weights(n):
        if n == 0:
            got(wrecv.at[0, pl.ds(0, 12)], S_WHX)
        else:
            got(wrecv.at[1, pl.ds(0, 11)], S_WF)
            got(wrecv.at[1, pl.ds(0, 3)], S_WFB)
        for s_ in range(T):
            block = wrecv[n, s_].astype(F32)
            xf[24 * s_:24 * (s_ + 1), 0:256] = block[0:24]
            xf[24 * s_:24 * (s_ + 1), 256:512] = block[24:48]
        out = nt(unpack[...], xf[...].astype(BF)).astype(BF)
        col = HID * (1 - n)
        wg_out[:, col:col + HID] = out

    dz, dc = gate_grads(0, await_dh(0), dc)
    bias_sum = bias_sum + dz
    back(0)
    share_dh(1)
    share_z(0)
    got(hq.at[pl.ds(0, T - 1), 0], S_HQ)
    hq_mine = hq.at[:, core]
    send(hq_mine, hq_mine, S_HQC, partner)
    share_blocks(1)
    share_blocks(0)
    share_x(0)

    got(st_tile.at[pl.ds(0, T - 1)], S_ST)
    stl_send[0:8, :] = jnp.sum(st_tile[...], axis=0)
    lane = lax.broadcasted_iota(jnp.int32, (8, W), 1)
    stl_send[8:16, :] = jnp.where(lane == idx[0], 1.0, 0.0)
    each_lead(lambda to: send(stl_send, stl.at[li], S_STL, lead_dev(to)))
    stl[li] = stl_send[...]

    got(hq.at[:, 0], S_HQC)
    got(cotb.at[pl.ds(0, 12)], S_COTX)
    gamma_q = 1.0 + film_q[row, :, 0:1]
    beta_q = film_q[row, :, 1:2]

    def head_rows(r, carry):
        block = cotb[r].astype(F32)
        at = pl.multiple_of((r + 2) * W, W)
        for b in range(3):
            cc[96 * b:96 * (b + 1), pl.ds(at, W)] = shifted(block, 2 * (1 - b)).astype(BF)
        uq = gamma_q * hq[r].reshape(96, W).astype(F32) + beta_q
        vv[0:96, pl.ds(pl.multiple_of(r * W, W), W)] = (uq * jax.nn.sigmoid(uq)).astype(BF)
        return carry

    lax.fori_loop(0, T, head_rows, 0)
    for a in range(3):
        first = (4 - 2 * a) * W
        part = nt(cc[:, first:first + T * W], vv[...])
        for b in range(3):
            k = 3 * a + b
            for d in range(4):
                pbuf[d * 256 + k * 24:d * 256 + (k + 1) * 24, :] = part[b * 96 + d * 24:b * 96 + (d + 1) * 24]
    psend[...] = pbuf[...].astype(BF).reshape(L, 32, W)
    prec[li] = psend[8 * lax.rem(li, 4) + lax.div(li, 4)]

    dz, dc = gate_grads(1, await_dh(1), dc)
    bias_sum = bias_sum + dz
    back(1)
    share_dh(2)
    share_z(1)
    each_lead(lambda to: send(psend.at[8 * lax.rem(to, 4) + lax.div(to, 4)], prec.at[li], S_PR, lead_dev(to)))
    swap_blocks(1)
    swap_blocks(0)
    share_x(1)
    await_x(0)
    got(fblk.at[:, pl.ds(0, 3)], S_FRC)
    await_blocks(1)
    grads = weight_part(0)

    dz, dc = gate_grads(2, await_dh(2), dc)

    got(prec.at[pl.ds(0, L - 1)], S_PR)
    psum[...] = (jnp.sum(prec[...].astype(F32), axis=0) * (1.0 / 256.0)).astype(BF)
    owner = col * 4 + lax.rem(li, 4)
    gathers = lax.rem(li, 4) == col

    @pl.when(owner != ti)
    def _():
        send(psum, ptile.at[row], S_PT, tile_dev(owner))

    @pl.when(owner == ti)
    def _():
        ptile[row] = psum[...]

    await_x(1)
    await_blocks(0)
    grads = grads + weight_part(1)
    share_weights(0, grads[2 * PAD:4 * PAD])
    bias_sum = bias_sum + dz
    column = jnp.sum(bias_sum, axis=1, keepdims=True)
    lane = lax.broadcasted_iota(jnp.int32, (GR, W), 1)
    sub = lax.broadcasted_iota(jnp.int32, (GR, W), 0)
    line = jnp.sum(jnp.where(lane == sub, column, 0.0), axis=0, keepdims=True)
    bi_send[...] = jnp.broadcast_to(line, (8, W))
    each_tile_far_first(lambda to: send(bi_send, bi.at[ti], S_BI, tile_dev(to)))
    bi[ti] = bi_send[...]

    @pl.when(gathers)
    def _():
        @pl.when(owner == ti)
        def _():
            got(ptile.at[pl.ds(0, 3)], S_PT)

        @pl.when(owner != ti)
        def _():
            got(ptile, S_PT)

        each_lead(lambda to: send(ptile, plead.at[lax.div(li, 4)], S_PL, lead_dev(to)))
        plead[lax.div(li, 4)] = ptile[...]

    got(dzbuf.at[2, pl.ds(0, T - 1)], S_DZ0)
    share_weights_x()
    grads0 = weight_part(2)
    share_weights(1, grads[0:2 * PAD] + grads0[0:2 * PAD])
    forward_weights()

    got(stl.at[pl.ds(0, L - 1)], S_STL)

    def table(l, acc):
        block = stl[l]
        return tuple(acc[m] + block[8:16, m:m + 1] * block[0:8, :] for m in range(16))

    acc = lax.fori_loop(0, L, table, tuple(jnp.zeros((8, W), F32) for _ in range(16)))
    for m in range(16):
        fg_out[m] = acc[m] * (1.0 / 256.0)
    got(bi.at[pl.ds(0, T - 1)], S_BI)
    bg_out[...] = jnp.sum(bi[...], axis=0) * (1.0 / 256.0)
    finish_weights(0)

    @pl.when(gathers)
    def _():
        got(plead.at[pl.ds(0, 7)], S_PL)

    @pl.when(jnp.logical_not(gathers))
    def _():
        got(plead, S_PL)

    wide = jnp.concatenate([plead[:, q].reshape(256, W) for q in range(4)], 1)
    hg_out[...] = nn(wide, spread[...])[0:TAPS * 24].astype(BF)
    finish_weights(1)

    for t in range(3):
        sent(rx.at[t], (S_YX0, S_YX1, S_YX2)[t])
        sent(hbuf.at[t, pl.ds(0, L - 1)], (S_H1, S_H2, S_H3)[t])
        sent(dhr.at[t, pl.ds(0, L - 1)], (S_DH3, S_DH2, S_DH1)[t])
    for t in range(2):
        sent(rh.at[t], (S_YH1, S_YH2)[t])
        sent(dznear.at[t], (S_DZN2, S_DZN1)[t])
        sent(dzbuf.at[t, pl.ds(0, 3)], (S_DZZ2, S_DZZ1)[t])
        sent(dzbuf.at[t, pl.ds(0, 12)], (S_DZX2, S_DZX1)[t])
        sent(hblk.at[t, pl.ds(0, T - 1), 0], (S_HB1, S_HB2)[t])
        sent(hblk.at[t, :, 0], (S_HB1C, S_HB2C)[t])
    sent(dzbuf.at[2, pl.ds(0, T - 1)], S_DZ0)
    sent(wrecv.at[0, pl.ds(0, 3)], S_WHZ)
    sent(wrecv.at[0, pl.ds(0, 12)], S_WHX)
    sent(wrecv.at[1, pl.ds(0, 11)], S_WF)
    sent(wrecv.at[1, 0], S_WFA)
    sent(wrecv.at[1, pl.ds(0, 3)], S_WFB)
    sent(coth.at[0], S_COTH)
    sent(coth.at[1], S_COTH2)
    sent(cotz.at[pl.ds(0, 3)], S_COTZ)
    sent(cotb.at[pl.ds(0, 12)], S_COTX)
    sent(fblk.at[pl.ds(0, T - 1), pl.ds(0, 3)], S_FR)
    sent(fblk.at[:, pl.ds(0, 3)], S_FRC)
    sent(hq.at[pl.ds(0, T - 1), 0], S_HQ)
    sent(hq.at[:, 0], S_HQC)
    sent(st_tile.at[pl.ds(0, T - 1)], S_ST)
    sent(stl.at[pl.ds(0, L - 1)], S_STL)
    sent(bi.at[pl.ds(0, T - 1)], S_BI)
    sent(prec.at[pl.ds(0, L - 1)], S_PR)

    @pl.when(owner != ti)
    def _():
        sent(psum, S_PT)

    @pl.when(gathers)
    def _():
        def body(d, carry):
            sent(ptile, S_PL)
            return carry
        lax.fori_loop(1, L, body, 0)


def finish(wg, bg, hg, fg, wg_out, bg_out, hg_out, fg_out):
    wg_out[...] = wg[...].astype(F32).reshape(OWN, TAPS, GATES, 2 * HID).astype(BF)
    hg_out[...] = hg[...]
    for j in range(GATES):
        bg_out[j:j + 1, :] = bg[0:1, j * OWN:(j + 1) * OWN]
    for m in range(16):
        for n in range(2):
            for q in range(3):
                fg_out[m, n:n + 1, W * q:W * (q + 1)] = fg[m, 3 * n + q:3 * n + q + 1, :]


def shards(frames, enc_weight, enc_bias, head_weight, film_table, lead_index, cotangent):
    a, pack, unpack, e, et, spread, rsel = [jnp.asarray(x) for x in one_hots()]
    wsrc = enc_weight.transpose(0, 2, 1, 3)
    hw = head_weight.transpose(1, 0, 2).reshape(TAPS * HID, HID)
    vm = pltpu.VMEM
    inputs = (
        wsrc, a, frames.reshape(3, HID, W), enc_bias.T, e, et, film_table, cotangent.reshape(HID, W), hw, pack, rsel,
        unpack, spread,
    )
    outs = pl.pallas_call(
        kernel,
        out_shape=(
            jax.ShapeDtypeStruct((OWN * TAPS * GATES, 2 * HID), BF),
            jax.ShapeDtypeStruct((8, W), F32),
            jax.ShapeDtypeStruct((TAPS * 24, HID), BF),
            jax.ShapeDtypeStruct((16, 8, W), F32),
        ),
        in_specs=[pl.BlockSpec(memory_space=pl.ANY)] * (N_IN - 1) + [pl.BlockSpec(memory_space=pltpu.SMEM)],
        out_specs=(pl.BlockSpec(memory_space=vm),) * 4,
        scratch_shapes=[vm(x.shape, x.dtype) for x in inputs] + [
            vm((TAPS * GR, 2 * HID), BF),
            vm((TAPS * GR, CP), BF),
            vm((CP, 3 * GR), BF),
            vm((CP, 6 * GR), BF),
            vm((W, HID), F32),
            vm((3, 3, GR, W), F32),
            vm((2, 3, GR, W), F32),
            vm((3, 2, GR, W), F32),
            vm((2, 2, GR, W), F32),
            vm((3, L, PAD, W), BF),
            vm((2, HID, W), BF),
            vm((4, 96, W), BF),
            vm((4, 96, W), BF),
            vm((T, 96, W), BF),
            vm((T, 6, PAD, W), BF),
            vm((T, 6, PAD, W), BF),
            vm((2, T, 2, PAD, W), BF),
            vm((2, L, PAD, W), F32),
            vm((3, L, PAD, W), BF),
            vm((3, L, PAD, W), BF),
            vm((8, 48, W), BF),
            vm((T, 2, 48, W), BF),
            vm((8, W), F32),
            vm((T, 8, W), F32),
            vm((16, W), F32),
            vm((L, 16, W), F32),
            vm((3, GR, W), BF),
            vm((2, 2, GR, W), BF),
            vm((3, T, GR, W), BF),
            vm((8, W), F32),
            vm((T, 8, W), F32),
            vm((3 * GR, (T + 2) * W), BF),
            vm((4 * PAD, T * W), BF),
            vm((2, 48, 256), BF),
            vm((2, T, 48, 256), BF),
            vm((HID, 512), F32),
            vm((3 * 96, (T + 4) * W), BF),
            vm((W, T * W), BF),
            vm((L * 32, W), F32),
            vm((L, 32, W), BF),
            vm((L, 32, W), BF),
            vm((32, W), BF),
            vm((4, 32, W), BF),
            vm((8, 4, 32, W), BF),
            vm((L, PAD, 8), F32),
            vm((4, 96, 8), F32),
            vm((HID, W), F32),
            pltpu.SemaphoreType.DMA((NSEM,)),
            pltpu.SemaphoreType.DMA((NSEM,)),
            pltpu.SemaphoreType.DMA((N_IN - 1,)),
        ],
        compiler_params=pltpu.CompilerParams(
            collective_id=0, has_side_effects=True, vmem_limit_bytes=56 * 2**20
        ),
    )(*inputs, lead_index)
    wg, bg, hg, fg = pl.pallas_call(
        finish,
        out_shape=(
            jax.ShapeDtypeStruct((OWN, TAPS, GATES, 2 * HID), BF),
            jax.ShapeDtypeStruct((GATES, OWN), F32),
            jax.ShapeDtypeStruct((TAPS * 24, HID), BF),
            jax.ShapeDtypeStruct((16, 2, HID), F32),
        ),
        in_specs=[pl.BlockSpec(memory_space=vm)] * 4,
        out_specs=(pl.BlockSpec(memory_space=vm),) * 4,
    )(*outs)
    return wg.transpose(0, 2, 1, 3), bg.T, hg.reshape(TAPS, 24, HID).transpose(1, 0, 2), fg


def solution(mesh):
    in_specs = (
        P(None, None, "tile", None),
        P("lead", None, None, None),
        P("lead", None),
        P(),
        P(),
        P("lead"),
        P("lead", None, "tile", None),
    )
    out_specs = (P("lead", None, None, None), P("lead", None), P("tile", None, None), P())
    return jax.shard_map(shards, mesh=mesh, in_specs=in_specs, out_specs=out_specs, check_vma=False)
```

```python
import numpy as np
import jax
import jax.numpy as jnp
import ml_dtypes
from jax import lax
from jax.experimental import pallas as pl
from jax.experimental.pallas import tpu as pltpu
from jax.sharding import PartitionSpec as P

MESH = pl.DeviceIdType.MESH
BF = jnp.bfloat16
F32 = jnp.float32
L, T, HID, W = 32, 16, 384, 128
OWN, PAD, GATES, TAPS = 12, 16, 4, 9
GR = GATES * OWN
CP = L * PAD


def one_hots():
    a = np.zeros((TAPS * GR, OWN * TAPS * GATES), np.float32)
    pack = np.zeros((TAPS * GR, 512), np.float32)
    unpack = np.zeros((OWN * TAPS * GATES, 512), np.float32)
    for k in range(TAPS):
        for j in range(GATES):
            for o in range(OWN):
                inner = k * GR + j * OWN + o
                outer = (o * TAPS + k) * GATES + j
                column = inner + (0 if k < 5 else 16)
                a[inner, outer] = 1
                pack[inner, column] = 1
                unpack[outer, column] = 1
    e = np.zeros((HID, CP), np.float32)
    for i in range(L):
        for o in range(OWN):
            e[i * OWN + o, i * PAD + o] = 1
    spread = np.zeros((512, HID), np.float32)
    for q in range(4):
        for c in range(96):
            spread[128 * q + c, 96 * q + c] = 1
    rows = np.zeros((2, 48, 32), np.float32)
    for half in range(2):
        for c in range(24):
            rows[half, 24 * half + c, (c // OWN) * PAD + c % OWN] = 1
    return [x.astype(ml_dtypes.bfloat16) for x in (a, pack, unpack, e, e.T.copy(), spread, rows)]


def nn(a, b):
    return lax.dot_general(a, b, (((1,), (0,)), ((), ())), preferred_element_type=F32)


def nt(a, b):
    return lax.dot_general(a, b, (((1,), (1,)), ((), ())), preferred_element_type=F32)


def shifted(x, s):
    if s == 0:
        return x
    lane = lax.broadcasted_iota(jnp.int32, x.shape, 1)
    keep = lane < W - s if s > 0 else lane >= -s
    return jnp.where(keep, pltpu.roll(x, (-s) % W, 1), 0.0)


def shifted_rows(x, s):
    if s == 0:
        return x
    row = lax.broadcasted_iota(jnp.int32, x.shape, 0)
    keep = row < W - s if s > 0 else row >= -s
    return jnp.where(keep, pltpu.roll(x, (-s) % W, 0), 0.0)


(S_YX0, S_YX1, S_YX2, S_H1, S_H2, S_H3, S_YH1, S_YH2, S_COTH, S_COTZ, S_COTX, S_FR, S_FRC, S_HB1, S_HB2, S_HB1C, S_HB2C,
 S_DH3, S_DH2, S_DH1, S_HQ, S_HQC, S_ST, S_STL, S_DZN2, S_DZN1, S_DZ0, S_DZZ2, S_DZZ1, S_DZX2, S_DZX1, S_BI, S_WHZ, S_WHX, S_WF,
 S_WFA, S_WFB, S_PR, S_PT, S_PL, S_COTH2, NSEM) = range(42)


N_IN = 14


def kernel(*refs):
    inputs, (wg_out, bg_out, hg_out, fg_out), refs = refs[:N_IN], refs[N_IN:N_IN + 4], refs[N_IN + 4:]
    held, refs = refs[:N_IN - 1], refs[N_IN - 1:]
    idx = inputs[N_IN - 1]
    (
        wt, whp, whpt, dvt_ref, yx, yh, rx, rh, hbuf, coth, cot4, cotz, cotb, fsend, fblk, hblk, dv_ref, dhp, dhr,
        h8, hq, st_send, st_tile, stl_send, stl, dz_send, dznear, dzbuf, bi_send, bi, stack, scat,
        wsend, wrecv, xf, cc, vv, pbuf, psend, prec, psum, ptile, plead, film_col, film_q, flat, ssem, rsem, lsem,
    ) = refs
    wsrc, a_ref, frames, bias, e_ref, et_ref, film, cot, hw, pack, rsel, unpack, spread = held
    li = lax.axis_index("lead")
    ti = lax.axis_index("tile")

    def lead_dev(to):
        return (to, ti)

    def tile_dev(to):
        return (li, to)

    def send(src, dst, sem, dev):
        pltpu.make_async_remote_copy(
            src_ref=src, dst_ref=dst, send_sem=ssem.at[sem], recv_sem=rsem.at[sem], device_id=dev, device_id_type=MESH
        ).start()

    def got(ref, sem):
        pltpu.make_async_copy(ref, ref, rsem.at[sem]).wait()

    def sent(ref, sem):
        pltpu.make_async_copy(ref, ref, ssem.at[sem]).wait()

    def load(n):
        return pltpu.make_async_copy(inputs[n], held[n], lsem.at[n])

    def each_lead(fn):
        ring, side = lax.rem(lax.div(li, 2), 8), lax.div(li, 16)

        def body(n, carry):
            m = lax.div(n, 4)
            step = lax.div(m + 1, 2) * (1 - 2 * lax.rem(m, 2))
            other = lax.rem(ring + 12 + step, 8)
            rest = 3 - lax.rem(n, 4)
            side_to = lax.rem(side + lax.div(rest, 2), 2)
            core_to = lax.rem(core + lax.rem(rest, 2), 2)
            fn(side_to * 16 + other * 2 + core_to)
            return carry
        lax.fori_loop(0, L - 1, body, 0)

    row, col = lax.div(ti, 4), lax.rem(ti, 4)
    core = lax.rem(li, 2)
    partner = lead_dev(li + 1 - 2 * core)

    def each_z(fn):
        for m in (2, 1, 3):
            fn(lax.rem(col + m, 4))

    def each_x(fn):
        for m in (2, 1, 3):
            fn(lax.rem(row + m, 4))

    def each_tile_far_first(fn):

        def away(m):
            return 6 + lax.div(m + 1, 2) * (1 - 2 * lax.rem(m, 2))

        def body(n, carry):
            fn(lax.rem(row + away(lax.div(n, 4)), 4) * 4 + lax.rem(col + away(lax.rem(n, 4)), 4))
            return carry
        lax.fori_loop(0, T - 1, body, 0)

    def each_tile(fn, first=1, last=T):
        def body(d, carry):
            fn(lax.rem(ti + d, T))
            return carry
        lax.fori_loop(first, last, body, 0)

    bar = pltpu.get_barrier_semaphore()
    each_lead(lambda to: pl.semaphore_signal(bar, inc=1, device_id=lead_dev(to), device_id_type=MESH))
    each_tile_far_first(lambda to: pl.semaphore_signal(bar, inc=1, device_id=tile_dev(to), device_id_type=MESH))
    for n in range(N_IN - 1):
        load(n).start()

    up = lax.rem(ti + 1, T)
    down = lax.rem(ti + T - 1, T)
    has_up = ti < T - 1
    has_down = ti > 0

    for n in range(4):
        load(n).wait()
    outer = wsrc[...].astype(F32).reshape(OWN * TAPS * GATES, 2 * HID).astype(BF)
    wt[...] = nn(a_ref[...], outer).astype(BF)
    sub = lax.broadcasted_iota(jnp.int32, (OWN, OWN), 0)
    lane = lax.broadcasted_iota(jnp.int32, (OWN, OWN), 1)
    bias_cols = [jnp.sum(jnp.where(sub == lane, bias[j:j + 1, :], 0.0), axis=1, keepdims=True) for j in range(GATES)]

    def row_parts(g):
        return [sum(shifted(g[(3 * a + b) * GR:(3 * a + b + 1) * GR], b - 1) for b in range(3)) for a in range(3)]

    own_x = []

    def frame_parts(t):
        parts = row_parts(nn(wt[:, 0:HID], frames[t]))
        for a in (0, 2):
            yx[t, a] = parts[a].astype(BF)
        own_x.append(parts[1])

    frame_parts(0)
    pl.semaphore_wait(bar, L + T - 2)

    def halo(src, dst, sem):
        send(src.at[0], dst.at[0], sem, tile_dev(up))
        send(src.at[2], dst.at[1], sem, tile_dev(down))

    halo(yx.at[0], rx.at[0], S_YX0)
    for n in range(4, N_IN - 1):
        load(n).wait()
    whp[...] = nn(wt[:, HID:], e_ref[...]).astype(BF)
    whpt[...] = nt(et_ref[...], wt[:, HID:]).astype(BF)
    def from_neighbours(r):
        return jnp.where(has_down, r[0].astype(F32), 0.0) + jnp.where(has_up, r[1].astype(F32), 0.0)

    def padded(x):
        return jnp.concatenate([x, jnp.zeros((PAD - OWN, W), F32)], 0)

    def cell(z, previous):
        z = [padded(z[j * OWN:(j + 1) * OWN] + bias_cols[j]) for j in range(GATES)]
        i_g = jax.nn.sigmoid(z[0])
        f_g = jax.nn.sigmoid(z[1])
        g_g = jnp.tanh(z[2])
        o_g = jax.nn.sigmoid(z[3])
        now = f_g * previous + i_g * g_g
        return (i_g, f_g, g_g, o_g, previous, now), (o_g * jnp.tanh(now)).astype(BF)

    def share_h(t, h):
        buf = hbuf.at[t]
        buf[li] = h
        sem = (S_H1, S_H2, S_H3)[t]
        each_lead(lambda to: send(buf.at[li], buf.at[li], sem, lead_dev(to)))

    def await_h(t):
        got(hbuf.at[t, pl.ds(0, L - 1)], (S_H1, S_H2, S_H3)[t])

    saved = []
    got(rx.at[0], S_YX0)
    z = own_x[0] + from_neighbours(rx.at[0])
    state, h = cell(z, jnp.zeros((PAD, W), F32))
    saved.append(state)
    share_h(0, h)
    for t in (1, 2):
        frame_parts(t)
        halo(yx.at[t], rx.at[t], (S_YX0, S_YX1, S_YX2)[t])
    send(cot, coth.at[0], S_COTH, tile_dev(lax.rem(ti + 2, T)))
    for t in range(3):
        fsend[:, 2 * t:2 * t + 2] = nn(et_ref[...], frames[t]).astype(BF).reshape(T, 2, PAD, W)
    for p in range(4):
        cot4[p] = cot[96 * p:96 * (p + 1), :]
    slot = lax.broadcasted_iota(jnp.int32, (16, 2, HID), 0)
    lines = jnp.sum(jnp.where(slot == idx[0], film[...], 0.0), axis=0)
    lines = jnp.concatenate([lines, jnp.zeros((6, HID), F32)], 0).T
    film_col[...] = jnp.zeros_like(film_col)
    for i in range(L):
        film_col[i, 0:OWN, :] = lines[i * OWN:(i + 1) * OWN]
    film_q[...] = lines.reshape(4, 96, 8)
    for at in (0, (T + 1) * W):
        stack[:, at:at + W] = jnp.zeros((3 * GR, W), BF)
    for at in (0, (T + 2) * W):
        cc[:, at:at + 2 * W] = jnp.zeros((3 * 96, 2 * W), BF)
    vv[96:W, :] = jnp.zeros((W - 96, T * W), BF)
    for d in range(4):
        pbuf[256 * d + 216:256 * (d + 1), :] = jnp.zeros((40, W), F32)
    scat[...] = jnp.zeros_like(scat)

    def half(x):
        return x.at[pl.ds(3 * core, 3)]

    def send_frames(to):
        send(half(fsend.at[to]), half(fblk.at[ti]), S_FR, tile_dev(to))

    zero_row = jnp.zeros((HID, W), BF)

    def head_product(a, x):
        ct = x.astype(F32).T
        total = None
        for b in range(3):
            k = 3 * a + b
            term = nn(shifted_rows(ct, -2 * (b - 1)).astype(BF), hw[k * HID:(k + 1) * HID, :])
            total = term if total is None else total + term
        return total

    for t in (1, 2):
        await_h(t - 1)
        parts = row_parts(nn(whp[...], hbuf[t - 1].reshape(CP, W)))
        for a in (0, 2):
            yh[t - 1, a] = parts[a].astype(BF)
        sem = (S_YH1, S_YH2)[t - 1]
        halo(yh.at[t - 1], rh.at[t - 1], sem)
        got(rx.at[t], (S_YX0, S_YX1, S_YX2)[t])
        base = own_x[t] + from_neighbours(rx.at[t]) + parts[1]
        got(rh.at[t - 1], sem)
        z = base + from_neighbours(rh.at[t - 1])
        state, h = cell(z, saved[-1][5])
        saved.append(state)
        share_h(t, h)
        if t == 1:
            send(cot, coth.at[1], S_COTH2, tile_dev(lax.rem(ti + T - 2, T)))
            dvt = head_product(1, cot[...])
            got(coth.at[0], S_COTH)
            dvt_ref[...] = dvt + head_product(2, jnp.where(ti >= 2, coth[0], zero_row))
    each_tile_far_first(send_frames)
    fblk[ti, pl.ds(3 * core, 3)] = fsend[ti, pl.ds(3 * core, 3)]
    each_z(lambda to: send(cot4.at[to], cotz.at[col], S_COTZ, tile_dev(row * 4 + to)))
    cotz[col] = cot4[col]
    got(coth.at[1], S_COTH2)
    dv = (dvt_ref[...] + head_product(0, jnp.where(ti < T - 2, coth[1], zero_row))).T
    dv_ref[...] = jnp.zeros_like(dv_ref)
    for i in range(L):
        dv_ref[0, i, 0:OWN, :] = dv[i * OWN:(i + 1) * OWN]
    dv_ref[1] = nn(et_ref[...], cot[...]).reshape(L, PAD, W)
    factors = []
    for i_g, f_g, g_g, o_g, previous, now in saved:
        sq = jnp.tanh(now)
        factors.append((
            o_g * (1.0 - sq * sq), g_g * i_g * (1.0 - i_g), previous * f_g * (1.0 - f_g), i_g * (1.0 - g_g * g_g),
            sq * o_g * (1.0 - o_g), f_g,
        ))

    def share_blocks(t):
        hsem = (S_HB1, S_HB2)[t]
        hb = hblk.at[t]
        hs = hbuf.at[t]
        hb[ti, core] = hs[2 * ti + core]
        each_tile_far_first(lambda to: send(hs.at[2 * to + core], hb.at[ti, core], hsem, tile_dev(to)))

    def swap_blocks(t):
        got(hblk.at[t, pl.ds(0, T - 1), 0], (S_HB1, S_HB2)[t])
        mine = hblk.at[t, :, core]
        send(mine, mine, (S_HB1C, S_HB2C)[t], partner)

    def await_blocks(t):
        got(hblk.at[t, :, 0], (S_HB1C, S_HB2C)[t])

    await_h(2)
    h_wide = hbuf[2].reshape(CP, W).astype(F32)
    columns = film_col[...].reshape(CP, 8)
    gamma = 1.0 + columns[:, 0:1]
    u = gamma * h_wide + columns[:, 1:2]
    s = jax.nn.sigmoid(u)
    du = dv_ref[0].reshape(CP, W) * s * (1.0 + u * (1.0 - s))
    dhp[0] = (dv_ref[1].reshape(CP, W) + gamma * du).astype(BF).reshape(L, PAD, W)

    def share_dh(n):
        sem = (S_DH3, S_DH2, S_DH1)[n]
        src = dhp.at[n]
        dst = dhr.at[n]
        each_lead(lambda to: send(src.at[to], dst.at[li], sem, lead_dev(to)))
        dst[li] = src[li]

    def await_dh(n):
        got(dhr.at[n, pl.ds(0, L - 1)], (S_DH3, S_DH2, S_DH1)[n])
        return jnp.sum(dhr[n].astype(F32), axis=0)

    share_dh(0)
    h8[...] = nn(e_ref[...], hbuf[2].reshape(CP, W)).astype(BF).reshape(8, 48, W)
    each_tile_far_first(lambda to: send(h8.at[2 * lax.div(to, 4) + core], hq.at[ti, core], S_HQ, tile_dev(to)))
    hq[ti, core] = h8[2 * row + core]
    got(cotz.at[pl.ds(0, 3)], S_COTZ)
    each_x(lambda to: send(cotz, cotb.at[pl.ds(4 * row, 4)], S_COTX, tile_dev(to * 4 + col)))
    cotb[pl.ds(4 * row, 4)] = cotz[...]
    st_send[...] = jnp.zeros_like(st_send)
    for n, field in enumerate((du * h_wide, du)):
        for i in range(L):
            flat[i * OWN:(i + 1) * OWN, :] = field[i * PAD:i * PAD + OWN]
        line = jnp.sum(flat[...].T, axis=0, keepdims=True)
        for q in range(3):
            st_send[3 * n + q:3 * n + q + 1, :] = line[:, 128 * q:128 * (q + 1)]
    each_tile_far_first(lambda to: send(st_send, st_tile.at[ti], S_ST, tile_dev(to)))
    st_tile[ti] = st_send[...]
    got(fblk.at[pl.ds(0, T - 1), pl.ds(0, 3)], S_FR)
    fr_mine = fblk.at[:, pl.ds(3 * core, 3)]
    send(fr_mine, fr_mine, S_FRC, partner)

    bias_sum = jnp.zeros((GR, W), F32)
    dc = jnp.zeros((PAD, W), F32)

    def gate_grads(n, dh, dc):
        to_c, to_i, to_f, to_g, to_o, f_g = factors[2 - n]
        dc = dc + dh * to_c
        dz = jnp.concatenate([x[0:OWN] for x in (dc * to_i, dc * to_f, dc * to_g, dh * to_o)], 0)
        src = dz_send.at[n]
        dst = dzbuf.at[n]
        src[...] = dz.astype(BF)
        dst[ti] = src[...]
        if n < 2:
            send(src, dznear.at[n, 0], (S_DZN2, S_DZN1)[n], tile_dev(up))
            send(src, dznear.at[n, 1], (S_DZN2, S_DZN1)[n], tile_dev(down))
        else:
            each_tile_far_first(lambda to: send(src, dst.at[ti], S_DZ0, tile_dev(to)))
        return dz, dc * f_g

    def await_near(n):
        got(dznear.at[n], (S_DZN2, S_DZN1)[n])

    def share_z(n):
        each_z(lambda to: send(dz_send.at[n], dzbuf.at[n, ti], (S_DZZ2, S_DZZ1)[n], tile_dev(row * 4 + to)))

    def share_x(n):
        got(dzbuf.at[n, pl.ds(0, 3)], (S_DZZ2, S_DZZ1)[n])
        mine = dzbuf.at[n, pl.ds(4 * row, 4)]
        each_x(lambda to: send(mine, mine, (S_DZX2, S_DZX1)[n], tile_dev(to * 4 + col)))

    def await_x(n):
        got(dzbuf.at[n, pl.ds(0, 12)], (S_DZX2, S_DZX1)[n])

    def back(n):
        zero = jnp.zeros((GR, W), F32)

        def stacked(x):
            return [shifted(x, 1 - b).astype(BF) for b in range(3)]

        await_near(n)
        above = stacked(jnp.where(has_up, dznear[n, 1].astype(F32), zero))
        below = stacked(jnp.where(has_down, dznear[n, 0].astype(F32), zero))
        whole = nn(whpt[...], jnp.concatenate(above + stacked(dz_send[n].astype(F32)) + below, 0))
        dhp[n + 1] = whole.astype(BF).reshape(L, PAD, W)

    def weight_part(n):
        t = 2 - n
        src = dzbuf.at[n]

        def body(r, carry):
            block = src[r].astype(F32)
            for b in range(3):
                stack[b * GR:(b + 1) * GR, pl.ds(pl.multiple_of((r + 1) * W, W), W)] = shifted(block, 1 - b).astype(BF)
            at = pl.multiple_of(r * W, W)
            scat[0:2 * PAD, pl.ds(at, W)] = fblk[r, 2 * t:2 * t + 2].reshape(2 * PAD, W)
            if t > 0:
                scat[2 * PAD:4 * PAD, pl.ds(at, W)] = hblk[t - 1, r].reshape(2 * PAD, W)
            return carry

        lax.fori_loop(0, T, body, 0, unroll=8)
        return jnp.concatenate([nt(stack[:, (2 - a) * W:(2 - a + T) * W], scat[...]) for a in range(3)], 0).T

    def share_weights(n, x):
        y = nn((x * (1.0 / 256.0)).astype(BF), pack[...]).astype(BF)
        wsend[n] = (nn(rsel[0], y[:, :256]) + nn(rsel[1], y[:, 256:])).astype(BF)
        src = wsend.at[n]
        dst = wrecv.at[n]
        dst[ti] = src[...]
        if n == 0:
            each_z(lambda to: send(src, dst.at[ti], S_WHZ, tile_dev(row * 4 + to)))
        else:
            send(src, dst.at[ti], S_WFA, tile_dev(row * 4 + lax.rem(col + 2, 4)))
            for mx in (2, 1, 3, 0):
                for mz in (1, 3, 0) if mx else (1, 3):
                    to = lax.rem(row + mx, 4) * 4 + lax.rem(col + mz, 4)
                    send(src, dst.at[ti], S_WF, tile_dev(to))

    def forward_weights():
        opposite = row * 4 + lax.rem(col + 2, 4)
        got(wrecv.at[1, 0], S_WFA)
        mine = wrecv.at[1, opposite]
        each_x(lambda to: send(mine, mine, S_WFB, tile_dev(to * 4 + col)))

    def share_weights_x():
        got(wrecv.at[0, pl.ds(0, 3)], S_WHZ)
        mine = wrecv.at[0, pl.ds(4 * row, 4)]
        each_x(lambda to: send(mine, mine, S_WHX, tile_dev(to * 4 + col)))

    def finish_weights(n):
        if n == 0:
            got(wrecv.at[0, pl.ds(0, 12)], S_WHX)
        else:
            got(wrecv.at[1, pl.ds(0, 11)], S_WF)
            got(wrecv.at[1, pl.ds(0, 3)], S_WFB)
        for s_ in range(T):
            block = wrecv[n, s_].astype(F32)
            xf[24 * s_:24 * (s_ + 1), 0:256] = block[0:24]
            xf[24 * s_:24 * (s_ + 1), 256:512] = block[24:48]
        out = nt(unpack[...], xf[...].astype(BF)).reshape(OWN, TAPS, GATES, HID).astype(BF)
        first = HID * (1 - n)
        wg_out[:, :, :, first:first + HID] = out

    dz, dc = gate_grads(0, await_dh(0), dc)
    bias_sum = bias_sum + dz
    back(0)
    share_dh(1)
    share_z(0)
    got(hq.at[pl.ds(0, T - 1), 0], S_HQ)
    hq_mine = hq.at[:, core]
    send(hq_mine, hq_mine, S_HQC, partner)
    share_blocks(1)
    share_blocks(0)
    share_x(0)

    got(st_tile.at[pl.ds(0, T - 1)], S_ST)
    stl_send[0:8, :] = jnp.sum(st_tile[...], axis=0)
    lane = lax.broadcasted_iota(jnp.int32, (8, W), 1)
    stl_send[8:16, :] = jnp.where(lane == idx[0], 1.0, 0.0)
    each_lead(lambda to: send(stl_send, stl.at[li], S_STL, lead_dev(to)))
    stl[li] = stl_send[...]

    got(hq.at[:, 0], S_HQC)
    got(cotb.at[pl.ds(0, 12)], S_COTX)
    gamma_q = 1.0 + film_q[row, :, 0:1]
    beta_q = film_q[row, :, 1:2]

    def head_rows(r, carry):
        block = cotb[r].astype(F32)
        at = pl.multiple_of((r + 2) * W, W)
        for b in range(3):
            cc[96 * b:96 * (b + 1), pl.ds(at, W)] = shifted(block, 2 * (1 - b)).astype(BF)
        uq = gamma_q * hq[r].reshape(96, W).astype(F32) + beta_q
        vv[0:96, pl.ds(pl.multiple_of(r * W, W), W)] = (uq * jax.nn.sigmoid(uq)).astype(BF)
        return carry

    lax.fori_loop(0, T, head_rows, 0)
    for a in range(3):
        first = (4 - 2 * a) * W
        part = nt(cc[:, first:first + T * W], vv[...])
        for b in range(3):
            k = 3 * a + b
            for d in range(4):
                pbuf[d * 256 + k * 24:d * 256 + (k + 1) * 24, :] = part[b * 96 + d * 24:b * 96 + (d + 1) * 24]
    psend[...] = pbuf[...].astype(BF).reshape(L, 32, W)
    prec[li] = psend[8 * lax.rem(li, 4) + lax.div(li, 4)]

    dz, dc = gate_grads(1, await_dh(1), dc)
    bias_sum = bias_sum + dz
    back(1)
    share_dh(2)
    share_z(1)
    each_lead(lambda to: send(psend.at[8 * lax.rem(to, 4) + lax.div(to, 4)], prec.at[li], S_PR, lead_dev(to)))
    swap_blocks(1)
    swap_blocks(0)
    share_x(1)
    await_x(0)
    got(fblk.at[:, pl.ds(0, 3)], S_FRC)
    await_blocks(1)
    grads = weight_part(0)

    dz, dc = gate_grads(2, await_dh(2), dc)

    got(prec.at[pl.ds(0, L - 1)], S_PR)
    psum[...] = (jnp.sum(prec[...].astype(F32), axis=0) * (1.0 / 256.0)).astype(BF)
    owner = col * 4 + lax.rem(li, 4)
    gathers = lax.rem(li, 4) == col

    @pl.when(owner != ti)
    def _():
        send(psum, ptile.at[row], S_PT, tile_dev(owner))

    @pl.when(owner == ti)
    def _():
        ptile[row] = psum[...]

    await_x(1)
    await_blocks(0)
    grads = grads + weight_part(1)
    share_weights(0, grads[2 * PAD:4 * PAD])
    bias_sum = bias_sum + dz
    column = jnp.sum(bias_sum, axis=1, keepdims=True)
    lane = lax.broadcasted_iota(jnp.int32, (GR, W), 1)
    sub = lax.broadcasted_iota(jnp.int32, (GR, W), 0)
    line = jnp.sum(jnp.where(lane == sub, column, 0.0), axis=0, keepdims=True)
    bi_send[...] = jnp.broadcast_to(line, (8, W))
    each_tile_far_first(lambda to: send(bi_send, bi.at[ti], S_BI, tile_dev(to)))
    bi[ti] = bi_send[...]

    @pl.when(gathers)
    def _():
        @pl.when(owner == ti)
        def _():
            got(ptile.at[pl.ds(0, 3)], S_PT)

        @pl.when(owner != ti)
        def _():
            got(ptile, S_PT)

        each_lead(lambda to: send(ptile, plead.at[lax.div(li, 4)], S_PL, lead_dev(to)))
        plead[lax.div(li, 4)] = ptile[...]

    got(dzbuf.at[2, pl.ds(0, T - 1)], S_DZ0)
    share_weights_x()
    grads0 = weight_part(2)
    share_weights(1, grads[0:2 * PAD] + grads0[0:2 * PAD])
    forward_weights()

    got(stl.at[pl.ds(0, L - 1)], S_STL)

    def table(l, acc):
        block = stl[l]
        return tuple(acc[m] + block[8:16, m:m + 1] * block[0:8, :] for m in range(16))

    acc = lax.fori_loop(0, L, table, tuple(jnp.zeros((8, W), F32) for _ in range(16)))
    for m in range(16):
        rows6 = acc[m] * (1.0 / 256.0)
        for n in range(2):
            for q in range(3):
                fg_out[m, n:n + 1, W * q:W * (q + 1)] = rows6[3 * n + q:3 * n + q + 1]
    got(bi.at[pl.ds(0, T - 1)], S_BI)
    line = jnp.sum(bi[...], axis=0) * (1.0 / 256.0)
    for j in range(GATES):
        bg_out[j:j + 1, :] = line[0:1, j * OWN:(j + 1) * OWN]
    finish_weights(0)

    @pl.when(gathers)
    def _():
        got(plead.at[pl.ds(0, 7)], S_PL)

    @pl.when(jnp.logical_not(gathers))
    def _():
        got(plead, S_PL)

    wide = jnp.concatenate([plead[:, q].reshape(256, W) for q in range(4)], 1)
    hg_out[...] = nn(wide, spread[...])[0:TAPS * 24].astype(BF)
    finish_weights(1)

    for t in range(3):
        sent(rx.at[t], (S_YX0, S_YX1, S_YX2)[t])
        sent(hbuf.at[t, pl.ds(0, L - 1)], (S_H1, S_H2, S_H3)[t])
        sent(dhr.at[t, pl.ds(0, L - 1)], (S_DH3, S_DH2, S_DH1)[t])
    for t in range(2):
        sent(rh.at[t], (S_YH1, S_YH2)[t])
        sent(dznear.at[t], (S_DZN2, S_DZN1)[t])
        sent(dzbuf.at[t, pl.ds(0, 3)], (S_DZZ2, S_DZZ1)[t])
        sent(dzbuf.at[t, pl.ds(0, 12)], (S_DZX2, S_DZX1)[t])
        sent(hblk.at[t, pl.ds(0, T - 1), 0], (S_HB1, S_HB2)[t])
        sent(hblk.at[t, :, 0], (S_HB1C, S_HB2C)[t])
    sent(dzbuf.at[2, pl.ds(0, T - 1)], S_DZ0)
    sent(wrecv.at[0, pl.ds(0, 3)], S_WHZ)
    sent(wrecv.at[0, pl.ds(0, 12)], S_WHX)
    sent(wrecv.at[1, pl.ds(0, 11)], S_WF)
    sent(wrecv.at[1, 0], S_WFA)
    sent(wrecv.at[1, pl.ds(0, 3)], S_WFB)
    sent(coth.at[0], S_COTH)
    sent(coth.at[1], S_COTH2)
    sent(cotz.at[pl.ds(0, 3)], S_COTZ)
    sent(cotb.at[pl.ds(0, 12)], S_COTX)
    sent(fblk.at[pl.ds(0, T - 1), pl.ds(0, 3)], S_FR)
    sent(fblk.at[:, pl.ds(0, 3)], S_FRC)
    sent(hq.at[pl.ds(0, T - 1), 0], S_HQ)
    sent(hq.at[:, 0], S_HQC)
    sent(st_tile.at[pl.ds(0, T - 1)], S_ST)
    sent(stl.at[pl.ds(0, L - 1)], S_STL)
    sent(bi.at[pl.ds(0, T - 1)], S_BI)
    sent(prec.at[pl.ds(0, L - 1)], S_PR)

    @pl.when(owner != ti)
    def _():
        sent(psum, S_PT)

    @pl.when(gathers)
    def _():
        def body(d, carry):
            sent(ptile, S_PL)
            return carry
        lax.fori_loop(1, L, body, 0)


def finish(*refs):
    sems = refs[8]
    copies = [pltpu.make_async_copy(refs[0].at[n], refs[4].at[n], sems.at[n]) for n in range(OWN)]
    copies += [pltpu.make_async_copy(refs[n], refs[n + 4], sems.at[OWN + n]) for n in (1, 2, 3)]
    for copy in copies:
        copy.start()
    for copy in copies:
        copy.wait()


def shards(frames, enc_weight, enc_bias, head_weight, film_table, lead_index, cotangent):
    a, pack, unpack, e, et, spread, rsel = [jnp.asarray(x) for x in one_hots()]
    wsrc = enc_weight.transpose(0, 2, 1, 3)
    hw = head_weight.transpose(1, 0, 2).reshape(TAPS * HID, HID)
    vm = pltpu.VMEM
    inputs = (
        wsrc, a, frames.reshape(3, HID, W), enc_bias.T, e, et, film_table, cotangent.reshape(HID, W), hw, pack, rsel,
        unpack, spread,
    )
    outs = pl.pallas_call(
        kernel,
        out_shape=(
            jax.ShapeDtypeStruct((OWN, TAPS, GATES, 2 * HID), BF),
            jax.ShapeDtypeStruct((GATES, OWN), F32),
            jax.ShapeDtypeStruct((TAPS * 24, HID), BF),
            jax.ShapeDtypeStruct((16, 2, HID), F32),
        ),
        in_specs=[pl.BlockSpec(memory_space=pl.ANY)] * (N_IN - 1) + [pl.BlockSpec(memory_space=pltpu.SMEM)],
        out_specs=(pl.BlockSpec(memory_space=vm),) * 4,
        scratch_shapes=[vm(x.shape, x.dtype) for x in inputs] + [
            vm((TAPS * GR, 2 * HID), BF),
            vm((TAPS * GR, CP), BF),
            vm((CP, TAPS * GR), BF),
            vm((W, HID), F32),
            vm((3, 3, GR, W), BF),
            vm((2, 3, GR, W), BF),
            vm((3, 2, GR, W), BF),
            vm((2, 2, GR, W), BF),
            vm((3, L, PAD, W), BF),
            vm((2, HID, W), BF),
            vm((4, 96, W), BF),
            vm((4, 96, W), BF),
            vm((T, 96, W), BF),
            vm((T, 6, PAD, W), BF),
            vm((T, 6, PAD, W), BF),
            vm((2, T, 2, PAD, W), BF),
            vm((2, L, PAD, W), F32),
            vm((3, L, PAD, W), BF),
            vm((3, L, PAD, W), BF),
            vm((8, 48, W), BF),
            vm((T, 2, 48, W), BF),
            vm((8, W), F32),
            vm((T, 8, W), F32),
            vm((16, W), F32),
            vm((L, 16, W), F32),
            vm((3, GR, W), BF),
            vm((2, 2, GR, W), BF),
            vm((3, T, GR, W), BF),
            vm((8, W), F32),
            vm((T, 8, W), F32),
            vm((3 * GR, (T + 2) * W), BF),
            vm((4 * PAD, T * W), BF),
            vm((2, 48, 256), BF),
            vm((2, T, 48, 256), BF),
            vm((HID, 512), F32),
            vm((3 * 96, (T + 4) * W), BF),
            vm((W, T * W), BF),
            vm((L * 32, W), F32),
            vm((L, 32, W), BF),
            vm((L, 32, W), BF),
            vm((32, W), BF),
            vm((4, 32, W), BF),
            vm((8, 4, 32, W), BF),
            vm((L, PAD, 8), F32),
            vm((4, 96, 8), F32),
            vm((HID, W), F32),
            pltpu.SemaphoreType.DMA((NSEM,)),
            pltpu.SemaphoreType.DMA((NSEM,)),
            pltpu.SemaphoreType.DMA((N_IN - 1,)),
        ],
        compiler_params=pltpu.CompilerParams(
            collective_id=0, has_side_effects=True, vmem_limit_bytes=56 * 2**20
        ),
    )(*inputs, lead_index)
    wg, bg, hg, fg = pl.pallas_call(
        finish,
        out_shape=(
            jax.ShapeDtypeStruct((OWN, TAPS, GATES, 2 * HID), BF),
            jax.ShapeDtypeStruct((GATES, OWN), F32),
            jax.ShapeDtypeStruct((TAPS * 24, HID), BF),
            jax.ShapeDtypeStruct((16, 2, HID), F32),
        ),
        in_specs=[pl.BlockSpec(memory_space=pl.ANY)] * 4,
        out_specs=(pl.BlockSpec(memory_space=pl.ANY),) * 4,
        scratch_shapes=[pltpu.SemaphoreType.DMA((OWN + 4,))],
    )(*outs)
    return wg.transpose(0, 2, 1, 3), bg.T, hg.reshape(TAPS, 24, HID).transpose(1, 0, 2), fg


def solution(mesh):
    in_specs = (
        P(None, None, "tile", None),
        P("lead", None, None, None),
        P("lead", None),
        P(),
        P(),
        P("lead"),
        P("lead", None, "tile", None),
    )
    out_specs = (P("lead", None, None, None), P("lead", None), P("tile", None, None), P())
    return jax.shard_map(shards, mesh=mesh, in_specs=in_specs, out_specs=out_specs, check_vma=False)
```

```python
import numpy as np
import jax
import jax.numpy as jnp
import ml_dtypes
from jax import lax
from jax.experimental import pallas as pl
from jax.experimental.pallas import tpu as pltpu
from jax.sharding import PartitionSpec as P

MESH = pl.DeviceIdType.MESH
BF = jnp.bfloat16
F32 = jnp.float32
L, T, HID, W = 32, 16, 384, 128
OWN, PAD, GATES, TAPS = 12, 16, 4, 9
GR = GATES * OWN
CP = L * PAD


def one_hots():
    a = np.zeros((TAPS * GR, OWN * TAPS * GATES), np.float32)
    pack = np.zeros((TAPS * GR, 512), np.float32)
    unpack = np.zeros((OWN * TAPS * GATES, 512), np.float32)
    for k in range(TAPS):
        for j in range(GATES):
            for o in range(OWN):
                inner = k * GR + j * OWN + o
                outer = (o * TAPS + k) * GATES + j
                column = inner + (0 if k < 5 else 16)
                a[inner, outer] = 1
                pack[inner, column] = 1
                unpack[outer, column] = 1
    e = np.zeros((HID, CP), np.float32)
    for i in range(L):
        for o in range(OWN):
            e[i * OWN + o, i * PAD + o] = 1
    spread = np.zeros((512, HID), np.float32)
    for q in range(4):
        for c in range(96):
            spread[128 * q + c, 96 * q + c] = 1
    rows = np.zeros((2, 48, 32), np.float32)
    for half in range(2):
        for c in range(24):
            rows[half, 24 * half + c, (c // OWN) * PAD + c % OWN] = 1
    return [x.astype(ml_dtypes.bfloat16) for x in (a, pack, unpack, e, e.T.copy(), spread, rows)]


def nn(a, b):
    return lax.dot_general(a, b, (((1,), (0,)), ((), ())), preferred_element_type=F32)


def nt(a, b):
    return lax.dot_general(a, b, (((1,), (1,)), ((), ())), preferred_element_type=F32)


def shifted(x, s):
    if s == 0:
        return x
    lane = lax.broadcasted_iota(jnp.int32, x.shape, 1)
    keep = lane < W - s if s > 0 else lane >= -s
    return jnp.where(keep, pltpu.roll(x, (-s) % W, 1), 0.0)


def shifted_rows(x, s):
    if s == 0:
        return x
    row = lax.broadcasted_iota(jnp.int32, x.shape, 0)
    keep = row < W - s if s > 0 else row >= -s
    return jnp.where(keep, pltpu.roll(x, (-s) % W, 0), 0.0)


(S_YX0, S_YX1, S_YX2, S_H1, S_H2, S_H3, S_YH1, S_YH2, S_COTH, S_COTZ, S_COTX, S_FR, S_FRC, S_HB1, S_HB2, S_HB1C, S_HB2C,
 S_DH3, S_DH2, S_DH1, S_HQ, S_HQC, S_ST, S_STL, S_DZN2, S_DZN1, S_DZ0, S_DZZ2, S_DZZ1, S_DZX2, S_DZX1, S_BI, S_WHZ, S_WHX, S_WF,
 S_WFA, S_WFB, S_PR, S_PT, S_PL, S_COTH2, NSEM) = range(42)


N_IN = 14


def kernel(*refs):
    inputs, (wg_out, bg_out, hg_out, fg_out), refs = refs[:N_IN], refs[N_IN:N_IN + 4], refs[N_IN + 4:]
    held, refs = refs[:N_IN - 1], refs[N_IN - 1:]
    idx = inputs[N_IN - 1]
    (
        wt, whp, whpt, dvt_ref, yx, yh, rx, rh, hbuf, coth, cot4, cotz, cotb, fsend, fblk, hblk, dv_ref, dhp, dhr,
        h8, hq, st_send, st_tile, stl_send, stl, dz_send, dznear, dzbuf, bi_send, bi, stack, scat,
        wsend, wrecv, xf, cc, vv, pbuf, psend, prec, psum, ptile, plead, film_col, film_q, flat, ssem, rsem, lsem,
    ) = refs
    wsrc, a_ref, frames, bias, e_ref, et_ref, film, cot, hw, pack, rsel, unpack, spread = held
    li = lax.axis_index("lead")
    ti = lax.axis_index("tile")

    def lead_dev(to):
        return (to, ti)

    def tile_dev(to):
        return (li, to)

    def send(src, dst, sem, dev):
        pltpu.make_async_remote_copy(
            src_ref=src, dst_ref=dst, send_sem=ssem.at[sem], recv_sem=rsem.at[sem], device_id=dev, device_id_type=MESH
        ).start()

    def got(ref, sem):
        pltpu.make_async_copy(ref, ref, rsem.at[sem]).wait()

    def sent(ref, sem):
        pltpu.make_async_copy(ref, ref, ssem.at[sem]).wait()

    def load(n):
        return pltpu.make_async_copy(inputs[n], held[n], lsem.at[n])

    def each_lead(fn):
        ring, side = lax.rem(lax.div(li, 2), 8), lax.div(li, 16)

        def body(n, carry):
            m = lax.div(n, 4)
            step = lax.div(m + 1, 2) * (1 - 2 * lax.rem(m, 2))
            other = lax.rem(ring + 12 + step, 8)
            rest = 3 - lax.rem(n, 4)
            side_to = lax.rem(side + lax.div(rest, 2), 2)
            core_to = lax.rem(core + lax.rem(rest, 2), 2)
            fn(side_to * 16 + other * 2 + core_to)
            return carry
        lax.fori_loop(0, L - 1, body, 0)

    row, col = lax.div(ti, 4), lax.rem(ti, 4)
    core = lax.rem(li, 2)
    partner = lead_dev(li + 1 - 2 * core)

    def each_z(fn):
        for m in (2, 1, 3):
            fn(lax.rem(col + m, 4))

    def each_x(fn):
        for m in (2, 1, 3):
            fn(lax.rem(row + m, 4))

    def each_tile_far_first(fn):

        def away(m):
            return 6 + lax.div(m + 1, 2) * (1 - 2 * lax.rem(m, 2))

        def body(n, carry):
            fn(lax.rem(row + away(lax.div(n, 4)), 4) * 4 + lax.rem(col + away(lax.rem(n, 4)), 4))
            return carry
        lax.fori_loop(0, T - 1, body, 0)

    def each_tile(fn, first=1, last=T):
        def body(d, carry):
            fn(lax.rem(ti + d, T))
            return carry
        lax.fori_loop(first, last, body, 0)

    bar = pltpu.get_barrier_semaphore()
    each_lead(lambda to: pl.semaphore_signal(bar, inc=1, device_id=lead_dev(to), device_id_type=MESH))
    each_tile_far_first(lambda to: pl.semaphore_signal(bar, inc=1, device_id=tile_dev(to), device_id_type=MESH))
    for n in range(N_IN - 1):
        load(n).start()

    up = lax.rem(ti + 1, T)
    down = lax.rem(ti + T - 1, T)
    has_up = ti < T - 1
    has_down = ti > 0

    for n in range(4):
        load(n).wait()
    outer = wsrc[...].astype(F32).reshape(OWN * TAPS * GATES, 2 * HID).astype(BF)
    wt[...] = nn(a_ref[...], outer).astype(BF)
    sub = lax.broadcasted_iota(jnp.int32, (OWN, OWN), 0)
    lane = lax.broadcasted_iota(jnp.int32, (OWN, OWN), 1)
    bias_cols = [jnp.sum(jnp.where(sub == lane, bias[j:j + 1, :], 0.0), axis=1, keepdims=True) for j in range(GATES)]

    def row_parts(g):
        return [sum(shifted(g[(3 * a + b) * GR:(3 * a + b + 1) * GR], b - 1) for b in range(3)) for a in range(3)]

    own_x = []

    def frame_parts(t):
        parts = row_parts(nn(wt[:, 0:HID], frames[t]))
        for a in (0, 2):
            yx[t, a] = parts[a].astype(BF)
        own_x.append(parts[1])

    frame_parts(0)
    pl.semaphore_wait(bar, L + T - 2)

    def halo(src, dst, sem):
        send(src.at[0], dst.at[0], sem, tile_dev(up))
        send(src.at[2], dst.at[1], sem, tile_dev(down))

    halo(yx.at[0], rx.at[0], S_YX0)
    for n in range(4, N_IN - 1):
        load(n).wait()
    whp[...] = nn(wt[:, HID:], e_ref[...]).astype(BF)
    whpt[...] = nt(et_ref[...], wt[:, HID:]).astype(BF)
    def from_neighbours(r):
        return jnp.where(has_down, r[0].astype(F32), 0.0) + jnp.where(has_up, r[1].astype(F32), 0.0)

    def padded(x):
        return jnp.concatenate([x, jnp.zeros((PAD - OWN, W), F32)], 0)

    def cell(z, previous):
        z = [padded(z[j * OWN:(j + 1) * OWN] + bias_cols[j]) for j in range(GATES)]
        i_g = jax.nn.sigmoid(z[0])
        f_g = jax.nn.sigmoid(z[1])
        g_g = jnp.tanh(z[2])
        o_g = jax.nn.sigmoid(z[3])
        now = f_g * previous + i_g * g_g
        return (i_g, f_g, g_g, o_g, previous, now), (o_g * jnp.tanh(now)).astype(BF)

    def share_h(t, h):
        buf = hbuf.at[t]
        buf[li] = h
        sem = (S_H1, S_H2, S_H3)[t]
        each_lead(lambda to: send(buf.at[li], buf.at[li], sem, lead_dev(to)))

    def await_h(t):
        got(hbuf.at[t, pl.ds(0, L - 1)], (S_H1, S_H2, S_H3)[t])

    saved = []
    got(rx.at[0], S_YX0)
    z = own_x[0] + from_neighbours(rx.at[0])
    state, h = cell(z, jnp.zeros((PAD, W), F32))
    saved.append(state)
    share_h(0, h)
    for t in (1, 2):
        frame_parts(t)
        halo(yx.at[t], rx.at[t], (S_YX0, S_YX1, S_YX2)[t])
    send(cot, coth.at[0], S_COTH, tile_dev(lax.rem(ti + 2, T)))
    for t in range(3):
        fsend[:, 2 * t:2 * t + 2] = nn(et_ref[...], frames[t]).astype(BF).reshape(T, 2, PAD, W)
    for p in range(4):
        cot4[p] = cot[96 * p:96 * (p + 1), :]
    slot = lax.broadcasted_iota(jnp.int32, (16, 2, HID), 0)
    lines = jnp.sum(jnp.where(slot == idx[0], film[...], 0.0), axis=0)
    lines = jnp.concatenate([lines, jnp.zeros((6, HID), F32)], 0).T
    film_col[...] = jnp.zeros_like(film_col)
    for i in range(L):
        film_col[i, 0:OWN, :] = lines[i * OWN:(i + 1) * OWN]
    film_q[...] = lines.reshape(4, 96, 8)
    for at in (0, (T + 1) * W):
        stack[:, at:at + W] = jnp.zeros((3 * GR, W), BF)
    for at in (0, (T + 2) * W):
        cc[:, at:at + 2 * W] = jnp.zeros((3 * 96, 2 * W), BF)
    vv[96:W, :] = jnp.zeros((W - 96, T * W), BF)
    for d in range(4):
        pbuf[256 * d + 216:256 * (d + 1), :] = jnp.zeros((40, W), F32)
    scat[...] = jnp.zeros_like(scat)

    def half(x):
        return x.at[pl.ds(3 * core, 3)]

    def send_frames(to):
        send(half(fsend.at[to]), half(fblk.at[ti]), S_FR, tile_dev(to))

    zero_row = jnp.zeros((HID, W), BF)

    def head_product(a, x):
        ct = x.astype(F32).T
        total = None
        for b in range(3):
            k = 3 * a + b
            term = nn(shifted_rows(ct, -2 * (b - 1)).astype(BF), hw[k * HID:(k + 1) * HID, :])
            total = term if total is None else total + term
        return total

    for t in (1, 2):
        await_h(t - 1)
        parts = row_parts(nn(whp[...], hbuf[t - 1].reshape(CP, W)))
        for a in (0, 2):
            yh[t - 1, a] = parts[a].astype(BF)
        sem = (S_YH1, S_YH2)[t - 1]
        halo(yh.at[t - 1], rh.at[t - 1], sem)
        got(rx.at[t], (S_YX0, S_YX1, S_YX2)[t])
        base = own_x[t] + from_neighbours(rx.at[t]) + parts[1]
        got(rh.at[t - 1], sem)
        z = base + from_neighbours(rh.at[t - 1])
        state, h = cell(z, saved[-1][5])
        saved.append(state)
        share_h(t, h)
        if t == 1:
            send(cot, coth.at[1], S_COTH2, tile_dev(lax.rem(ti + T - 2, T)))
            dvt = head_product(1, cot[...])
            got(coth.at[0], S_COTH)
            dvt_ref[...] = dvt + head_product(2, jnp.where(ti >= 2, coth[0], zero_row))
    each_tile_far_first(send_frames)
    fblk[ti, pl.ds(3 * core, 3)] = fsend[ti, pl.ds(3 * core, 3)]
    each_z(lambda to: send(cot4.at[to], cotz.at[col], S_COTZ, tile_dev(row * 4 + to)))
    cotz[col] = cot4[col]
    got(coth.at[1], S_COTH2)
    dv = (dvt_ref[...] + head_product(0, jnp.where(ti < T - 2, coth[1], zero_row))).T
    dv_ref[...] = jnp.zeros_like(dv_ref)
    for i in range(L):
        dv_ref[0, i, 0:OWN, :] = dv[i * OWN:(i + 1) * OWN]
    dv_ref[1] = nn(et_ref[...], cot[...]).reshape(L, PAD, W)
    factors = []
    for i_g, f_g, g_g, o_g, previous, now in saved:
        sq = jnp.tanh(now)
        factors.append((
            o_g * (1.0 - sq * sq), g_g * i_g * (1.0 - i_g), previous * f_g * (1.0 - f_g), i_g * (1.0 - g_g * g_g),
            sq * o_g * (1.0 - o_g), f_g,
        ))

    def share_blocks(t):
        hsem = (S_HB1, S_HB2)[t]
        hb = hblk.at[t]
        hs = hbuf.at[t]
        hb[ti, core] = hs[2 * ti + core]
        each_tile_far_first(lambda to: send(hs.at[2 * to + core], hb.at[ti, core], hsem, tile_dev(to)))

    def swap_blocks(t):
        got(hblk.at[t, pl.ds(0, T - 1), 0], (S_HB1, S_HB2)[t])
        mine = hblk.at[t, :, core]
        send(mine, mine, (S_HB1C, S_HB2C)[t], partner)

    def await_blocks(t):
        got(hblk.at[t, :, 0], (S_HB1C, S_HB2C)[t])

    await_h(2)
    h_wide = hbuf[2].reshape(CP, W).astype(F32)
    columns = film_col[...].reshape(CP, 8)
    gamma = 1.0 + columns[:, 0:1]
    u = gamma * h_wide + columns[:, 1:2]
    s = jax.nn.sigmoid(u)
    du = dv_ref[0].reshape(CP, W) * s * (1.0 + u * (1.0 - s))
    dhp[0] = (dv_ref[1].reshape(CP, W) + gamma * du).astype(BF).reshape(L, PAD, W)

    def share_dh(n):
        sem = (S_DH3, S_DH2, S_DH1)[n]
        src = dhp.at[n]
        dst = dhr.at[n]
        each_lead(lambda to: send(src.at[to], dst.at[li], sem, lead_dev(to)))
        dst[li] = src[li]

    def await_dh(n):
        got(dhr.at[n, pl.ds(0, L - 1)], (S_DH3, S_DH2, S_DH1)[n])
        return jnp.sum(dhr[n].astype(F32), axis=0)

    share_dh(0)
    h8[...] = nn(e_ref[...], hbuf[2].reshape(CP, W)).astype(BF).reshape(8, 48, W)
    each_tile_far_first(lambda to: send(h8.at[2 * lax.div(to, 4) + core], hq.at[ti, core], S_HQ, tile_dev(to)))
    hq[ti, core] = h8[2 * row + core]
    got(cotz.at[pl.ds(0, 3)], S_COTZ)
    each_x(lambda to: send(cotz, cotb.at[pl.ds(4 * row, 4)], S_COTX, tile_dev(to * 4 + col)))
    cotb[pl.ds(4 * row, 4)] = cotz[...]
    st_send[...] = jnp.zeros_like(st_send)
    for n, field in enumerate((du * h_wide, du)):
        for i in range(L):
            flat[i * OWN:(i + 1) * OWN, :] = field[i * PAD:i * PAD + OWN]
        line = jnp.sum(flat[...].T, axis=0, keepdims=True)
        for q in range(3):
            st_send[3 * n + q:3 * n + q + 1, :] = line[:, 128 * q:128 * (q + 1)]
    each_tile_far_first(lambda to: send(st_send, st_tile.at[ti], S_ST, tile_dev(to)))
    st_tile[ti] = st_send[...]
    got(fblk.at[pl.ds(0, T - 1), pl.ds(0, 3)], S_FR)
    fr_mine = fblk.at[:, pl.ds(3 * core, 3)]
    send(fr_mine, fr_mine, S_FRC, partner)

    bias_sum = jnp.zeros((GR, W), F32)
    dc = jnp.zeros((PAD, W), F32)

    def gate_grads(n, dh, dc):
        to_c, to_i, to_f, to_g, to_o, f_g = factors[2 - n]
        dc = dc + dh * to_c
        dz = jnp.concatenate([x[0:OWN] for x in (dc * to_i, dc * to_f, dc * to_g, dh * to_o)], 0)
        src = dz_send.at[n]
        dst = dzbuf.at[n]
        src[...] = dz.astype(BF)
        dst[ti] = src[...]
        if n < 2:
            send(src, dznear.at[n, 0], (S_DZN2, S_DZN1)[n], tile_dev(up))
            send(src, dznear.at[n, 1], (S_DZN2, S_DZN1)[n], tile_dev(down))
        else:
            each_tile_far_first(lambda to: send(src, dst.at[ti], S_DZ0, tile_dev(to)))
        return dz, dc * f_g

    def await_near(n):
        got(dznear.at[n], (S_DZN2, S_DZN1)[n])

    def share_z(n):
        each_z(lambda to: send(dz_send.at[n], dzbuf.at[n, ti], (S_DZZ2, S_DZZ1)[n], tile_dev(row * 4 + to)))

    def share_x(n):
        got(dzbuf.at[n, pl.ds(0, 3)], (S_DZZ2, S_DZZ1)[n])
        mine = dzbuf.at[n, pl.ds(4 * row, 4)]
        each_x(lambda to: send(mine, mine, (S_DZX2, S_DZX1)[n], tile_dev(to * 4 + col)))

    def await_x(n):
        got(dzbuf.at[n, pl.ds(0, 12)], (S_DZX2, S_DZX1)[n])

    def back(n):
        zero = jnp.zeros((GR, W), F32)

        def stacked(x):
            return [shifted(x, 1 - b).astype(BF) for b in range(3)]

        await_near(n)
        above = stacked(jnp.where(has_up, dznear[n, 1].astype(F32), zero))
        below = stacked(jnp.where(has_down, dznear[n, 0].astype(F32), zero))
        whole = nn(whpt[...], jnp.concatenate(above + stacked(dz_send[n].astype(F32)) + below, 0))
        dhp[n + 1] = whole.astype(BF).reshape(L, PAD, W)

    def weight_part(n):
        t = 2 - n
        src = dzbuf.at[n]

        def body(r, carry):
            block = src[r].astype(F32)
            for b in range(3):
                stack[b * GR:(b + 1) * GR, pl.ds(pl.multiple_of((r + 1) * W, W), W)] = shifted(block, 1 - b).astype(BF)
            at = pl.multiple_of(r * W, W)
            scat[0:2 * PAD, pl.ds(at, W)] = fblk[r, 2 * t:2 * t + 2].reshape(2 * PAD, W)
            if t > 0:
                scat[2 * PAD:4 * PAD, pl.ds(at, W)] = hblk[t - 1, r].reshape(2 * PAD, W)
            return carry

        lax.fori_loop(0, T, body, 0, unroll=8)
        return jnp.concatenate([nt(stack[:, (2 - a) * W:(2 - a + T) * W], scat[...]) for a in range(3)], 0).T

    def share_weights(n, x):
        y = nn((x * (1.0 / 256.0)).astype(BF), pack[...]).astype(BF)
        wsend[n] = (nn(rsel[0], y[:, :256]) + nn(rsel[1], y[:, 256:])).astype(BF)
        src = wsend.at[n]
        dst = wrecv.at[n]
        dst[ti] = src[...]
        if n == 0:
            each_z(lambda to: send(src, dst.at[ti], S_WHZ, tile_dev(row * 4 + to)))
        else:
            send(src, dst.at[ti], S_WFA, tile_dev(row * 4 + lax.rem(col + 2, 4)))
            for mx in (2, 1, 3, 0):
                for mz in (1, 3, 0) if mx else (1, 3):
                    to = lax.rem(row + mx, 4) * 4 + lax.rem(col + mz, 4)
                    send(src, dst.at[ti], S_WF, tile_dev(to))

    def forward_weights():
        opposite = row * 4 + lax.rem(col + 2, 4)
        got(wrecv.at[1, 0], S_WFA)
        mine = wrecv.at[1, opposite]
        each_x(lambda to: send(mine, mine, S_WFB, tile_dev(to * 4 + col)))

    def share_weights_x():
        got(wrecv.at[0, pl.ds(0, 3)], S_WHZ)
        mine = wrecv.at[0, pl.ds(4 * row, 4)]
        each_x(lambda to: send(mine, mine, S_WHX, tile_dev(to * 4 + col)))

    def finish_weights(n):
        if n == 0:
            got(wrecv.at[0, pl.ds(0, 12)], S_WHX)
        else:
            got(wrecv.at[1, pl.ds(0, 11)], S_WF)
            got(wrecv.at[1, pl.ds(0, 3)], S_WFB)
        for s_ in range(T):
            block = wrecv[n, s_].astype(F32)
            xf[24 * s_:24 * (s_ + 1), 0:256] = block[0:24]
            xf[24 * s_:24 * (s_ + 1), 256:512] = block[24:48]
        first = HID * (1 - n)
        wg_out[:, first:first + HID] = nt(unpack[...], xf[...].astype(BF)).astype(BF)

    dz, dc = gate_grads(0, await_dh(0), dc)
    bias_sum = bias_sum + dz
    back(0)
    share_dh(1)
    share_z(0)
    got(hq.at[pl.ds(0, T - 1), 0], S_HQ)
    hq_mine = hq.at[:, core]
    send(hq_mine, hq_mine, S_HQC, partner)
    share_blocks(1)
    share_blocks(0)
    share_x(0)

    got(st_tile.at[pl.ds(0, T - 1)], S_ST)
    stl_send[0:8, :] = jnp.sum(st_tile[...], axis=0)
    lane = lax.broadcasted_iota(jnp.int32, (8, W), 1)
    stl_send[8:16, :] = jnp.where(lane == idx[0], 1.0, 0.0)
    each_lead(lambda to: send(stl_send, stl.at[li], S_STL, lead_dev(to)))
    stl[li] = stl_send[...]

    got(hq.at[:, 0], S_HQC)
    got(cotb.at[pl.ds(0, 12)], S_COTX)
    gamma_q = 1.0 + film_q[row, :, 0:1]
    beta_q = film_q[row, :, 1:2]

    def head_rows(r, carry):
        block = cotb[r].astype(F32)
        at = pl.multiple_of((r + 2) * W, W)
        for b in range(3):
            cc[96 * b:96 * (b + 1), pl.ds(at, W)] = shifted(block, 2 * (1 - b)).astype(BF)
        uq = gamma_q * hq[r].reshape(96, W).astype(F32) + beta_q
        vv[0:96, pl.ds(pl.multiple_of(r * W, W), W)] = (uq * jax.nn.sigmoid(uq)).astype(BF)
        return carry

    lax.fori_loop(0, T, head_rows, 0)
    for a in range(3):
        first = (4 - 2 * a) * W
        part = nt(cc[:, first:first + T * W], vv[...])
        for b in range(3):
            k = 3 * a + b
            for d in range(4):
                pbuf[d * 256 + k * 24:d * 256 + (k + 1) * 24, :] = part[b * 96 + d * 24:b * 96 + (d + 1) * 24]
    psend[...] = pbuf[...].astype(BF).reshape(L, 32, W)
    prec[li] = psend[8 * lax.rem(li, 4) + lax.div(li, 4)]

    dz, dc = gate_grads(1, await_dh(1), dc)
    bias_sum = bias_sum + dz
    back(1)
    share_dh(2)
    share_z(1)
    each_lead(lambda to: send(psend.at[8 * lax.rem(to, 4) + lax.div(to, 4)], prec.at[li], S_PR, lead_dev(to)))
    swap_blocks(1)
    swap_blocks(0)
    share_x(1)
    await_x(0)
    got(fblk.at[:, pl.ds(0, 3)], S_FRC)
    await_blocks(1)
    grads = weight_part(0)

    dz, dc = gate_grads(2, await_dh(2), dc)

    got(prec.at[pl.ds(0, L - 1)], S_PR)
    psum[...] = (jnp.sum(prec[...].astype(F32), axis=0) * (1.0 / 256.0)).astype(BF)
    owner = col * 4 + lax.rem(li, 4)
    gathers = lax.rem(li, 4) == col

    @pl.when(owner != ti)
    def _():
        send(psum, ptile.at[row], S_PT, tile_dev(owner))

    @pl.when(owner == ti)
    def _():
        ptile[row] = psum[...]

    await_x(1)
    await_blocks(0)
    grads = grads + weight_part(1)
    share_weights(0, grads[2 * PAD:4 * PAD])
    bias_sum = bias_sum + dz
    column = jnp.sum(bias_sum, axis=1, keepdims=True)
    lane = lax.broadcasted_iota(jnp.int32, (GR, W), 1)
    sub = lax.broadcasted_iota(jnp.int32, (GR, W), 0)
    line = jnp.sum(jnp.where(lane == sub, column, 0.0), axis=0, keepdims=True)
    bi_send[...] = jnp.broadcast_to(line, (8, W))
    each_tile_far_first(lambda to: send(bi_send, bi.at[ti], S_BI, tile_dev(to)))
    bi[ti] = bi_send[...]

    @pl.when(gathers)
    def _():
        @pl.when(owner == ti)
        def _():
            got(ptile.at[pl.ds(0, 3)], S_PT)

        @pl.when(owner != ti)
        def _():
            got(ptile, S_PT)

        each_lead(lambda to: send(ptile, plead.at[lax.div(li, 4)], S_PL, lead_dev(to)))
        plead[lax.div(li, 4)] = ptile[...]

    got(dzbuf.at[2, pl.ds(0, T - 1)], S_DZ0)
    share_weights_x()
    grads0 = weight_part(2)
    share_weights(1, grads[0:2 * PAD] + grads0[0:2 * PAD])
    forward_weights()

    got(stl.at[pl.ds(0, L - 1)], S_STL)

    def table(l, acc):
        block = stl[l]
        return tuple(acc[m] + block[8:16, m:m + 1] * block[0:8, :] for m in range(16))

    acc = lax.fori_loop(0, L, table, tuple(jnp.zeros((8, W), F32) for _ in range(16)))
    for m in range(16):
        rows6 = acc[m] * (1.0 / 256.0)
        for n in range(2):
            for q in range(3):
                fg_out[m, n:n + 1, W * q:W * (q + 1)] = rows6[3 * n + q:3 * n + q + 1]
    got(bi.at[pl.ds(0, T - 1)], S_BI)
    line = jnp.sum(bi[...], axis=0) * (1.0 / 256.0)
    for j in range(GATES):
        bg_out[j:j + 1, :] = line[0:1, j * OWN:(j + 1) * OWN]
    finish_weights(0)

    @pl.when(gathers)
    def _():
        got(plead.at[pl.ds(0, 7)], S_PL)

    @pl.when(jnp.logical_not(gathers))
    def _():
        got(plead, S_PL)

    wide = jnp.concatenate([plead[:, q].reshape(256, W) for q in range(4)], 1)
    hg_out[...] = nn(wide, spread[...])[0:TAPS * 24].astype(BF)
    finish_weights(1)

    for t in range(3):
        sent(rx.at[t], (S_YX0, S_YX1, S_YX2)[t])
        sent(hbuf.at[t, pl.ds(0, L - 1)], (S_H1, S_H2, S_H3)[t])
        sent(dhr.at[t, pl.ds(0, L - 1)], (S_DH3, S_DH2, S_DH1)[t])
    for t in range(2):
        sent(rh.at[t], (S_YH1, S_YH2)[t])
        sent(dznear.at[t], (S_DZN2, S_DZN1)[t])
        sent(dzbuf.at[t, pl.ds(0, 3)], (S_DZZ2, S_DZZ1)[t])
        sent(dzbuf.at[t, pl.ds(0, 12)], (S_DZX2, S_DZX1)[t])
        sent(hblk.at[t, pl.ds(0, T - 1), 0], (S_HB1, S_HB2)[t])
        sent(hblk.at[t, :, 0], (S_HB1C, S_HB2C)[t])
    sent(dzbuf.at[2, pl.ds(0, T - 1)], S_DZ0)
    sent(wrecv.at[0, pl.ds(0, 3)], S_WHZ)
    sent(wrecv.at[0, pl.ds(0, 12)], S_WHX)
    sent(wrecv.at[1, pl.ds(0, 11)], S_WF)
    sent(wrecv.at[1, 0], S_WFA)
    sent(wrecv.at[1, pl.ds(0, 3)], S_WFB)
    sent(coth.at[0], S_COTH)
    sent(coth.at[1], S_COTH2)
    sent(cotz.at[pl.ds(0, 3)], S_COTZ)
    sent(cotb.at[pl.ds(0, 12)], S_COTX)
    sent(fblk.at[pl.ds(0, T - 1), pl.ds(0, 3)], S_FR)
    sent(fblk.at[:, pl.ds(0, 3)], S_FRC)
    sent(hq.at[pl.ds(0, T - 1), 0], S_HQ)
    sent(hq.at[:, 0], S_HQC)
    sent(st_tile.at[pl.ds(0, T - 1)], S_ST)
    sent(stl.at[pl.ds(0, L - 1)], S_STL)
    sent(bi.at[pl.ds(0, T - 1)], S_BI)
    sent(prec.at[pl.ds(0, L - 1)], S_PR)

    @pl.when(owner != ti)
    def _():
        sent(psum, S_PT)

    @pl.when(gathers)
    def _():
        def body(d, carry):
            sent(ptile, S_PL)
            return carry
        lax.fori_loop(1, L, body, 0)


def finish(wg, bg, hg, fg, wg_out, bg_out, hg_out, fg_out):
    wg_out[...] = wg[...].astype(F32).reshape(OWN, TAPS, GATES, 2 * HID).astype(BF)
    bg_out[...] = bg[...]
    hg_out[...] = hg[...]
    fg_out[...] = fg[...]


def shards(frames, enc_weight, enc_bias, head_weight, film_table, lead_index, cotangent):
    a, pack, unpack, e, et, spread, rsel = [jnp.asarray(x) for x in one_hots()]
    wsrc = enc_weight.transpose(0, 2, 1, 3)
    hw = head_weight.transpose(1, 0, 2).reshape(TAPS * HID, HID)
    vm = pltpu.VMEM
    inputs = (
        wsrc, a, frames.reshape(3, HID, W), enc_bias.T, e, et, film_table, cotangent.reshape(HID, W), hw, pack, rsel,
        unpack, spread,
    )
    outs = pl.pallas_call(
        kernel,
        out_shape=(
            jax.ShapeDtypeStruct((OWN * TAPS * GATES, 2 * HID), BF),
            jax.ShapeDtypeStruct((GATES, OWN), F32),
            jax.ShapeDtypeStruct((TAPS * 24, HID), BF),
            jax.ShapeDtypeStruct((16, 2, HID), F32),
        ),
        in_specs=[pl.BlockSpec(memory_space=pl.ANY)] * (N_IN - 1) + [pl.BlockSpec(memory_space=pltpu.SMEM)],
        out_specs=(pl.BlockSpec(memory_space=vm),) * 4,
        scratch_shapes=[vm(x.shape, x.dtype) for x in inputs] + [
            vm((TAPS * GR, 2 * HID), BF),
            vm((TAPS * GR, CP), BF),
            vm((CP, TAPS * GR), BF),
            vm((W, HID), F32),
            vm((3, 3, GR, W), BF),
            vm((2, 3, GR, W), BF),
            vm((3, 2, GR, W), BF),
            vm((2, 2, GR, W), BF),
            vm((3, L, PAD, W), BF),
            vm((2, HID, W), BF),
            vm((4, 96, W), BF),
            vm((4, 96, W), BF),
            vm((T, 96, W), BF),
            vm((T, 6, PAD, W), BF),
            vm((T, 6, PAD, W), BF),
            vm((2, T, 2, PAD, W), BF),
            vm((2, L, PAD, W), F32),
            vm((3, L, PAD, W), BF),
            vm((3, L, PAD, W), BF),
            vm((8, 48, W), BF),
            vm((T, 2, 48, W), BF),
            vm((8, W), F32),
            vm((T, 8, W), F32),
            vm((16, W), F32),
            vm((L, 16, W), F32),
            vm((3, GR, W), BF),
            vm((2, 2, GR, W), BF),
            vm((3, T, GR, W), BF),
            vm((8, W), F32),
            vm((T, 8, W), F32),
            vm((3 * GR, (T + 2) * W), BF),
            vm((4 * PAD, T * W), BF),
            vm((2, 48, 256), BF),
            vm((2, T, 48, 256), BF),
            vm((HID, 512), F32),
            vm((3 * 96, (T + 4) * W), BF),
            vm((W, T * W), BF),
            vm((L * 32, W), F32),
            vm((L, 32, W), BF),
            vm((L, 32, W), BF),
            vm((32, W), BF),
            vm((4, 32, W), BF),
            vm((8, 4, 32, W), BF),
            vm((L, PAD, 8), F32),
            vm((4, 96, 8), F32),
            vm((HID, W), F32),
            pltpu.SemaphoreType.DMA((NSEM,)),
            pltpu.SemaphoreType.DMA((NSEM,)),
            pltpu.SemaphoreType.DMA((N_IN - 1,)),
        ],
        compiler_params=pltpu.CompilerParams(
            collective_id=0, has_side_effects=True, vmem_limit_bytes=24 * 2**20
        ),
    )(*inputs, lead_index)
    wg, bg, hg, fg = pl.pallas_call(
        finish,
        out_shape=(
            jax.ShapeDtypeStruct((OWN, TAPS, GATES, 2 * HID), BF),
            jax.ShapeDtypeStruct((GATES, OWN), F32),
            jax.ShapeDtypeStruct((TAPS * 24, HID), BF),
            jax.ShapeDtypeStruct((16, 2, HID), F32),
        ),
        in_specs=[pl.BlockSpec(memory_space=vm)] * 4,
        out_specs=(pl.BlockSpec(memory_space=vm),) * 4,
    )(*outs)
    return wg.transpose(0, 2, 1, 3), bg.T, hg.reshape(TAPS, 24, HID).transpose(1, 0, 2), fg


def solution(mesh):
    in_specs = (
        P(None, None, "tile", None),
        P("lead", None, None, None),
        P("lead", None),
        P(),
        P(),
        P("lead"),
        P("lead", None, "tile", None),
    )
    out_specs = (P("lead", None, None, None), P("lead", None), P("tile", None, None), P())
    return jax.shard_map(shards, mesh=mesh, in_specs=in_specs, out_specs=out_specs, check_vma=False)
```

```python
import numpy as np
import jax
import jax.numpy as jnp
import ml_dtypes
from jax import lax
from jax.experimental import pallas as pl
from jax.experimental.pallas import tpu as pltpu
from jax.sharding import PartitionSpec as P

MESH = pl.DeviceIdType.MESH
BF = jnp.bfloat16
F32 = jnp.float32
L, T, HID, W = 32, 16, 384, 128
OWN, PAD, GATES, TAPS = 12, 16, 4, 9
GR = GATES * OWN
CP = L * PAD


def one_hots():
    a = np.zeros((TAPS * GR, OWN * TAPS * GATES), np.float32)
    pack = np.zeros((TAPS * GR, 512), np.float32)
    unpack = np.zeros((OWN * TAPS * GATES, 512), np.float32)
    for k in range(TAPS):
        for j in range(GATES):
            for o in range(OWN):
                inner = k * GR + j * OWN + o
                outer = (o * TAPS + k) * GATES + j
                column = inner + (0 if k < 5 else 16)
                a[inner, outer] = 1
                pack[inner, column] = 1
                unpack[outer, column] = 1
    e = np.zeros((HID, CP), np.float32)
    for i in range(L):
        for o in range(OWN):
            e[i * OWN + o, i * PAD + o] = 1
    spread = np.zeros((512, HID), np.float32)
    for q in range(4):
        for c in range(96):
            spread[128 * q + c, 96 * q + c] = 1
    rows = np.zeros((2, 48, 32), np.float32)
    for half in range(2):
        for c in range(24):
            rows[half, 24 * half + c, (c // OWN) * PAD + c % OWN] = 1
    return [x.astype(ml_dtypes.bfloat16) for x in (a, pack, unpack, e, e.T.copy(), spread, rows)]


def nn(a, b):
    return lax.dot_general(a, b, (((1,), (0,)), ((), ())), preferred_element_type=F32)


def nt(a, b):
    return lax.dot_general(a, b, (((1,), (1,)), ((), ())), preferred_element_type=F32)


def shifted(x, s):
    if s == 0:
        return x
    lane = lax.broadcasted_iota(jnp.int32, x.shape, 1)
    keep = lane < W - s if s > 0 else lane >= -s
    return jnp.where(keep, pltpu.roll(x, (-s) % W, 1), 0.0)


def shifted_rows(x, s):
    if s == 0:
        return x
    row = lax.broadcasted_iota(jnp.int32, x.shape, 0)
    keep = row < W - s if s > 0 else row >= -s
    return jnp.where(keep, pltpu.roll(x, (-s) % W, 0), 0.0)


(S_YX0, S_YX1, S_YX2, S_H1, S_H2, S_H3, S_YH1, S_YH2, S_COTH, S_COTZ, S_COTX, S_FR, S_FRC, S_HB1, S_HB2, S_HB1C, S_HB2C,
 S_DH3, S_DH2, S_DH1, S_HQ, S_HQC, S_ST, S_STL, S_DZN2, S_DZN1, S_DZ0, S_DZZ2, S_DZZ1, S_DZX2, S_DZX1, S_BI, S_WHZ, S_WHX, S_WF,
 S_WFA, S_WFB, S_PR, S_PT, S_PL, S_COTH2, NSEM) = range(42)


N_IN = 14


def kernel(*refs):
    inputs, (wg_out, bg_out, hg_out, fg_out), refs = refs[:N_IN], refs[N_IN:N_IN + 4], refs[N_IN + 4:]
    held, refs = refs[:N_IN - 1], refs[N_IN - 1:]
    idx = inputs[N_IN - 1]
    (
        wt, whp, whpt, dvt_ref, yx, yh, rx, rh, hbuf, coth, cot4, cotz, cotb, fsend, fblk, hblk, dv_ref, dhp, dhr,
        h8, hq, st_send, st_tile, stl_send, stl, dz_send, dznear, dzbuf, bi_send, bi, stack, scat,
        wsend, wrecv, xf, cc, vv, pbuf, psend, prec, psum, ptile, plead, film_col, film_q, flat, ssem, rsem, lsem,
    ) = refs
    wsrc, a_ref, frames, bias, e_ref, et_ref, film, cot, hw, pack, rsel, unpack, spread = held
    li = lax.axis_index("lead")
    ti = lax.axis_index("tile")

    def lead_dev(to):
        return (to, ti)

    def tile_dev(to):
        return (li, to)

    def send(src, dst, sem, dev):
        pltpu.make_async_remote_copy(
            src_ref=src, dst_ref=dst, send_sem=ssem.at[sem], recv_sem=rsem.at[sem], device_id=dev, device_id_type=MESH
        ).start()

    def got(ref, sem):
        pltpu.make_async_copy(ref, ref, rsem.at[sem]).wait()

    def sent(ref, sem):
        pltpu.make_async_copy(ref, ref, ssem.at[sem]).wait()

    def load(n):
        return pltpu.make_async_copy(inputs[n], held[n], lsem.at[n])

    def each_lead(fn):
        ring, side = lax.rem(lax.div(li, 2), 8), lax.div(li, 16)

        def body(n, carry):
            m = lax.div(n, 4)
            step = lax.div(m + 1, 2) * (1 - 2 * lax.rem(m, 2))
            other = lax.rem(ring + 12 + step, 8)
            rest = 3 - lax.rem(n, 4)
            side_to = lax.rem(side + lax.div(rest, 2), 2)
            core_to = lax.rem(core + lax.rem(rest, 2), 2)
            fn(side_to * 16 + other * 2 + core_to)
            return carry
        lax.fori_loop(0, L - 1, body, 0)

    row, col = lax.div(ti, 4), lax.rem(ti, 4)
    core = lax.rem(li, 2)
    partner = lead_dev(li + 1 - 2 * core)

    def each_z(fn):
        for m in (2, 1, 3):
            fn(lax.rem(col + m, 4))

    def each_x(fn):
        for m in (2, 1, 3):
            fn(lax.rem(row + m, 4))

    def each_tile_far_first(fn):

        def away(m):
            return 6 + lax.div(m + 1, 2) * (1 - 2 * lax.rem(m, 2))

        def body(n, carry):
            fn(lax.rem(row + away(lax.div(n, 4)), 4) * 4 + lax.rem(col + away(lax.rem(n, 4)), 4))
            return carry
        lax.fori_loop(0, T - 1, body, 0)

    def each_tile(fn, first=1, last=T):
        def body(d, carry):
            fn(lax.rem(ti + d, T))
            return carry
        lax.fori_loop(first, last, body, 0)

    bar = pltpu.get_barrier_semaphore()
    each_lead(lambda to: pl.semaphore_signal(bar, inc=1, device_id=lead_dev(to), device_id_type=MESH))
    each_tile_far_first(lambda to: pl.semaphore_signal(bar, inc=1, device_id=tile_dev(to), device_id_type=MESH))
    for n in range(N_IN - 1):
        load(n).start()

    up = lax.rem(ti + 1, T)
    down = lax.rem(ti + T - 1, T)
    has_up = ti < T - 1
    has_down = ti > 0

    for n in range(4):
        load(n).wait()
    outer = wsrc[...].astype(F32).reshape(OWN * TAPS * GATES, 2 * HID).astype(BF)
    wt[...] = nn(a_ref[...], outer).astype(BF)
    sub = lax.broadcasted_iota(jnp.int32, (OWN, OWN), 0)
    lane = lax.broadcasted_iota(jnp.int32, (OWN, OWN), 1)
    bias_cols = [jnp.sum(jnp.where(sub == lane, bias[j:j + 1, :], 0.0), axis=1, keepdims=True) for j in range(GATES)]

    def row_parts(g):
        return [sum(shifted(g[(3 * a + b) * GR:(3 * a + b + 1) * GR], b - 1) for b in range(3)) for a in range(3)]

    own_x = []

    def frame_parts(t):
        parts = row_parts(nn(wt[:, 0:HID], frames[t]))
        for a in (0, 2):
            yx[t, a] = parts[a].astype(BF)
        own_x.append(parts[1])

    frame_parts(0)
    pl.semaphore_wait(bar, L + T - 2)

    def halo(src, dst, sem):
        send(src.at[0], dst.at[0], sem, tile_dev(up))
        send(src.at[2], dst.at[1], sem, tile_dev(down))

    halo(yx.at[0], rx.at[0], S_YX0)
    for n in range(4, N_IN - 1):
        load(n).wait()
    whp[...] = nn(wt[:, HID:], e_ref[...]).astype(BF)
    whpt[...] = nt(et_ref[...], wt[:, HID:]).astype(BF)
    def from_neighbours(r):
        return jnp.where(has_down, r[0].astype(F32), 0.0) + jnp.where(has_up, r[1].astype(F32), 0.0)

    def padded(x):
        return jnp.concatenate([x, jnp.zeros((PAD - OWN, W), F32)], 0)

    def cell(z, previous):
        z = [padded(z[j * OWN:(j + 1) * OWN] + bias_cols[j]) for j in range(GATES)]
        i_g = jax.nn.sigmoid(z[0])
        f_g = jax.nn.sigmoid(z[1])
        g_g = jnp.tanh(z[2])
        o_g = jax.nn.sigmoid(z[3])
        now = f_g * previous + i_g * g_g
        return (i_g, f_g, g_g, o_g, previous, now), (o_g * jnp.tanh(now)).astype(BF)

    def share_h(t, h):
        buf = hbuf.at[t]
        buf[li] = h
        sem = (S_H1, S_H2, S_H3)[t]
        each_lead(lambda to: send(buf.at[li], buf.at[li], sem, lead_dev(to)))

    def await_h(t):
        got(hbuf.at[t, pl.ds(0, L - 1)], (S_H1, S_H2, S_H3)[t])

    saved = []
    got(rx.at[0], S_YX0)
    z = own_x[0] + from_neighbours(rx.at[0])
    state, h = cell(z, jnp.zeros((PAD, W), F32))
    saved.append(state)
    share_h(0, h)
    for t in (1, 2):
        frame_parts(t)
        halo(yx.at[t], rx.at[t], (S_YX0, S_YX1, S_YX2)[t])
    send(cot, coth.at[0], S_COTH, tile_dev(lax.rem(ti + 2, T)))
    for t in range(3):
        fsend[:, 2 * t:2 * t + 2] = nn(et_ref[...], frames[t]).astype(BF).reshape(T, 2, PAD, W)
    for p in range(4):
        cot4[p] = cot[96 * p:96 * (p + 1), :]
    slot = lax.broadcasted_iota(jnp.int32, (16, 2, HID), 0)
    lines = jnp.sum(jnp.where(slot == idx[0], film[...], 0.0), axis=0)
    lines = jnp.concatenate([lines, jnp.zeros((6, HID), F32)], 0).T
    film_col[...] = jnp.zeros_like(film_col)
    for i in range(L):
        film_col[i, 0:OWN, :] = lines[i * OWN:(i + 1) * OWN]
    film_q[...] = lines.reshape(4, 96, 8)
    for at in (0, (T + 1) * W):
        stack[:, at:at + W] = jnp.zeros((3 * GR, W), BF)
    for at in (0, (T + 2) * W):
        cc[:, at:at + 2 * W] = jnp.zeros((3 * 96, 2 * W), BF)
    vv[96:W, :] = jnp.zeros((W - 96, T * W), BF)
    for d in range(4):
        pbuf[256 * d + 216:256 * (d + 1), :] = jnp.zeros((40, W), F32)
    scat[...] = jnp.zeros_like(scat)

    def half(x):
        return x.at[pl.ds(3 * core, 3)]

    def send_frames(to):
        send(half(fsend.at[to]), half(fblk.at[ti]), S_FR, tile_dev(to))

    zero_row = jnp.zeros((HID, W), BF)

    def head_product(a, x):
        ct = x.astype(F32).T
        total = None
        for b in range(3):
            k = 3 * a + b
            term = nn(shifted_rows(ct, -2 * (b - 1)).astype(BF), hw[k * HID:(k + 1) * HID, :])
            total = term if total is None else total + term
        return total

    for t in (1, 2):
        await_h(t - 1)
        parts = row_parts(nn(whp[...], hbuf[t - 1].reshape(CP, W)))
        for a in (0, 2):
            yh[t - 1, a] = parts[a].astype(BF)
        sem = (S_YH1, S_YH2)[t - 1]
        halo(yh.at[t - 1], rh.at[t - 1], sem)
        got(rx.at[t], (S_YX0, S_YX1, S_YX2)[t])
        base = own_x[t] + from_neighbours(rx.at[t]) + parts[1]
        got(rh.at[t - 1], sem)
        z = base + from_neighbours(rh.at[t - 1])
        state, h = cell(z, saved[-1][5])
        saved.append(state)
        share_h(t, h)
        if t == 1:
            send(cot, coth.at[1], S_COTH2, tile_dev(lax.rem(ti + T - 2, T)))
            dvt = head_product(1, cot[...])
            got(coth.at[0], S_COTH)
            dvt_ref[...] = dvt + head_product(2, jnp.where(ti >= 2, coth[0], zero_row))
    each_tile_far_first(send_frames)
    fblk[ti, pl.ds(3 * core, 3)] = fsend[ti, pl.ds(3 * core, 3)]
    each_z(lambda to: send(cot4.at[to], cotz.at[col], S_COTZ, tile_dev(row * 4 + to)))
    cotz[col] = cot4[col]
    got(coth.at[1], S_COTH2)
    dv = (dvt_ref[...] + head_product(0, jnp.where(ti < T - 2, coth[1], zero_row))).T
    dv_ref[...] = jnp.zeros_like(dv_ref)
    for i in range(L):
        dv_ref[0, i, 0:OWN, :] = dv[i * OWN:(i + 1) * OWN]
    dv_ref[1] = nn(et_ref[...], cot[...]).reshape(L, PAD, W)
    factors = []
    for i_g, f_g, g_g, o_g, previous, now in saved:
        sq = jnp.tanh(now)
        factors.append((
            o_g * (1.0 - sq * sq), g_g * i_g * (1.0 - i_g), previous * f_g * (1.0 - f_g), i_g * (1.0 - g_g * g_g),
            sq * o_g * (1.0 - o_g), f_g,
        ))

    def share_blocks(t):
        hsem = (S_HB1, S_HB2)[t]
        hb = hblk.at[t]
        hs = hbuf.at[t]
        hb[ti, core] = hs[2 * ti + core]
        each_tile_far_first(lambda to: send(hs.at[2 * to + core], hb.at[ti, core], hsem, tile_dev(to)))

    def swap_blocks(t):
        got(hblk.at[t, pl.ds(0, T - 1), 0], (S_HB1, S_HB2)[t])
        mine = hblk.at[t, :, core]
        send(mine, mine, (S_HB1C, S_HB2C)[t], partner)

    def await_blocks(t):
        got(hblk.at[t, :, 0], (S_HB1C, S_HB2C)[t])

    await_h(2)
    h_wide = hbuf[2].reshape(CP, W).astype(F32)
    columns = film_col[...].reshape(CP, 8)
    gamma = 1.0 + columns[:, 0:1]
    u = gamma * h_wide + columns[:, 1:2]
    s = jax.nn.sigmoid(u)
    du = dv_ref[0].reshape(CP, W) * s * (1.0 + u * (1.0 - s))
    dhp[0] = (dv_ref[1].reshape(CP, W) + gamma * du).astype(BF).reshape(L, PAD, W)

    def share_dh(n):
        sem = (S_DH3, S_DH2, S_DH1)[n]
        src = dhp.at[n]
        dst = dhr.at[n]
        each_lead(lambda to: send(src.at[to], dst.at[li], sem, lead_dev(to)))
        dst[li] = src[li]

    def await_dh(n):
        got(dhr.at[n, pl.ds(0, L - 1)], (S_DH3, S_DH2, S_DH1)[n])
        return jnp.sum(dhr[n].astype(F32), axis=0)

    share_dh(0)
    h8[...] = nn(e_ref[...], hbuf[2].reshape(CP, W)).astype(BF).reshape(8, 48, W)
    each_tile_far_first(lambda to: send(h8.at[2 * lax.div(to, 4) + core], hq.at[ti, core], S_HQ, tile_dev(to)))
    hq[ti, core] = h8[2 * row + core]
    got(cotz.at[pl.ds(0, 3)], S_COTZ)
    each_x(lambda to: send(cotz, cotb.at[pl.ds(4 * row, 4)], S_COTX, tile_dev(to * 4 + col)))
    cotb[pl.ds(4 * row, 4)] = cotz[...]
    st_send[...] = jnp.zeros_like(st_send)
    for n, field in enumerate((du * h_wide, du)):
        for i in range(L):
            flat[i * OWN:(i + 1) * OWN, :] = field[i * PAD:i * PAD + OWN]
        line = jnp.sum(flat[...].T, axis=0, keepdims=True)
        for q in range(3):
            st_send[3 * n + q:3 * n + q + 1, :] = line[:, 128 * q:128 * (q + 1)]
    each_tile_far_first(lambda to: send(st_send, st_tile.at[ti], S_ST, tile_dev(to)))
    st_tile[ti] = st_send[...]
    got(fblk.at[pl.ds(0, T - 1), pl.ds(0, 3)], S_FR)
    fr_mine = fblk.at[:, pl.ds(3 * core, 3)]
    send(fr_mine, fr_mine, S_FRC, partner)

    bias_sum = jnp.zeros((GR, W), F32)
    dc = jnp.zeros((PAD, W), F32)

    def gate_grads(n, dh, dc):
        to_c, to_i, to_f, to_g, to_o, f_g = factors[2 - n]
        dc = dc + dh * to_c
        dz = jnp.concatenate([x[0:OWN] for x in (dc * to_i, dc * to_f, dc * to_g, dh * to_o)], 0)
        src = dz_send.at[n]
        dst = dzbuf.at[n]
        src[...] = dz.astype(BF)
        dst[ti] = src[...]
        if n < 2:
            send(src, dznear.at[n, 0], (S_DZN2, S_DZN1)[n], tile_dev(up))
            send(src, dznear.at[n, 1], (S_DZN2, S_DZN1)[n], tile_dev(down))
        else:
            each_tile_far_first(lambda to: send(src, dst.at[ti], S_DZ0, tile_dev(to)))
        return dz, dc * f_g

    def await_near(n):
        got(dznear.at[n], (S_DZN2, S_DZN1)[n])

    def share_z(n):
        each_z(lambda to: send(dz_send.at[n], dzbuf.at[n, ti], (S_DZZ2, S_DZZ1)[n], tile_dev(row * 4 + to)))

    def share_x(n):
        got(dzbuf.at[n, pl.ds(0, 3)], (S_DZZ2, S_DZZ1)[n])
        mine = dzbuf.at[n, pl.ds(4 * row, 4)]
        each_x(lambda to: send(mine, mine, (S_DZX2, S_DZX1)[n], tile_dev(to * 4 + col)))

    def await_x(n):
        got(dzbuf.at[n, pl.ds(0, 12)], (S_DZX2, S_DZX1)[n])

    def back(n):
        zero = jnp.zeros((GR, W), F32)

        def stacked(x):
            return [shifted(x, 1 - b).astype(BF) for b in range(3)]

        await_near(n)
        above = stacked(jnp.where(has_up, dznear[n, 1].astype(F32), zero))
        below = stacked(jnp.where(has_down, dznear[n, 0].astype(F32), zero))
        whole = nn(whpt[...], jnp.concatenate(above + stacked(dz_send[n].astype(F32)) + below, 0))
        dhp[n + 1] = whole.astype(BF).reshape(L, PAD, W)

    def weight_part(n):
        t = 2 - n
        src = dzbuf.at[n]

        def body(r, carry):
            block = src[r].astype(F32)
            for b in range(3):
                stack[b * GR:(b + 1) * GR, pl.ds(pl.multiple_of((r + 1) * W, W), W)] = shifted(block, 1 - b).astype(BF)
            at = pl.multiple_of(r * W, W)
            scat[0:2 * PAD, pl.ds(at, W)] = fblk[r, 2 * t:2 * t + 2].reshape(2 * PAD, W)
            if t > 0:
                scat[2 * PAD:4 * PAD, pl.ds(at, W)] = hblk[t - 1, r].reshape(2 * PAD, W)
            return carry

        lax.fori_loop(0, T, body, 0, unroll=8)
        return jnp.concatenate([nt(stack[:, (2 - a) * W:(2 - a + T) * W], scat[...]) for a in range(3)], 0).T

    def share_weights(n, x):
        y = nn((x * (1.0 / 256.0)).astype(BF), pack[...]).astype(BF)
        wsend[n] = (nn(rsel[0], y[:, :256]) + nn(rsel[1], y[:, 256:])).astype(BF)
        src = wsend.at[n]
        dst = wrecv.at[n]
        dst[ti] = src[...]
        if n == 0:
            each_z(lambda to: send(src, dst.at[ti], S_WHZ, tile_dev(row * 4 + to)))
        else:
            send(src, dst.at[ti], S_WFA, tile_dev(row * 4 + lax.rem(col + 2, 4)))
            for mx in (2, 1, 3, 0):
                for mz in (1, 3, 0) if mx else (1, 3):
                    to = lax.rem(row + mx, 4) * 4 + lax.rem(col + mz, 4)
                    send(src, dst.at[ti], S_WF, tile_dev(to))

    def forward_weights():
        opposite = row * 4 + lax.rem(col + 2, 4)
        got(wrecv.at[1, 0], S_WFA)
        mine = wrecv.at[1, opposite]
        each_x(lambda to: send(mine, mine, S_WFB, tile_dev(to * 4 + col)))

    def share_weights_x():
        got(wrecv.at[0, pl.ds(0, 3)], S_WHZ)
        mine = wrecv.at[0, pl.ds(4 * row, 4)]
        each_x(lambda to: send(mine, mine, S_WHX, tile_dev(to * 4 + col)))

    def finish_weights(n):
        if n == 0:
            got(wrecv.at[0, pl.ds(0, 12)], S_WHX)
        else:
            got(wrecv.at[1, pl.ds(0, 11)], S_WF)
            got(wrecv.at[1, pl.ds(0, 3)], S_WFB)
        for s_ in range(T):
            block = wrecv[n, s_].astype(F32)
            xf[24 * s_:24 * (s_ + 1), 0:256] = block[0:24]
            xf[24 * s_:24 * (s_ + 1), 256:512] = block[24:48]
        first = HID * (1 - n)
        wg_out[:, first:first + HID] = nt(unpack[...], xf[...].astype(BF)).astype(BF)

    dz, dc = gate_grads(0, await_dh(0), dc)
    bias_sum = bias_sum + dz
    back(0)
    share_dh(1)
    share_z(0)
    got(hq.at[pl.ds(0, T - 1), 0], S_HQ)
    hq_mine = hq.at[:, core]
    send(hq_mine, hq_mine, S_HQC, partner)
    share_blocks(1)
    share_blocks(0)
    share_x(0)

    got(st_tile.at[pl.ds(0, T - 1)], S_ST)
    stl_send[0:8, :] = jnp.sum(st_tile[...], axis=0)
    lane = lax.broadcasted_iota(jnp.int32, (8, W), 1)
    stl_send[8:16, :] = jnp.where(lane == idx[0], 1.0, 0.0)
    each_lead(lambda to: send(stl_send, stl.at[li], S_STL, lead_dev(to)))
    stl[li] = stl_send[...]

    got(hq.at[:, 0], S_HQC)
    got(cotb.at[pl.ds(0, 12)], S_COTX)
    gamma_q = 1.0 + film_q[row, :, 0:1]
    beta_q = film_q[row, :, 1:2]

    def head_rows(r, carry):
        block = cotb[r].astype(F32)
        at = pl.multiple_of((r + 2) * W, W)
        for b in range(3):
            cc[96 * b:96 * (b + 1), pl.ds(at, W)] = shifted(block, 2 * (1 - b)).astype(BF)
        uq = gamma_q * hq[r].reshape(96, W).astype(F32) + beta_q
        vv[0:96, pl.ds(pl.multiple_of(r * W, W), W)] = (uq * jax.nn.sigmoid(uq)).astype(BF)
        return carry

    lax.fori_loop(0, T, head_rows, 0)
    for a in range(3):
        first = (4 - 2 * a) * W
        part = nt(cc[:, first:first + T * W], vv[...])
        for b in range(3):
            k = 3 * a + b
            for d in range(4):
                pbuf[d * 256 + k * 24:d * 256 + (k + 1) * 24, :] = part[b * 96 + d * 24:b * 96 + (d + 1) * 24]
    psend[...] = pbuf[...].astype(BF).reshape(L, 32, W)
    prec[li] = psend[8 * lax.rem(li, 4) + lax.div(li, 4)]

    dz, dc = gate_grads(1, await_dh(1), dc)
    bias_sum = bias_sum + dz
    back(1)
    share_dh(2)
    share_z(1)
    each_lead(lambda to: send(psend.at[8 * lax.rem(to, 4) + lax.div(to, 4)], prec.at[li], S_PR, lead_dev(to)))
    swap_blocks(1)
    swap_blocks(0)
    share_x(1)
    await_x(0)
    got(fblk.at[:, pl.ds(0, 3)], S_FRC)
    await_blocks(1)
    grads = weight_part(0)

    dz, dc = gate_grads(2, await_dh(2), dc)

    got(prec.at[pl.ds(0, L - 1)], S_PR)
    psum[...] = (jnp.sum(prec[...].astype(F32), axis=0) * (1.0 / 256.0)).astype(BF)
    owner = col * 4 + lax.rem(li, 4)
    gathers = lax.rem(li, 4) == col

    @pl.when(owner != ti)
    def _():
        send(psum, ptile.at[row], S_PT, tile_dev(owner))

    @pl.when(owner == ti)
    def _():
        ptile[row] = psum[...]

    await_x(1)
    await_blocks(0)
    grads = grads + weight_part(1)
    share_weights(0, grads[2 * PAD:4 * PAD])
    bias_sum = bias_sum + dz
    column = jnp.sum(bias_sum, axis=1, keepdims=True)
    lane = lax.broadcasted_iota(jnp.int32, (GR, W), 1)
    sub = lax.broadcasted_iota(jnp.int32, (GR, W), 0)
    line = jnp.sum(jnp.where(lane == sub, column, 0.0), axis=0, keepdims=True)
    bi_send[...] = jnp.broadcast_to(line, (8, W))
    each_tile_far_first(lambda to: send(bi_send, bi.at[ti], S_BI, tile_dev(to)))
    bi[ti] = bi_send[...]

    @pl.when(gathers)
    def _():
        @pl.when(owner == ti)
        def _():
            got(ptile.at[pl.ds(0, 3)], S_PT)

        @pl.when(owner != ti)
        def _():
            got(ptile, S_PT)

        each_lead(lambda to: send(ptile, plead.at[lax.div(li, 4)], S_PL, lead_dev(to)))
        plead[lax.div(li, 4)] = ptile[...]

    got(dzbuf.at[2, pl.ds(0, T - 1)], S_DZ0)
    share_weights_x()
    grads0 = weight_part(2)
    share_weights(1, grads[0:2 * PAD] + grads0[0:2 * PAD])
    forward_weights()

    got(stl.at[pl.ds(0, L - 1)], S_STL)

    def table(l, acc):
        block = stl[l]
        return tuple(acc[m] + block[8:16, m:m + 1] * block[0:8, :] for m in range(16))

    acc = lax.fori_loop(0, L, table, tuple(jnp.zeros((8, W), F32) for _ in range(16)))
    for m in range(16):
        rows6 = acc[m] * (1.0 / 256.0)
        for n in range(2):
            for q in range(3):
                fg_out[m, n:n + 1, W * q:W * (q + 1)] = rows6[3 * n + q:3 * n + q + 1]
    got(bi.at[pl.ds(0, T - 1)], S_BI)
    line = jnp.sum(bi[...], axis=0) * (1.0 / 256.0)
    for j in range(GATES):
        bg_out[j:j + 1, :] = line[0:1, j * OWN:(j + 1) * OWN]
    finish_weights(0)

    @pl.when(gathers)
    def _():
        got(plead.at[pl.ds(0, 7)], S_PL)

    @pl.when(jnp.logical_not(gathers))
    def _():
        got(plead, S_PL)

    wide = jnp.concatenate([plead[:, q].reshape(256, W) for q in range(4)], 1)
    hg_out[...] = nn(wide, spread[...])[0:TAPS * 24].astype(BF)
    finish_weights(1)

    for t in range(3):
        sent(rx.at[t], (S_YX0, S_YX1, S_YX2)[t])
        sent(hbuf.at[t, pl.ds(0, L - 1)], (S_H1, S_H2, S_H3)[t])
        sent(dhr.at[t, pl.ds(0, L - 1)], (S_DH3, S_DH2, S_DH1)[t])
    for t in range(2):
        sent(rh.at[t], (S_YH1, S_YH2)[t])
        sent(dznear.at[t], (S_DZN2, S_DZN1)[t])
        sent(dzbuf.at[t, pl.ds(0, 3)], (S_DZZ2, S_DZZ1)[t])
        sent(dzbuf.at[t, pl.ds(0, 12)], (S_DZX2, S_DZX1)[t])
        sent(hblk.at[t, pl.ds(0, T - 1), 0], (S_HB1, S_HB2)[t])
        sent(hblk.at[t, :, 0], (S_HB1C, S_HB2C)[t])
    sent(dzbuf.at[2, pl.ds(0, T - 1)], S_DZ0)
    sent(wrecv.at[0, pl.ds(0, 3)], S_WHZ)
    sent(wrecv.at[0, pl.ds(0, 12)], S_WHX)
    sent(wrecv.at[1, pl.ds(0, 11)], S_WF)
    sent(wrecv.at[1, 0], S_WFA)
    sent(wrecv.at[1, pl.ds(0, 3)], S_WFB)
    sent(coth.at[0], S_COTH)
    sent(coth.at[1], S_COTH2)
    sent(cotz.at[pl.ds(0, 3)], S_COTZ)
    sent(cotb.at[pl.ds(0, 12)], S_COTX)
    sent(fblk.at[pl.ds(0, T - 1), pl.ds(0, 3)], S_FR)
    sent(fblk.at[:, pl.ds(0, 3)], S_FRC)
    sent(hq.at[pl.ds(0, T - 1), 0], S_HQ)
    sent(hq.at[:, 0], S_HQC)
    sent(st_tile.at[pl.ds(0, T - 1)], S_ST)
    sent(stl.at[pl.ds(0, L - 1)], S_STL)
    sent(bi.at[pl.ds(0, T - 1)], S_BI)
    sent(prec.at[pl.ds(0, L - 1)], S_PR)

    @pl.when(owner != ti)
    def _():
        sent(psum, S_PT)

    @pl.when(gathers)
    def _():
        def body(d, carry):
            sent(ptile, S_PL)
            return carry
        lax.fori_loop(1, L, body, 0)


def finish(wg, bg, hg, fg, wg_out, bg_out, hg_out, fg_out):
    wg_out[...] = wg[...].astype(F32).reshape(OWN, TAPS, GATES, 2 * HID).astype(BF)
    bg_out[...] = bg[...]
    hg_out[...] = hg[...]
    fg_out[...] = fg[...]


def shards(frames, enc_weight, enc_bias, head_weight, film_table, lead_index, cotangent):
    a, pack, unpack, e, et, spread, rsel = [jnp.asarray(x) for x in one_hots()]
    wsrc = enc_weight.transpose(0, 2, 1, 3)
    hw = head_weight.transpose(1, 0, 2).reshape(TAPS * HID, HID)
    vm = pltpu.VMEM
    inputs = (
        wsrc, a, frames.reshape(3, HID, W), enc_bias.T, e, et, film_table, cotangent.reshape(HID, W), hw, pack, rsel,
        unpack, spread,
    )
    outs = pl.pallas_call(
        kernel,
        out_shape=(
            jax.ShapeDtypeStruct((OWN * TAPS * GATES, 2 * HID), BF),
            jax.ShapeDtypeStruct((GATES, OWN), F32),
            jax.ShapeDtypeStruct((TAPS * 24, HID), BF),
            jax.ShapeDtypeStruct((16, 2, HID), F32),
        ),
        in_specs=[pl.BlockSpec(memory_space=pl.ANY)] * (N_IN - 1) + [pl.BlockSpec(memory_space=pltpu.SMEM)],
        out_specs=(pl.BlockSpec(memory_space=vm),) * 4,
        scratch_shapes=[vm(x.shape, x.dtype) for x in inputs] + [
            vm((TAPS * GR, 2 * HID), BF),
            vm((TAPS * GR, CP), BF),
            vm((CP, TAPS * GR), BF),
            vm((W, HID), F32),
            vm((3, 3, GR, W), BF),
            vm((2, 3, GR, W), BF),
            vm((3, 2, GR, W), BF),
            vm((2, 2, GR, W), BF),
            vm((3, L, PAD, W), BF),
            vm((2, HID, W), BF),
            vm((4, 96, W), BF),
            vm((4, 96, W), BF),
            vm((T, 96, W), BF),
            vm((T, 6, PAD, W), BF),
            vm((T, 6, PAD, W), BF),
            vm((2, T, 2, PAD, W), BF),
            vm((2, L, PAD, W), F32),
            vm((3, L, PAD, W), BF),
            vm((3, L, PAD, W), BF),
            vm((8, 48, W), BF),
            vm((T, 2, 48, W), BF),
            vm((8, W), F32),
            vm((T, 8, W), F32),
            vm((16, W), F32),
            vm((L, 16, W), F32),
            vm((3, GR, W), BF),
            vm((2, 2, GR, W), BF),
            vm((3, T, GR, W), BF),
            vm((8, W), F32),
            vm((T, 8, W), F32),
            vm((3 * GR, (T + 2) * W), BF),
            vm((4 * PAD, T * W), BF),
            vm((2, 48, 256), BF),
            vm((2, T, 48, 256), BF),
            vm((HID, 512), F32),
            vm((3 * 96, (T + 4) * W), BF),
            vm((W, T * W), BF),
            vm((L * 32, W), F32),
            vm((L, 32, W), BF),
            vm((L, 32, W), BF),
            vm((32, W), BF),
            vm((4, 32, W), BF),
            vm((8, 4, 32, W), BF),
            vm((L, PAD, 8), F32),
            vm((4, 96, 8), F32),
            vm((HID, W), F32),
            pltpu.SemaphoreType.DMA((NSEM,)),
            pltpu.SemaphoreType.DMA((NSEM,)),
            pltpu.SemaphoreType.DMA((N_IN - 1,)),
        ],
        compiler_params=pltpu.CompilerParams(
            collective_id=0, has_side_effects=True, vmem_limit_bytes=56 * 2**20
        ),
    )(*inputs, lead_index)
    wg, bg, hg, fg = pl.pallas_call(
        finish,
        out_shape=(
            jax.ShapeDtypeStruct((OWN, TAPS, GATES, 2 * HID), BF),
            jax.ShapeDtypeStruct((GATES, OWN), F32),
            jax.ShapeDtypeStruct((TAPS * 24, HID), BF),
            jax.ShapeDtypeStruct((16, 2, HID), F32),
        ),
        in_specs=[pl.BlockSpec(memory_space=vm)] * 4,
        out_specs=(pl.BlockSpec(memory_space=vm),) * 4,
    )(*outs)
    return wg.transpose(0, 2, 1, 3), bg.T, hg.reshape(TAPS, 24, HID).transpose(1, 0, 2), fg


def solution(mesh):
    in_specs = (
        P(None, None, "tile", None),
        P("lead", None, None, None),
        P("lead", None),
        P(),
        P(),
        P("lead"),
        P("lead", None, "tile", None),
    )
    out_specs = (P("lead", None, None, None), P("lead", None), P("tile", None, None), P())
    return jax.shard_map(shards, mesh=mesh, in_specs=in_specs, out_specs=out_specs, check_vma=False)
```

```python
import numpy as np
import jax
import jax.numpy as jnp
import ml_dtypes
from jax import lax
from jax.experimental import pallas as pl
from jax.experimental.pallas import tpu as pltpu
from jax.sharding import PartitionSpec as P

MESH = pl.DeviceIdType.MESH
BF = jnp.bfloat16
F32 = jnp.float32
L, T, HID, W = 32, 16, 384, 128
OWN, PAD, GATES, TAPS = 12, 16, 4, 9
GR = GATES * OWN
CP = L * PAD


def one_hots():
    a = np.zeros((TAPS * GR, OWN * TAPS * GATES), np.float32)
    pack = np.zeros((TAPS * GR, 512), np.float32)
    unpack = np.zeros((OWN * TAPS * GATES, 512), np.float32)
    for k in range(TAPS):
        for j in range(GATES):
            for o in range(OWN):
                inner = k * GR + j * OWN + o
                outer = (o * TAPS + k) * GATES + j
                column = inner + (0 if k < 5 else 16)
                a[inner, outer] = 1
                pack[inner, column] = 1
                unpack[outer, column] = 1
    e = np.zeros((HID, CP), np.float32)
    for i in range(L):
        for o in range(OWN):
            e[i * OWN + o, i * PAD + o] = 1
    spread = np.zeros((512, HID), np.float32)
    for q in range(4):
        for c in range(96):
            spread[128 * q + c, 96 * q + c] = 1
    rows = np.zeros((2, 48, 32), np.float32)
    for half in range(2):
        for c in range(24):
            rows[half, 24 * half + c, (c // OWN) * PAD + c % OWN] = 1
    return [x.astype(ml_dtypes.bfloat16) for x in (a, pack, unpack, e, e.T.copy(), spread, rows)]


def nn(a, b):
    return lax.dot_general(a, b, (((1,), (0,)), ((), ())), preferred_element_type=F32)


def nt(a, b):
    return lax.dot_general(a, b, (((1,), (1,)), ((), ())), preferred_element_type=F32)


def shifted(x, s):
    if s == 0:
        return x
    lane = lax.broadcasted_iota(jnp.int32, x.shape, 1)
    keep = lane < W - s if s > 0 else lane >= -s
    return jnp.where(keep, pltpu.roll(x, (-s) % W, 1), 0.0)


def shifted_rows(x, s):
    if s == 0:
        return x
    row = lax.broadcasted_iota(jnp.int32, x.shape, 0)
    keep = row < W - s if s > 0 else row >= -s
    return jnp.where(keep, pltpu.roll(x, (-s) % W, 0), 0.0)


(S_YX0, S_YX1, S_YX2, S_H1, S_H2, S_H3, S_YH1, S_YH2, S_COTH, S_COTZ, S_COTX, S_FR, S_FRC, S_HB1, S_HB2, S_HB1C, S_HB2C,
 S_DH3, S_DH2, S_DH1, S_HQ, S_HQC, S_ST, S_STL, S_DZN2, S_DZN1, S_DZ0, S_DZZ2, S_DZZ1, S_DZX2, S_DZX1, S_BI, S_WHZ, S_WHX, S_WF,
 S_WFA, S_WFB, S_PR, S_PT, S_PL, S_COTH2, NSEM) = range(42)


N_IN = 14


def kernel(*refs):
    inputs, (wg_out, bg_out, hg_out, fg_out), refs = refs[:N_IN], refs[N_IN:N_IN + 4], refs[N_IN + 4:]
    held, refs = refs[:N_IN - 1], refs[N_IN - 1:]
    idx = inputs[N_IN - 1]
    (
        wt, whp, whpt, dvt_ref, yx, yh, rx, rh, hbuf, coth, cot4, cotz, cotb, fsend, fblk, hblk, dv_ref, dhp, dhr,
        h8, hq, st_send, st_tile, stl_send, stl, dz_send, dznear, dzbuf, bi_send, bi, stack, scat,
        wsend, wrecv, xf, cc, vv, pbuf, psend, prec, psum, ptile, plead, film_col, film_q, flat, ssem, rsem, lsem,
    ) = refs
    wsrc, a_ref, frames, bias, e_ref, et_ref, film, cot, hw, pack, rsel, unpack, spread = held
    li = lax.axis_index("lead")
    ti = lax.axis_index("tile")

    def lead_dev(to):
        return (to, ti)

    def tile_dev(to):
        return (li, to)

    def send(src, dst, sem, dev):
        pltpu.make_async_remote_copy(
            src_ref=src, dst_ref=dst, send_sem=ssem.at[sem], recv_sem=rsem.at[sem], device_id=dev, device_id_type=MESH
        ).start()

    def got(ref, sem):
        pltpu.make_async_copy(ref, ref, rsem.at[sem]).wait()

    def sent(ref, sem):
        pltpu.make_async_copy(ref, ref, ssem.at[sem]).wait()

    def load(n):
        return pltpu.make_async_copy(inputs[n], held[n], lsem.at[n])

    def each_lead(fn):
        ring, side = lax.rem(lax.div(li, 2), 8), lax.div(li, 16)

        def body(n, carry):
            m = lax.div(n, 4)
            step = lax.div(m + 1, 2) * (1 - 2 * lax.rem(m, 2))
            other = lax.rem(ring + 12 + step, 8)
            rest = 3 - lax.rem(n, 4)
            side_to = lax.rem(side + lax.div(rest, 2), 2)
            core_to = lax.rem(core + lax.rem(rest, 2), 2)
            fn(side_to * 16 + other * 2 + core_to)
            return carry
        lax.fori_loop(0, L - 1, body, 0)

    row, col = lax.div(ti, 4), lax.rem(ti, 4)
    core = lax.rem(li, 2)
    partner = lead_dev(li + 1 - 2 * core)

    def each_z(fn):
        for m in (2, 1, 3):
            fn(lax.rem(col + m, 4))

    def each_x(fn):
        for m in (2, 1, 3):
            fn(lax.rem(row + m, 4))

    def each_tile_far_first(fn):

        def away(m):
            return 6 + lax.div(m + 1, 2) * (1 - 2 * lax.rem(m, 2))

        def body(n, carry):
            fn(lax.rem(row + away(lax.div(n, 4)), 4) * 4 + lax.rem(col + away(lax.rem(n, 4)), 4))
            return carry
        lax.fori_loop(0, T - 1, body, 0)

    def each_tile(fn, first=1, last=T):
        def body(d, carry):
            fn(lax.rem(ti + d, T))
            return carry
        lax.fori_loop(first, last, body, 0)

    bar = pltpu.get_barrier_semaphore()
    each_lead(lambda to: pl.semaphore_signal(bar, inc=1, device_id=lead_dev(to), device_id_type=MESH))
    each_tile_far_first(lambda to: pl.semaphore_signal(bar, inc=1, device_id=tile_dev(to), device_id_type=MESH))
    for n in range(N_IN - 1):
        load(n).start()

    up = lax.rem(ti + 1, T)
    down = lax.rem(ti + T - 1, T)
    has_up = ti < T - 1
    has_down = ti > 0

    for n in range(4):
        load(n).wait()
    outer = wsrc[...].astype(F32).reshape(OWN * TAPS * GATES, 2 * HID).astype(BF)
    wt[...] = nn(a_ref[...], outer).astype(BF)
    sub = lax.broadcasted_iota(jnp.int32, (OWN, OWN), 0)
    lane = lax.broadcasted_iota(jnp.int32, (OWN, OWN), 1)
    bias_cols = [jnp.sum(jnp.where(sub == lane, bias[j:j + 1, :], 0.0), axis=1, keepdims=True) for j in range(GATES)]

    def row_parts(g):
        return [sum(shifted(g[(3 * a + b) * GR:(3 * a + b + 1) * GR], b - 1) for b in range(3)) for a in range(3)]

    own_x = []

    def frame_parts(t):
        parts = row_parts(nn(wt[:, 0:HID], frames[t]))
        for a in (0, 2):
            yx[t, a] = parts[a].astype(BF)
        own_x.append(parts[1])

    frame_parts(0)
    pl.semaphore_wait(bar, L + T - 2)

    def halo(src, dst, sem):
        send(src.at[0], dst.at[0], sem, tile_dev(up))
        send(src.at[2], dst.at[1], sem, tile_dev(down))

    halo(yx.at[0], rx.at[0], S_YX0)
    for n in range(4, N_IN - 1):
        load(n).wait()
    whp[...] = nn(wt[:, HID:], e_ref[...]).astype(BF)
    whpt[...] = nt(et_ref[...], wt[:, HID:]).astype(BF)
    def from_neighbours(r):
        return jnp.where(has_down, r[0].astype(F32), 0.0) + jnp.where(has_up, r[1].astype(F32), 0.0)

    def padded(x):
        return jnp.concatenate([x, jnp.zeros((PAD - OWN, W), F32)], 0)

    def cell(z, previous):
        z = [padded(z[j * OWN:(j + 1) * OWN] + bias_cols[j]) for j in range(GATES)]
        i_g = jax.nn.sigmoid(z[0])
        f_g = jax.nn.sigmoid(z[1])
        g_g = jnp.tanh(z[2])
        o_g = jax.nn.sigmoid(z[3])
        now = f_g * previous + i_g * g_g
        return (i_g, f_g, g_g, o_g, previous, now), (o_g * jnp.tanh(now)).astype(BF)

    def share_h(t, h):
        buf = hbuf.at[t]
        buf[li] = h
        sem = (S_H1, S_H2, S_H3)[t]
        each_lead(lambda to: send(buf.at[li], buf.at[li], sem, lead_dev(to)))

    def await_h(t):
        got(hbuf.at[t, pl.ds(0, L - 1)], (S_H1, S_H2, S_H3)[t])

    saved = []
    got(rx.at[0], S_YX0)
    z = own_x[0] + from_neighbours(rx.at[0])
    state, h = cell(z, jnp.zeros((PAD, W), F32))
    saved.append(state)
    share_h(0, h)
    for t in (1, 2):
        frame_parts(t)
        halo(yx.at[t], rx.at[t], (S_YX0, S_YX1, S_YX2)[t])
    send(cot, coth.at[0], S_COTH, tile_dev(lax.rem(ti + 2, T)))
    for t in range(3):
        fsend[:, 2 * t:2 * t + 2] = nn(et_ref[...], frames[t]).astype(BF).reshape(T, 2, PAD, W)
    for p in range(4):
        cot4[p] = cot[96 * p:96 * (p + 1), :]
    slot = lax.broadcasted_iota(jnp.int32, (16, 2, HID), 0)
    lines = jnp.sum(jnp.where(slot == idx[0], film[...], 0.0), axis=0)
    lines = jnp.concatenate([lines, jnp.zeros((6, HID), F32)], 0).T
    film_col[...] = jnp.zeros_like(film_col)
    for i in range(L):
        film_col[i, 0:OWN, :] = lines[i * OWN:(i + 1) * OWN]
    film_q[...] = lines.reshape(4, 96, 8)
    for at in (0, (T + 1) * W):
        stack[:, at:at + W] = jnp.zeros((3 * GR, W), BF)
    for at in (0, (T + 2) * W):
        cc[:, at:at + 2 * W] = jnp.zeros((3 * 96, 2 * W), BF)
    vv[96:W, :] = jnp.zeros((W - 96, T * W), BF)
    for d in range(4):
        pbuf[256 * d + 216:256 * (d + 1), :] = jnp.zeros((40, W), F32)
    scat[...] = jnp.zeros_like(scat)

    def half(x):
        return x.at[pl.ds(3 * core, 3)]

    def send_frames(to):
        send(half(fsend.at[to]), half(fblk.at[ti]), S_FR, tile_dev(to))

    zero_row = jnp.zeros((HID, W), BF)

    def head_product(a, x):
        ct = x.astype(F32).T
        total = None
        for b in range(3):
            k = 3 * a + b
            term = nn(shifted_rows(ct, -2 * (b - 1)).astype(BF), hw[k * HID:(k + 1) * HID, :])
            total = term if total is None else total + term
        return total

    for t in (1, 2):
        await_h(t - 1)
        parts = row_parts(nn(whp[...], hbuf[t - 1].reshape(CP, W)))
        for a in (0, 2):
            yh[t - 1, a] = parts[a].astype(BF)
        sem = (S_YH1, S_YH2)[t - 1]
        halo(yh.at[t - 1], rh.at[t - 1], sem)
        got(rx.at[t], (S_YX0, S_YX1, S_YX2)[t])
        base = own_x[t] + from_neighbours(rx.at[t]) + parts[1]
        got(rh.at[t - 1], sem)
        z = base + from_neighbours(rh.at[t - 1])
        state, h = cell(z, saved[-1][5])
        saved.append(state)
        share_h(t, h)
        if t == 1:
            send(cot, coth.at[1], S_COTH2, tile_dev(lax.rem(ti + T - 2, T)))
            dvt = head_product(1, cot[...])
            got(coth.at[0], S_COTH)
            dvt_ref[...] = dvt + head_product(2, jnp.where(ti >= 2, coth[0], zero_row))
    each_tile_far_first(send_frames)
    fblk[ti, pl.ds(3 * core, 3)] = fsend[ti, pl.ds(3 * core, 3)]
    each_z(lambda to: send(cot4.at[to], cotz.at[col], S_COTZ, tile_dev(row * 4 + to)))
    cotz[col] = cot4[col]
    got(coth.at[1], S_COTH2)
    dv = (dvt_ref[...] + head_product(0, jnp.where(ti < T - 2, coth[1], zero_row))).T
    dv_ref[...] = jnp.zeros_like(dv_ref)
    for i in range(L):
        dv_ref[0, i, 0:OWN, :] = dv[i * OWN:(i + 1) * OWN]
    dv_ref[1] = nn(et_ref[...], cot[...]).reshape(L, PAD, W)
    factors = []
    for i_g, f_g, g_g, o_g, previous, now in saved:
        sq = jnp.tanh(now)
        factors.append((
            o_g * (1.0 - sq * sq), g_g * i_g * (1.0 - i_g), previous * f_g * (1.0 - f_g), i_g * (1.0 - g_g * g_g),
            sq * o_g * (1.0 - o_g), f_g,
        ))

    def share_blocks(t):
        hsem = (S_HB1, S_HB2)[t]
        hb = hblk.at[t]
        hs = hbuf.at[t]
        hb[ti, core] = hs[2 * ti + core]
        each_tile_far_first(lambda to: send(hs.at[2 * to + core], hb.at[ti, core], hsem, tile_dev(to)))

    def swap_blocks(t):
        got(hblk.at[t, pl.ds(0, T - 1), 0], (S_HB1, S_HB2)[t])
        mine = hblk.at[t, :, core]
        send(mine, mine, (S_HB1C, S_HB2C)[t], partner)

    def await_blocks(t):
        got(hblk.at[t, :, 0], (S_HB1C, S_HB2C)[t])

    await_h(2)
    h_wide = hbuf[2].reshape(CP, W).astype(F32)
    columns = film_col[...].reshape(CP, 8)
    gamma = 1.0 + columns[:, 0:1]
    u = gamma * h_wide + columns[:, 1:2]
    s = jax.nn.sigmoid(u)
    du = dv_ref[0].reshape(CP, W) * s * (1.0 + u * (1.0 - s))
    dhp[0] = (dv_ref[1].reshape(CP, W) + gamma * du).astype(BF).reshape(L, PAD, W)

    def share_dh(n):
        sem = (S_DH3, S_DH2, S_DH1)[n]
        src = dhp.at[n]
        dst = dhr.at[n]
        each_lead(lambda to: send(src.at[to], dst.at[li], sem, lead_dev(to)))
        dst[li] = src[li]

    def await_dh(n):
        got(dhr.at[n, pl.ds(0, L - 1)], (S_DH3, S_DH2, S_DH1)[n])
        return jnp.sum(dhr[n].astype(F32), axis=0)

    share_dh(0)
    h8[...] = nn(e_ref[...], hbuf[2].reshape(CP, W)).astype(BF).reshape(8, 48, W)
    each_tile_far_first(lambda to: send(h8.at[2 * lax.div(to, 4) + core], hq.at[ti, core], S_HQ, tile_dev(to)))
    hq[ti, core] = h8[2 * row + core]
    got(cotz.at[pl.ds(0, 3)], S_COTZ)
    each_x(lambda to: send(cotz, cotb.at[pl.ds(4 * row, 4)], S_COTX, tile_dev(to * 4 + col)))
    cotb[pl.ds(4 * row, 4)] = cotz[...]
    st_send[...] = jnp.zeros_like(st_send)
    for n, field in enumerate((du * h_wide, du)):
        for i in range(L):
            flat[i * OWN:(i + 1) * OWN, :] = field[i * PAD:i * PAD + OWN]
        line = jnp.sum(flat[...].T, axis=0, keepdims=True)
        for q in range(3):
            st_send[3 * n + q:3 * n + q + 1, :] = line[:, 128 * q:128 * (q + 1)]
    each_tile_far_first(lambda to: send(st_send, st_tile.at[ti], S_ST, tile_dev(to)))
    st_tile[ti] = st_send[...]
    got(fblk.at[pl.ds(0, T - 1), pl.ds(0, 3)], S_FR)
    fr_mine = fblk.at[:, pl.ds(3 * core, 3)]
    send(fr_mine, fr_mine, S_FRC, partner)

    bias_sum = jnp.zeros((GR, W), F32)
    dc = jnp.zeros((PAD, W), F32)

    def gate_grads(n, dh, dc):
        to_c, to_i, to_f, to_g, to_o, f_g = factors[2 - n]
        dc = dc + dh * to_c
        dz = jnp.concatenate([x[0:OWN] for x in (dc * to_i, dc * to_f, dc * to_g, dh * to_o)], 0)
        src = dz_send.at[n]
        dst = dzbuf.at[n]
        src[...] = dz.astype(BF)
        dst[ti] = src[...]
        if n < 2:
            send(src, dznear.at[n, 0], (S_DZN2, S_DZN1)[n], tile_dev(up))
            send(src, dznear.at[n, 1], (S_DZN2, S_DZN1)[n], tile_dev(down))
        else:
            each_tile_far_first(lambda to: send(src, dst.at[ti], S_DZ0, tile_dev(to)))
        return dz, dc * f_g

    def await_near(n):
        got(dznear.at[n], (S_DZN2, S_DZN1)[n])

    def share_z(n):
        each_z(lambda to: send(dz_send.at[n], dzbuf.at[n, ti], (S_DZZ2, S_DZZ1)[n], tile_dev(row * 4 + to)))

    def share_x(n):
        got(dzbuf.at[n, pl.ds(0, 3)], (S_DZZ2, S_DZZ1)[n])
        mine = dzbuf.at[n, pl.ds(4 * row, 4)]
        each_x(lambda to: send(mine, mine, (S_DZX2, S_DZX1)[n], tile_dev(to * 4 + col)))

    def await_x(n):
        got(dzbuf.at[n, pl.ds(0, 12)], (S_DZX2, S_DZX1)[n])

    def back(n):
        zero = jnp.zeros((GR, W), F32)

        def stacked(x):
            return [shifted(x, 1 - b).astype(BF) for b in range(3)]

        await_near(n)
        above = stacked(jnp.where(has_up, dznear[n, 1].astype(F32), zero))
        below = stacked(jnp.where(has_down, dznear[n, 0].astype(F32), zero))
        whole = nn(whpt[...], jnp.concatenate(above + stacked(dz_send[n].astype(F32)) + below, 0))
        dhp[n + 1] = whole.astype(BF).reshape(L, PAD, W)

    def weight_part(n):
        t = 2 - n
        src = dzbuf.at[n]

        def body(r, carry):
            block = src[r].astype(F32)
            for b in range(3):
                stack[b * GR:(b + 1) * GR, pl.ds(pl.multiple_of((r + 1) * W, W), W)] = shifted(block, 1 - b).astype(BF)
            at = pl.multiple_of(r * W, W)
            scat[0:2 * PAD, pl.ds(at, W)] = fblk[r, 2 * t:2 * t + 2].reshape(2 * PAD, W)
            if t > 0:
                scat[2 * PAD:4 * PAD, pl.ds(at, W)] = hblk[t - 1, r].reshape(2 * PAD, W)
            return carry

        lax.fori_loop(0, T, body, 0, unroll=16)
        return jnp.concatenate([nt(stack[:, (2 - a) * W:(2 - a + T) * W], scat[...]) for a in range(3)], 0).T

    def share_weights(n, x):
        y = nn((x * (1.0 / 256.0)).astype(BF), pack[...]).astype(BF)
        wsend[n] = (nn(rsel[0], y[:, :256]) + nn(rsel[1], y[:, 256:])).astype(BF)
        src = wsend.at[n]
        dst = wrecv.at[n]
        dst[ti] = src[...]
        if n == 0:
            each_z(lambda to: send(src, dst.at[ti], S_WHZ, tile_dev(row * 4 + to)))
        else:
            send(src, dst.at[ti], S_WFA, tile_dev(row * 4 + lax.rem(col + 2, 4)))
            for mx in (2, 1, 3, 0):
                for mz in (1, 3, 0) if mx else (1, 3):
                    to = lax.rem(row + mx, 4) * 4 + lax.rem(col + mz, 4)
                    send(src, dst.at[ti], S_WF, tile_dev(to))

    def forward_weights():
        opposite = row * 4 + lax.rem(col + 2, 4)
        got(wrecv.at[1, 0], S_WFA)
        mine = wrecv.at[1, opposite]
        each_x(lambda to: send(mine, mine, S_WFB, tile_dev(to * 4 + col)))

    def share_weights_x():
        got(wrecv.at[0, pl.ds(0, 3)], S_WHZ)
        mine = wrecv.at[0, pl.ds(4 * row, 4)]
        each_x(lambda to: send(mine, mine, S_WHX, tile_dev(to * 4 + col)))

    def finish_weights(n):
        if n == 0:
            got(wrecv.at[0, pl.ds(0, 12)], S_WHX)
        else:
            got(wrecv.at[1, pl.ds(0, 11)], S_WF)
            got(wrecv.at[1, pl.ds(0, 3)], S_WFB)
        for s_ in range(T):
            block = wrecv[n, s_].astype(F32)
            xf[24 * s_:24 * (s_ + 1), 0:256] = block[0:24]
            xf[24 * s_:24 * (s_ + 1), 256:512] = block[24:48]
        first = HID * (1 - n)
        wg_out[:, first:first + HID] = nt(unpack[...], xf[...].astype(BF)).astype(BF)

    dz, dc = gate_grads(0, await_dh(0), dc)
    bias_sum = bias_sum + dz
    back(0)
    share_dh(1)
    share_z(0)
    got(hq.at[pl.ds(0, T - 1), 0], S_HQ)
    hq_mine = hq.at[:, core]
    send(hq_mine, hq_mine, S_HQC, partner)
    share_blocks(1)
    share_blocks(0)
    share_x(0)

    got(st_tile.at[pl.ds(0, T - 1)], S_ST)
    stl_send[0:8, :] = jnp.sum(st_tile[...], axis=0)
    lane = lax.broadcasted_iota(jnp.int32, (8, W), 1)
    stl_send[8:16, :] = jnp.where(lane == idx[0], 1.0, 0.0)
    each_lead(lambda to: send(stl_send, stl.at[li], S_STL, lead_dev(to)))
    stl[li] = stl_send[...]

    got(hq.at[:, 0], S_HQC)
    got(cotb.at[pl.ds(0, 12)], S_COTX)
    gamma_q = 1.0 + film_q[row, :, 0:1]
    beta_q = film_q[row, :, 1:2]

    def head_rows(r, carry):
        block = cotb[r].astype(F32)
        at = pl.multiple_of((r + 2) * W, W)
        for b in range(3):
            cc[96 * b:96 * (b + 1), pl.ds(at, W)] = shifted(block, 2 * (1 - b)).astype(BF)
        uq = gamma_q * hq[r].reshape(96, W).astype(F32) + beta_q
        vv[0:96, pl.ds(pl.multiple_of(r * W, W), W)] = (uq * jax.nn.sigmoid(uq)).astype(BF)
        return carry

    lax.fori_loop(0, T, head_rows, 0, unroll=4)
    for a in range(3):
        first = (4 - 2 * a) * W
        part = nt(cc[:, first:first + T * W], vv[...])
        for b in range(3):
            k = 3 * a + b
            for d in range(4):
                pbuf[d * 256 + k * 24:d * 256 + (k + 1) * 24, :] = part[b * 96 + d * 24:b * 96 + (d + 1) * 24]
    psend[...] = pbuf[...].astype(BF).reshape(L, 32, W)
    prec[li] = psend[8 * lax.rem(li, 4) + lax.div(li, 4)]

    dz, dc = gate_grads(1, await_dh(1), dc)
    bias_sum = bias_sum + dz
    back(1)
    share_dh(2)
    share_z(1)
    each_lead(lambda to: send(psend.at[8 * lax.rem(to, 4) + lax.div(to, 4)], prec.at[li], S_PR, lead_dev(to)))
    swap_blocks(1)
    swap_blocks(0)
    share_x(1)
    await_x(0)
    got(fblk.at[:, pl.ds(0, 3)], S_FRC)
    await_blocks(1)
    grads = weight_part(0)

    dz, dc = gate_grads(2, await_dh(2), dc)

    got(prec.at[pl.ds(0, L - 1)], S_PR)
    psum[...] = (jnp.sum(prec[...].astype(F32), axis=0) * (1.0 / 256.0)).astype(BF)
    owner = col * 4 + lax.rem(li, 4)
    gathers = lax.rem(li, 4) == col

    @pl.when(owner != ti)
    def _():
        send(psum, ptile.at[row], S_PT, tile_dev(owner))

    @pl.when(owner == ti)
    def _():
        ptile[row] = psum[...]

    await_x(1)
    await_blocks(0)
    grads = grads + weight_part(1)
    share_weights(0, grads[2 * PAD:4 * PAD])
    bias_sum = bias_sum + dz
    column = jnp.sum(bias_sum, axis=1, keepdims=True)
    lane = lax.broadcasted_iota(jnp.int32, (GR, W), 1)
    sub = lax.broadcasted_iota(jnp.int32, (GR, W), 0)
    line = jnp.sum(jnp.where(lane == sub, column, 0.0), axis=0, keepdims=True)
    bi_send[...] = jnp.broadcast_to(line, (8, W))
    each_tile_far_first(lambda to: send(bi_send, bi.at[ti], S_BI, tile_dev(to)))
    bi[ti] = bi_send[...]

    @pl.when(gathers)
    def _():
        @pl.when(owner == ti)
        def _():
            got(ptile.at[pl.ds(0, 3)], S_PT)

        @pl.when(owner != ti)
        def _():
            got(ptile, S_PT)

        each_lead(lambda to: send(ptile, plead.at[lax.div(li, 4)], S_PL, lead_dev(to)))
        plead[lax.div(li, 4)] = ptile[...]

    got(dzbuf.at[2, pl.ds(0, T - 1)], S_DZ0)
    share_weights_x()
    grads0 = weight_part(2)
    share_weights(1, grads[0:2 * PAD] + grads0[0:2 * PAD])
    forward_weights()

    got(stl.at[pl.ds(0, L - 1)], S_STL)

    def table(l, acc):
        block = stl[l]
        return tuple(acc[m] + block[8:16, m:m + 1] * block[0:8, :] for m in range(16))

    acc = lax.fori_loop(0, L, table, tuple(jnp.zeros((8, W), F32) for _ in range(16)))
    for m in range(16):
        rows6 = acc[m] * (1.0 / 256.0)
        for n in range(2):
            for q in range(3):
                fg_out[m, n:n + 1, W * q:W * (q + 1)] = rows6[3 * n + q:3 * n + q + 1]
    got(bi.at[pl.ds(0, T - 1)], S_BI)
    line = jnp.sum(bi[...], axis=0) * (1.0 / 256.0)
    for j in range(GATES):
        bg_out[j:j + 1, :] = line[0:1, j * OWN:(j + 1) * OWN]
    finish_weights(0)

    @pl.when(gathers)
    def _():
        got(plead.at[pl.ds(0, 7)], S_PL)

    @pl.when(jnp.logical_not(gathers))
    def _():
        got(plead, S_PL)

    wide = jnp.concatenate([plead[:, q].reshape(256, W) for q in range(4)], 1)
    hg_out[...] = nn(wide, spread[...])[0:TAPS * 24].astype(BF)
    finish_weights(1)

    for t in range(3):
        sent(rx.at[t], (S_YX0, S_YX1, S_YX2)[t])
        sent(hbuf.at[t, pl.ds(0, L - 1)], (S_H1, S_H2, S_H3)[t])
        sent(dhr.at[t, pl.ds(0, L - 1)], (S_DH3, S_DH2, S_DH1)[t])
    for t in range(2):
        sent(rh.at[t], (S_YH1, S_YH2)[t])
        sent(dznear.at[t], (S_DZN2, S_DZN1)[t])
        sent(dzbuf.at[t, pl.ds(0, 3)], (S_DZZ2, S_DZZ1)[t])
        sent(dzbuf.at[t, pl.ds(0, 12)], (S_DZX2, S_DZX1)[t])
        sent(hblk.at[t, pl.ds(0, T - 1), 0], (S_HB1, S_HB2)[t])
        sent(hblk.at[t, :, 0], (S_HB1C, S_HB2C)[t])
    sent(dzbuf.at[2, pl.ds(0, T - 1)], S_DZ0)
    sent(wrecv.at[0, pl.ds(0, 3)], S_WHZ)
    sent(wrecv.at[0, pl.ds(0, 12)], S_WHX)
    sent(wrecv.at[1, pl.ds(0, 11)], S_WF)
    sent(wrecv.at[1, 0], S_WFA)
    sent(wrecv.at[1, pl.ds(0, 3)], S_WFB)
    sent(coth.at[0], S_COTH)
    sent(coth.at[1], S_COTH2)
    sent(cotz.at[pl.ds(0, 3)], S_COTZ)
    sent(cotb.at[pl.ds(0, 12)], S_COTX)
    sent(fblk.at[pl.ds(0, T - 1), pl.ds(0, 3)], S_FR)
    sent(fblk.at[:, pl.ds(0, 3)], S_FRC)
    sent(hq.at[pl.ds(0, T - 1), 0], S_HQ)
    sent(hq.at[:, 0], S_HQC)
    sent(st_tile.at[pl.ds(0, T - 1)], S_ST)
    sent(stl.at[pl.ds(0, L - 1)], S_STL)
    sent(bi.at[pl.ds(0, T - 1)], S_BI)
    sent(prec.at[pl.ds(0, L - 1)], S_PR)

    @pl.when(owner != ti)
    def _():
        sent(psum, S_PT)

    @pl.when(gathers)
    def _():
        def body(d, carry):
            sent(ptile, S_PL)
            return carry
        lax.fori_loop(1, L, body, 0)


def finish(wg, bg, hg, fg, wg_out, bg_out, hg_out, fg_out):
    wg_out[...] = wg[...].astype(F32).reshape(OWN, TAPS, GATES, 2 * HID).astype(BF)
    bg_out[...] = bg[...]
    hg_out[...] = hg[...]
    fg_out[...] = fg[...]


def shards(frames, enc_weight, enc_bias, head_weight, film_table, lead_index, cotangent):
    a, pack, unpack, e, et, spread, rsel = [jnp.asarray(x) for x in one_hots()]
    wsrc = enc_weight.transpose(0, 2, 1, 3)
    hw = head_weight.transpose(1, 0, 2).reshape(TAPS * HID, HID)
    vm = pltpu.VMEM
    inputs = (
        wsrc, a, frames.reshape(3, HID, W), enc_bias.T, e, et, film_table, cotangent.reshape(HID, W), hw, pack, rsel,
        unpack, spread,
    )
    outs = pl.pallas_call(
        kernel,
        out_shape=(
            jax.ShapeDtypeStruct((OWN * TAPS * GATES, 2 * HID), BF),
            jax.ShapeDtypeStruct((GATES, OWN), F32),
            jax.ShapeDtypeStruct((TAPS * 24, HID), BF),
            jax.ShapeDtypeStruct((16, 2, HID), F32),
        ),
        in_specs=[pl.BlockSpec(memory_space=pl.ANY)] * (N_IN - 1) + [pl.BlockSpec(memory_space=pltpu.SMEM)],
        out_specs=(pl.BlockSpec(memory_space=vm),) * 4,
        scratch_shapes=[vm(x.shape, x.dtype) for x in inputs] + [
            vm((TAPS * GR, 2 * HID), BF),
            vm((TAPS * GR, CP), BF),
            vm((CP, TAPS * GR), BF),
            vm((W, HID), F32),
            vm((3, 3, GR, W), BF),
            vm((2, 3, GR, W), BF),
            vm((3, 2, GR, W), BF),
            vm((2, 2, GR, W), BF),
            vm((3, L, PAD, W), BF),
            vm((2, HID, W), BF),
            vm((4, 96, W), BF),
            vm((4, 96, W), BF),
            vm((T, 96, W), BF),
            vm((T, 6, PAD, W), BF),
            vm((T, 6, PAD, W), BF),
            vm((2, T, 2, PAD, W), BF),
            vm((2, L, PAD, W), F32),
            vm((3, L, PAD, W), BF),
            vm((3, L, PAD, W), BF),
            vm((8, 48, W), BF),
            vm((T, 2, 48, W), BF),
            vm((8, W), F32),
            vm((T, 8, W), F32),
            vm((16, W), F32),
            vm((L, 16, W), F32),
            vm((3, GR, W), BF),
            vm((2, 2, GR, W), BF),
            vm((3, T, GR, W), BF),
            vm((8, W), F32),
            vm((T, 8, W), F32),
            vm((3 * GR, (T + 2) * W), BF),
            vm((4 * PAD, T * W), BF),
            vm((2, 48, 256), BF),
            vm((2, T, 48, 256), BF),
            vm((HID, 512), F32),
            vm((3 * 96, (T + 4) * W), BF),
            vm((W, T * W), BF),
            vm((L * 32, W), F32),
            vm((L, 32, W), BF),
            vm((L, 32, W), BF),
            vm((32, W), BF),
            vm((4, 32, W), BF),
            vm((8, 4, 32, W), BF),
            vm((L, PAD, 8), F32),
            vm((4, 96, 8), F32),
            vm((HID, W), F32),
            pltpu.SemaphoreType.DMA((NSEM,)),
            pltpu.SemaphoreType.DMA((NSEM,)),
            pltpu.SemaphoreType.DMA((N_IN - 1,)),
        ],
        compiler_params=pltpu.CompilerParams(
            collective_id=0, has_side_effects=True, vmem_limit_bytes=56 * 2**20
        ),
    )(*inputs, lead_index)
    wg, bg, hg, fg = pl.pallas_call(
        finish,
        out_shape=(
            jax.ShapeDtypeStruct((OWN, TAPS, GATES, 2 * HID), BF),
            jax.ShapeDtypeStruct((GATES, OWN), F32),
            jax.ShapeDtypeStruct((TAPS * 24, HID), BF),
            jax.ShapeDtypeStruct((16, 2, HID), F32),
        ),
        in_specs=[pl.BlockSpec(memory_space=vm)] * 4,
        out_specs=(pl.BlockSpec(memory_space=vm),) * 4,
    )(*outs)
    return wg.transpose(0, 2, 1, 3), bg.T, hg.reshape(TAPS, 24, HID).transpose(1, 0, 2), fg


def solution(mesh):
    in_specs = (
        P(None, None, "tile", None),
        P("lead", None, None, None),
        P("lead", None),
        P(),
        P(),
        P("lead"),
        P("lead", None, "tile", None),
    )
    out_specs = (P("lead", None, None, None), P("lead", None), P("tile", None, None), P())
    return jax.shard_map(shards, mesh=mesh, in_specs=in_specs, out_specs=out_specs, check_vma=False)
```
